32 devices in a mesh: grp: 4 (over y, core), seq: 8 (over z, x).
Axes of the slice: x: 2, y: 2, z: 4, core: 2. Of those that a mesh axis runs over, the one named last changes fastest.
Arguments:
- tokens: bfloat16 [8, 2048, 1024], P('grp', 'seq'), may hold values from -6 to 6
- seq_lens: int32 [4, 2], P('grp'), may hold values from 1 to 2048, 2560 in all within a row
- norm_attn: bfloat16 [2, 1024], P(None, ('grp', 'seq')), may hold values from 0.25 to 1.75
- w_qkv: bfloat16 [2, 1024, 3072], P(None, ('grp', 'seq')), may hold values from -0.1875 to 0.1875
- w_out: bfloat16 [2, 1024, 1024], P(None, ('grp', 'seq')), may hold values from -3 to 3
- norm_ffn: bfloat16 [2, 1024], P(None, ('grp', 'seq')), may hold values from 0.25 to 1.75
- w_gate: bfloat16 [2, 1024, 2816], P(None, ('grp', 'seq')), may hold values from -0.1875 to 0.1875
- w_up: bfloat16 [2, 1024, 2816], P(None, ('grp', 'seq')), may hold values from -0.1875 to 0.1875
- w_down: bfloat16 [2, 2816, 1024], P(None, ('grp', 'seq')), may hold values from -0.109375 to 0.109375
- cotangent: bfloat16 [8, 2048, 1024], P('grp', 'seq'), may hold values from -6 to 6
Outputs:
- layer_out: bfloat16 [8, 2048, 1024], P('grp', 'seq')
- input_grad: float32 [8, 2048, 1024], P('grp', 'seq')
- norm_attn_grad: float32 [2, 1024], P(None, ('grp', 'seq'))
- w_qkv_grad: float32 [2, 1024, 3072], P(None, ('grp', 'seq'))
- w_out_grad: float32 [2, 1024, 1024], P(None, ('grp', 'seq'))
- norm_ffn_grad: float32 [2, 1024], P(None, ('grp', 'seq'))
- w_gate_grad: float32 [2, 1024, 2816], P(None, ('grp', 'seq'))
- w_up_grad: float32 [2, 1024, 2816], P(None, ('grp', 'seq'))
- w_down_grad: float32 [2, 2816, 1024], P(None, ('grp', 'seq'))
The draws below stay inside these ranges and needn't reach their ends.
Inputs may be any that keep to these rules, and one draw needn't show every extreme that they name: `seq_lens`: in each row the 2 lengths add up to 2560.
All inputs are finite; a program needn't handle non-finite values.
Results may differ from the reference program's by a relative error of at most 0.02.
Values may be sent and summed in bfloat16 or wider, within the bound.
No kernel may reach another device: no remote copies, remote signals or barrier semaphores. Data moves between devices by JAX's collectives and lax.ppermute only.
A program may use at most 640 MiB of HBM per device.

```python
import math
import jax
import jax.numpy as jnp
import numpy as np
from jax import lax

D = 1024
HEADS = 16
HEAD_DIM = 64
FF = 2816
LAYERS = 2
SEQ_LEN = 2048
SEQS = 2
GROUPS = 4
TOTAL_SEQS = 8


def block_scale(stream_key, dims, shards, least, high):
    def one(position, parts):
        heights = jax.random.uniform(jax.random.fold_in(jax.random.fold_in(stream_key, 6), position), (parts,), jnp.float32, least / len(shards), high / len(shards))
        return jnp.repeat(jnp.exp(heights), dims[position] // parts).reshape((-1,) + (1,) * (len(dims) - position - 1))

    level = one(*shards[0])
    for cut in shards[1:]:
        level = level * one(*cut)
    return level


def length_profile(amount, total, bound, skew):
    weights = [(1 << 20) // math.isqrt(rank ** skew) + 1 for rank in range(2, amount + 1)]
    surplus, holding = total - bound - (amount - 1), [1] * (amount - 1)
    while surplus > 0:
        candidates = [i for i in range(amount - 1) if holding[i] < bound]
        pool, budget = sum([weights[i] for i in candidates]), surplus
        for i in candidates:
            more = min(bound - holding[i], max(1, budget * weights[i] // pool), surplus)
            holding[i] = holding[i] + more
            surplus = surplus - more
    return np.array([bound] + holding)


def uneven(key, amount, total, reach, lean):
    if amount == 2:
        one = jax.random.randint(key, (), max(1, total - reach), min(reach, total - 1) + 1)
        return jnp.stack([one, total - one])
    sizes = jnp.asarray(length_profile(amount, total, reach, lean), jnp.int32)
    couples = (amount - 1) // 2
    giver, sink = sizes[1:1 + 2 * couples:2], sizes[2:2 + 2 * couples:2]
    margin = jnp.minimum(giver - 1, reach - sink)
    shifted = jax.random.randint(jax.random.fold_in(key, 1), (couples,), 0, 1 << 20) % (margin + 1)
    sizes = sizes.at[1:1 + 2 * couples:2].set(giver - shifted).at[2:2 + 2 * couples:2].set(sink + shifted)
    return sizes[jax.random.permutation(jax.random.fold_in(key, 2), amount)]


def scatter_about(key, dims, spread, limit, cuts=(), kind=jnp.bfloat16):
    drawn = spread * jax.random.normal(key, dims, jnp.float32)
    if cuts:
        drawn = drawn * block_scale(key, dims, cuts, -0.22, 0.18)
    return jnp.clip(drawn, -limit, limit).astype(kind)


def setup_inputs(seed: int = 0) -> dict:
    keys = jax.random.split(jax.random.key(seed), 11)
    tokens = scatter_about(keys[0], (TOTAL_SEQS, SEQ_LEN, D), 1.0, 6.0, ((0, 4), (1, 8)))
    seq_lens = jax.vmap(lambda own: uneven(own, SEQS, SEQS * SEQ_LEN * 5 // 8, SEQ_LEN, 2))(jax.random.split(keys[1], GROUPS)).reshape((GROUPS, SEQS)).astype(jnp.int32)
    norm_attn = jnp.clip(1.0 + 0.15 * jax.random.normal(keys[2], (LAYERS, D), jnp.float32), 0.25, 1.75).astype(jnp.bfloat16)
    w_qkv = scatter_about(keys[3], (LAYERS, D, 3 * D), D ** -0.5, 0.1875, ((1, 32),))
    w_out = scatter_about(keys[4], (LAYERS, D, D), (max(D // 256, 1)) ** -0.5, 3.0, ((1, 32),))
    norm_ffn = jnp.clip(1.0 + 0.15 * jax.random.normal(keys[5], (LAYERS, D), jnp.float32), 0.25, 1.75).astype(jnp.bfloat16)
    w_gate = scatter_about(keys[6], (LAYERS, D, FF), D ** -0.5, 0.1875, ((1, 32),))
    w_up = scatter_about(keys[7], (LAYERS, D, FF), D ** -0.5, 0.1875, ((1, 32),))
    w_down = scatter_about(keys[8], (LAYERS, FF, D), FF ** -0.5, 0.109375, ((1, 32),))
    cotangent = scatter_about(keys[9], (TOTAL_SEQS, SEQ_LEN, D), 1.0, 6.0, ((0, 4), (1, 8)))
    return {"tokens": tokens, "seq_lens": seq_lens, "norm_attn": norm_attn, "w_qkv": w_qkv, "w_out": w_out, "norm_ffn": norm_ffn, "w_gate": w_gate, "w_up": w_up, "w_down": w_down, "cotangent": cotangent}


EPSILON = 1e-06
PRECISE = lax.Precision.HIGHEST

@jax.custom_vjp
def low(v):
    return lax.optimization_barrier(v.astype(jnp.bfloat16)).astype(jnp.float32)

@jax.custom_vjp
def low_back(v):
    return v

def low_keep(v):
    return (low(v), None)

def low_pass(kept, grad):
    return (grad,)

def back_keep(v):
    return (v, None)

def back_low(kept, grad):
    return (low(grad),)
low.defvjp(low_keep, low_pass)
low_back.defvjp(back_keep, back_low)

def matmul_hi(left, right):
    return jnp.dot(left, right, precision=PRECISE, preferred_element_type=jnp.float32)

def rms_norm(inputs, gain):
    return inputs * lax.rsqrt(lax.optimization_barrier(jnp.mean(inputs * inputs, axis=-1, keepdims=True)) + EPSILON) * gain

def rotate(field, cosine, sine_table):
    half_dim = field.shape[-1] // 2
    first_half = field[..., :half_dim]
    second_half = field[..., half_dim:]
    return jnp.concatenate([first_half * cosine - second_half * sine_table, second_half * cosine + first_half * sine_table], axis=-1)

def rope_tables(seq_length):
    half_dim = HEAD_DIM // 2
    freqs = 10000.0 ** (-jnp.arange(half_dim, dtype=jnp.float32) / half_dim)
    angle = jnp.arange(seq_length, dtype=jnp.float32)[:, None] * freqs[None, :]
    return (jnp.cos(angle)[:, None, :], jnp.sin(angle)[:, None, :])

def attend_one(query, key, value, seq_length):
    block_rows = min(512, SEQ_LEN)
    key_pos = jnp.arange(SEQ_LEN, dtype=jnp.int32)

    def block(block_start):
        q_block = lax.dynamic_slice_in_dim(query, block_start, block_rows, 0)
        logits = jnp.einsum('qhd,khd->hqk', q_block, key, precision=PRECISE) * HEAD_DIM ** (-0.5)
        logits = low_back(logits)
        query_pos = block_start + jnp.arange(block_rows, dtype=jnp.int32)
        allowed_mask = (key_pos[None, :] <= query_pos[:, None]) & (key_pos[None, :] < seq_length)
        logits = jnp.where(allowed_mask[None], logits, -1e+30)
        probs = jax.nn.softmax(logits, axis=-1)
        return jnp.einsum('hqk,khd->qhd', probs, value, precision=PRECISE)
    starts = jnp.arange(0, SEQ_LEN, block_rows, dtype=jnp.int32)
    blocks = lax.map(jax.checkpoint(block), starts)
    return blocks.reshape(SEQ_LEN, HEADS, HEAD_DIM)

def layer(inputs, row_lengths, params, first_value):
    gain_one, mat_qkv, mat_out, gain_two, mat_gate, mat_up, mat_down = params
    batch_size, seq_length, model_width = inputs.shape
    normed = low(rms_norm(inputs, gain_one))
    projected = low_back(matmul_hi(normed, mat_qkv))
    query_raw = projected[..., :model_width]
    key_raw = projected[..., model_width:2 * model_width]
    value_raw = projected[..., 2 * model_width:]
    if first_value is None:
        values = low(value_raw)
    else:
        values = low(0.5 * value_raw + 0.5 * first_value)
    cosine, sine_table = rope_tables(seq_length)
    head_shape = (batch_size, seq_length, HEADS, HEAD_DIM)
    query = low(rotate(query_raw.reshape(head_shape), cosine, sine_table))
    key = low(rotate(key_raw.reshape(head_shape), cosine, sine_table))
    attended = jax.vmap(attend_one)(query, key, values.reshape(head_shape), row_lengths)
    attn_low = low_back(low(attended.reshape(batch_size, seq_length, model_width)))
    middle = inputs + low_back(matmul_hi(attn_low, mat_out))
    normed_two = low(rms_norm(middle, gain_two))
    gate_pre = low_back(matmul_hi(normed_two, mat_gate))
    up_pre = low_back(matmul_hi(normed_two, mat_up))
    hidden = low(jax.nn.silu(gate_pre) * up_pre)
    result = middle + low_back(matmul_hi(hidden, mat_down))
    return (result, values)

def reference(tokens, seq_lens, norm_attn, w_qkv, w_out, norm_ffn, w_gate, w_up, w_down, cotangent):
    params = (norm_attn.astype(jnp.float32), w_qkv.astype(jnp.float32), w_out.astype(jnp.float32), norm_ffn.astype(jnp.float32), w_gate.astype(jnp.float32), w_up.astype(jnp.float32), w_down.astype(jnp.float32))
    lengths = seq_lens.reshape(-1).astype(jnp.int32)
    positions = jnp.arange(SEQ_LEN, dtype=jnp.int32)
    valid_mask = (positions[None, :] < lengths[:, None]).astype(jnp.float32)
    grad_out = cotangent.astype(jnp.float32) * valid_mask[:, :, None]
    paired = 2

    def forward(inputs, weights):

        def both_layers(pack):
            rows, row_lengths = pack
            first_params = tuple((w[0] for w in weights))
            second_params = tuple((w[1] for w in weights))
            middle_rows, first_value = layer(rows, row_lengths, first_params, None)
            out_rows, unused = layer(middle_rows, row_lengths, second_params, first_value)
            return out_rows
        grouped = inputs.reshape(-1, paired, SEQ_LEN, D)
        outputs = lax.map(jax.checkpoint(both_layers), (grouped, lengths.reshape(-1, paired)))
        return outputs.reshape(inputs.shape)
    outputs, pullback = jax.vjp(forward, tokens.astype(jnp.float32), params)
    grad_inputs, grad_params = pullback(grad_out)
    return (outputs.astype(jnp.bfloat16), grad_inputs, grad_params[0], grad_params[1], grad_params[2], grad_params[3], grad_params[4], grad_params[5], grad_params[6])
```

```python
import jax
import jax.numpy as jnp
from jax import lax
from jax.experimental import pallas as pl
from jax.experimental.pallas import tpu as pltpu
from jax.sharding import Mesh
from jax.sharding import PartitionSpec as P

HEADS = 16
EPSILON = 1e-06
NEGATIVE = -1e30
PRECISE = lax.Precision.HIGHEST
BF = jnp.bfloat16
F32 = jnp.float32
ALL = ("y", "c", "z", "x")
PLANE = ("c", "y", "x")
VMEM_BYTES = 50 * 1024 * 1024
ANY = pl.BlockSpec(memory_space=pl.ANY)
SMEM = pl.BlockSpec(memory_space=pltpu.SMEM)
NT = (((1,), (1,)), ((), ()))
TN = (((0,), (0,)), ((), ()))


def params(**more):
    return pltpu.CompilerParams(vmem_limit_bytes=VMEM_BYTES, **more)


def assemble(where, pieces, relative, with_x):
    rows, cols = pieces[0].shape[1:]
    count = len(pieces)
    lead = (2, 2, 4, 2) if with_x else (2, 2, 4)

    def kernel(where_ref, *rest):
        ins, out, held, sems = rest[:count], rest[count], rest[count + 1], rest[count + 2]
        y, c, z, x = (where_ref[n] for n in range(4))
        copies, puts = [], []
        for n in range(count):
            dy, dc, dx = relative[n]
            for dz in range(4):
                slot = (y ^ dy, c ^ dc, z ^ dz) + ((x ^ dx,) if with_x else ())
                spot = held.at[n, dz]
                copies.append(pltpu.make_async_copy(ins[n].at[dz], spot, sems.at[0, n, dz]))
                puts.append(pltpu.make_async_copy(spot, out.at[slot], sems.at[1, n, dz]))
        for copy in copies:
            copy.start()
        for copy, put in zip(copies, puts):
            copy.wait()
            put.start()
        for put in puts:
            put.wait()

    out = pl.pallas_call(
        kernel,
        in_specs=[SMEM] + [ANY] * count,
        out_specs=ANY,
        out_shape=jax.ShapeDtypeStruct(lead + (rows, cols), pieces[0].dtype),
        scratch_shapes=[
            pltpu.VMEM((count, 4, rows, cols), pieces[0].dtype),
            pltpu.SemaphoreType.DMA((2, count, 4)),
        ],
        compiler_params=params(),
        name="assemble",
    )(where, *pieces)
    return out.reshape(-1, cols)


def swap(value, axis):
    return lax.ppermute(value, axis, [(0, 1), (1, 0)])


def hop(value, offset):
    return lax.ppermute(value, "z", [(i, i ^ offset) for i in range(4)])


def gather_z_first(where, shard, first, second):
    stack = jnp.stack([shard] + [hop(shard, k) for k in (1, 2, 3)])
    near = swap(stack, first)
    ring = [((0, 0), stack), ((1, 0), near)]
    ring += [((0, 1), swap(stack, second)), ((1, 1), swap(near, second))]
    pieces, relative = [], []
    for (one, two), piece in ring:
        moved = {first: one, second: two}
        for dc, held in ((0, piece), (1, swap(piece, "c"))):
            pieces.append(held)
            relative.append((moved["y"], dc, moved["x"]))
    return assemble(where, pieces, relative, True)


def gather_x_first(where, shard):
    near = swap(shard, "x")
    even = lax.axis_index("x") == 0
    pair = jnp.concatenate([jnp.where(even, shard, near), jnp.where(even, near, shard)])
    stack = jnp.stack([pair] + [hop(pair, k) for k in (1, 2, 3)])
    pieces, relative = [], []
    for dy, piece in ((0, stack), (1, swap(stack, "y"))):
        for dc, held in ((0, piece), (1, swap(piece, "c"))):
            pieces.append(held)
            relative.append((dy, dc, 0))
    return assemble(where, pieces, relative, False)


def reduce_rows(partial, order):
    names = ["y", "z", "x"]
    for step, axis in enumerate(order):
        dim = names.index(axis)
        names.pop(dim)
        here = lax.axis_index(axis)
        last = step == len(order) - 1

        def block(slot):
            return lax.dynamic_index_in_dim(partial, slot, dim, keepdims=False)

        if axis == "z":
            moved = [hop(block(here ^ k), k) for k in (1, 2, 3)]
        else:
            moved = [swap(block(1 - here), axis)]
        total = block(here).astype(F32)
        for part in moved:
            total = total + part.astype(F32)
        partial = total if last else total.astype(BF)
    return partial


def turn(field, cosine, signed_sine):
    lane = lax.broadcasted_iota(jnp.int32, field.shape, 1)
    other = jnp.where(
        lane % 64 < 32, pltpu.roll(field, 96, axis=1), pltpu.roll(field, 32, axis=1)
    )
    return field * cosine + other * signed_sine


def project_qkv(normed, w_qk, w_vo, cosine, signed_sine, first_value):
    rows, width = normed.shape

    def kernel(normed_ref, w_qk_ref, w_vo_ref, cos_ref, sin_ref, *rest):
        out_ref = rest[-1]
        step = pl.program_id(0)

        @pl.when(step < 8)
        def _():
            product = jnp.dot(normed_ref[...], w_qk_ref[...], preferred_element_type=F32)
            for half in range(2):
                field = product[:, 128 * half : 128 * half + 128]
                out_ref[half, 0] = turn(field, cos_ref[...], sin_ref[...]).astype(BF)

        @pl.when(step >= 8)
        def _():
            product = jnp.dot(normed_ref[...], w_vo_ref[...], preferred_element_type=F32)
            for half in range(2):
                field = product[:, 128 * half : 128 * half + 128]
                if first_value is not None:
                    field = 0.5 * field + 0.5 * rest[0][half, 0].astype(F32)
                out_ref[half, 0] = field.astype(BF)

    whole = lambda step: (0, 0)
    in_specs = [
        pl.BlockSpec((rows, width), whole),
        pl.BlockSpec((width, 256), lambda step: (0, jnp.minimum(step, 7))),
        pl.BlockSpec((width, 256), lambda step: (0, jnp.maximum(step - 8, 0))),
        pl.BlockSpec((rows, 128), whole),
        pl.BlockSpec((rows, 128), whole),
    ]
    operands = [normed, w_qk, w_vo, cosine, signed_sine]
    if first_value is not None:
        in_specs.append(
            pl.BlockSpec((2, 1, rows, 128), lambda step: (jnp.maximum(step - 8, 0), 2, 0, 0))
        )
        operands.append(first_value)
    return pl.pallas_call(
        kernel,
        grid=(12,),
        in_specs=in_specs,
        out_specs=pl.BlockSpec((2, 1, rows, 128), lambda step: (step % 4, step // 4, 0, 0)),
        out_shape=jax.ShapeDtypeStruct((8, 3, rows, 128), BF),
        compiler_params=params(dimension_semantics=("arbitrary",)),
        name="project_qkv",
    )(*operands)


def weight_grad(left_own, left_near, right_own, right_near, tile):
    rows, depth = left_own.shape
    cols = right_own.shape[1]

    def kernel(lo, ln, ro, rn, out_ref, flipped):
        @pl.when(pl.program_id(0) == 0)
        def _():
            flipped[:, :rows] = lo[...].T
            flipped[:, rows:] = ln[...].T

        total = jnp.dot(flipped[:, :rows], ro[...], preferred_element_type=F32)
        total += jnp.dot(flipped[:, rows:], rn[...], preferred_element_type=F32)
        out_ref[...] = total.astype(BF)

    whole = pl.BlockSpec((rows, depth), lambda n: (0, 0))
    block = pl.BlockSpec((rows, tile), lambda n: (0, n))
    return pl.pallas_call(
        kernel,
        grid=(cols // tile,),
        in_specs=[whole, whole, block, block],
        out_specs=pl.BlockSpec((depth, tile), lambda n: (0, n)),
        out_shape=jax.ShapeDtypeStruct((depth, cols), BF),
        scratch_shapes=[pltpu.VMEM((depth, 2 * rows), BF)],
        compiler_params=params(dimension_semantics=("arbitrary",)),
        name="weight_grad",
    )(left_own, left_near, right_own, right_near)


def rows_of(block):
    return block.reshape(-1, 128)


def attend(lengths, pieces):
    tile = 256
    slots = pieces.shape[3] * 128
    tiles = slots // tile
    per = tile // 128

    def kernel(len_ref, piece_ref, out_ref, lse_ref, held, flipped, logit, sems):
        seq, step = pl.program_id(0), pl.program_id(1)

        def load(which, device):
            return pltpu.make_async_copy(
                piece_ref.at[device, :, which],
                held.at[:, which, :, device],
                sems.at[which, device],
            )

        @pl.when((seq == 0) & (step == 0))
        def _():
            for which in range(2):
                for device in range(8):
                    load(which, device).start()
            for device in range(8):
                load(0, device).wait()

        @pl.when((seq == 1) & (step == 0))
        def _():
            for device in range(8):
                load(1, device).wait()

        @pl.when(step == 0)
        def _():
            for block in range(tiles):
                key = rows_of(held[1, seq, pl.ds(per * block, per)])
                flipped[block] = key.T

        used = len_ref[seq]
        query = rows_of(held[0, seq, pl.ds(per * step, per)]) * BF(0.125)
        lane = lax.broadcasted_iota(jnp.int32, (tile, 128), 1)
        low = lane < 64
        zero = jnp.zeros_like(query)
        queries = [jnp.where(low, query, zero), jnp.where(low, zero, query)]

        def score(block, tops, masked):
            key_t = flipped[block]
            result = []
            for head in range(2):
                field = jnp.dot(queries[head], key_t, preferred_element_type=F32)
                if masked:
                    query_pos = step * tile + lax.broadcasted_iota(jnp.int32, field.shape, 0)
                    key_pos = block * tile + lax.broadcasted_iota(jnp.int32, field.shape, 1)
                    seen = (key_pos <= query_pos) & (key_pos < used)
                    field = jnp.where(seen, field, NEGATIVE)
                logit[head, block] = field
                top = jnp.maximum(field[:, :128], field[:, 128:])
                result.append(jnp.maximum(tops[head], top))
            return tuple(result)

        full = jnp.minimum(step, used // tile)
        end = jnp.minimum(step + 1, (used + tile - 1) // tile)
        low_top = jnp.full((tile, 128), NEGATIVE, F32)
        tops = lax.fori_loop(0, full, lambda b, s: score(b, s, False), (low_top, low_top))
        tops = lax.fori_loop(full, end, lambda b, s: score(b, s, True), tops)
        tops = [jnp.max(top, axis=1, keepdims=True) for top in tops]
        wide = [jnp.broadcast_to(top, (tile, tile)) for top in tops]
        one = jnp.ones_like(query)

        def mix(block, sums):
            value = rows_of(held[2, seq, pl.ds(per * block, per)])
            values = [jnp.where(low, value, one), jnp.where(low, one, value)]
            result = []
            for head in range(2):
                probs = jnp.exp(logit[head, block] - wide[head]).astype(BF)
                result.append(
                    sums[head] + jnp.dot(probs, values[head], preferred_element_type=F32)
                )
            return tuple(result)

        nothing = jnp.zeros((tile, 128), F32)
        sums = lax.fori_loop(0, end, mix, (nothing, nothing))
        totals = [sums[0][:, 64:65], sums[1][:, 0:1]]
        out = jnp.where(low, sums[0] / totals[0], sums[1] / totals[1])
        out = out.astype(BF).reshape(per, 8, 16, 128)
        for device in range(8):
            out_ref[device, seq, pl.ds(per * step, per)] = out[:, device]
        level = jnp.where(low, tops[0] + jnp.log(totals[0]), tops[1] + jnp.log(totals[1])).T
        start = pl.multiple_of(step * tile, tile)
        lse_ref[seq, 0:1, pl.ds(start, tile)] = level[0:1]
        lse_ref[seq, 1:2, pl.ds(start, tile)] = level[64:65]

    return pl.pallas_call(
        kernel,
        grid=(2, tiles),
        in_specs=[SMEM, ANY],
        out_specs=[
            pl.BlockSpec((8, 2) + pieces.shape[3:], lambda s, i: (0, 0, 0, 0, 0)),
            pl.BlockSpec((2, 8, slots), lambda s, i: (0, 0, 0)),
        ],
        out_shape=[
            jax.ShapeDtypeStruct((8, 2) + pieces.shape[3:], BF),
            jax.ShapeDtypeStruct((2, 8, slots), F32),
        ],
        scratch_shapes=[
            pltpu.VMEM((3, 2, slots // 128, 8, 16, 128), BF),
            pltpu.VMEM((tiles, 128, tile), BF),
            pltpu.VMEM((2, tiles, tile, tile), F32),
            pltpu.SemaphoreType.DMA((2, 8)),
        ],
        compiler_params=params(dimension_semantics=("arbitrary", "arbitrary")),
        name="attend",
    )(lengths, pieces)


def attend_back(lengths, pieces, attended, grads, lse, cosine, signed_sine, passed):
    tile = 256
    slots = pieces.shape[3] * 128
    tiles = slots // tile
    per = tile // 128
    upper = passed is None

    def kernel(*refs):
        len_ref, piece_ref, att_ref, grad_ref, lse_ref, cos_ref, sin_ref = refs[:7]
        refs = refs[7:]
        if upper:
            passed_ref = None
            out_ref, give_ref = refs[:2]
            refs = refs[2:]
        else:
            passed_ref, out_ref = refs[:2]
            give_ref = None
            refs = refs[2:]
        held, att, grad, delta, level, query_acc, key_acc, value_acc, sems = refs
        seq, step = pl.program_id(0), pl.program_id(1)
        used = len_ref[seq]

        def loads(which):
            copies = []
            for device in range(8):
                copies.append(
                    pltpu.make_async_copy(
                        piece_ref.at[device, :, which],
                        held.at[:, which, :, device],
                        sems.at[0, which, device],
                    )
                )
                copies.append(
                    pltpu.make_async_copy(
                        att_ref.at[device, which],
                        att.at[which, :, device],
                        sems.at[1, which, device],
                    )
                )
                copies.append(
                    pltpu.make_async_copy(
                        grad_ref.at[device, which],
                        grad.at[which, :, device],
                        sems.at[2, which, device],
                    )
                )
            return copies

        @pl.when((seq == 0) & (step == 0))
        def _():
            for which in range(2):
                for copy in loads(which):
                    copy.start()
            for copy in loads(0):
                copy.wait()

        @pl.when((seq == 1) & (step == 0))
        def _():
            for copy in loads(1):
                copy.wait()

        @pl.when(step == 0)
        def _():
            query_acc[...] = jnp.zeros_like(query_acc)
            line = lax.broadcasted_iota(jnp.int32, (8, 128), 0)
            lane = lax.broadcasted_iota(jnp.int32, (8, 128), 1)
            pick = jnp.where(line == lane // 64, 1.0, 0.0).astype(F32)
            for block in range(tiles):
                span = slice(tile * block, tile * block + tile)
                product = rows_of(grad[seq, pl.ds(per * block, per)]).astype(F32) * rows_of(
                    att[seq, pl.ds(per * block, per)]
                ).astype(F32)
                delta[:, span] = lax.dot_general(
                    pick, product, NT, precision=PRECISE, preferred_element_type=F32
                )
            place = lax.broadcasted_iota(jnp.int32, (8, slots), 1)
            level[...] = jnp.where(place < used, lse_ref[seq], -NEGATIVE)

        key = rows_of(held[1, seq, pl.ds(per * step, per)])
        value = rows_of(held[2, seq, pl.ds(per * step, per)])
        lane = lax.broadcasted_iota(jnp.int32, (tile, 128), 1)
        low = lane < 64

        def head_part(field, head):
            keep = low if head == 0 else jnp.logical_not(low)
            return jnp.where(keep, field, jnp.zeros_like(field))

        scaled = key * BF(0.125)
        keys = [head_part(scaled, head) for head in range(2)]
        values = [head_part(value, head) for head in range(2)]
        key_acc[...] = jnp.zeros_like(key_acc)
        value_acc[...] = jnp.zeros_like(value_acc)

        def visit(block, masked):
            query = rows_of(held[0, seq, pl.ds(per * block, per)])
            grad_out = rows_of(grad[seq, pl.ds(per * block, per)])
            start = pl.multiple_of(block * tile, tile)
            spans = pl.ds(start, tile)
            query_sum = jnp.zeros((tile, 128), F32)
            key_sum = jnp.zeros((tile, 128), F32)
            value_sum = jnp.zeros((tile, 128), F32)
            for head in range(2):
                logits = lax.dot_general(keys[head], query, NT, preferred_element_type=F32)
                probs = jnp.exp(logits - level[head : head + 1, spans])
                if masked:
                    key_pos = lax.broadcasted_iota(jnp.int32, probs.shape, 0)
                    query_pos = lax.broadcasted_iota(jnp.int32, probs.shape, 1)
                    probs = jnp.where(key_pos <= query_pos, probs, 0.0)
                grad_probs = lax.dot_general(
                    values[head], grad_out, NT, preferred_element_type=F32
                )
                grad_logits = (probs * (grad_probs - delta[head : head + 1, spans])).astype(BF)
                value_sum += jnp.dot(
                    probs.astype(BF), head_part(grad_out, head), preferred_element_type=F32
                )
                key_sum += jnp.dot(
                    grad_logits, head_part(query, head), preferred_element_type=F32
                )
                query_sum += lax.dot_general(
                    grad_logits, keys[head], TN, preferred_element_type=F32
                )
            query_acc[spans, :] += query_sum
            key_acc[...] += key_sum
            value_acc[...] += value_sum

        end = (used + tile - 1) // tile

        @pl.when(step < end)
        def _():
            visit(step, True)

            def body(block, carry):
                visit(block, False)
                return carry

            lax.fori_loop(step + 1, end, body, 0)

        def put(member, block, field):
            field = field.astype(BF).reshape(per, 8, 16, 128)
            for device in range(8):
                out_ref[device, member, seq, pl.ds(per * block, per)] = field[:, device]

        start = pl.multiple_of(step * tile, tile)
        spans = pl.ds(start, tile)
        key_grad = key_acc[...] * 0.125
        put(1, step, turn(key_grad, cos_ref[spans, :], -sin_ref[spans, :]))
        if upper:
            half = 0.5 * value_acc[...]
            give_ref[seq, spans, :] = half
            put(2, step, half)
        else:
            put(2, step, value_acc[...] + passed_ref[seq, spans, :])

        @pl.when(step == tiles - 1)
        def _():
            for block in range(tiles):
                part = slice(tile * block, tile * block + tile)
                put(0, block, turn(query_acc[part, :], cos_ref[part, :], -sin_ref[part, :]))

    flat = lambda s, i: (0, 0)
    cube = lambda s, i: (0, 0, 0)
    in_specs = [
        SMEM,
        ANY,
        ANY,
        ANY,
        pl.BlockSpec((2, 8, slots), cube),
        pl.BlockSpec((slots, 128), flat),
        pl.BlockSpec((slots, 128), flat),
    ]
    operands = [lengths, pieces, attended, grads, lse, cosine, signed_sine]
    out_specs = [pl.BlockSpec(pieces.shape, lambda s, i: (0, 0, 0, 0, 0, 0))]
    out_shape = [jax.ShapeDtypeStruct(pieces.shape, BF)]
    carried = pl.BlockSpec((2, slots, 128), cube)
    if upper:
        out_specs.append(carried)
        out_shape.append(jax.ShapeDtypeStruct((2, slots, 128), F32))
    else:
        in_specs.append(carried)
        operands.append(passed)
    outs = pl.pallas_call(
        kernel,
        grid=(2, tiles),
        in_specs=in_specs,
        out_specs=out_specs,
        out_shape=out_shape,
        scratch_shapes=[
            pltpu.VMEM((3, 2, slots // 128, 8, 16, 128), BF),
            pltpu.VMEM((2, slots // 128, 8, 16, 128), BF),
            pltpu.VMEM((2, slots // 128, 8, 16, 128), BF),
            pltpu.VMEM((8, slots), F32),
            pltpu.VMEM((8, slots), F32),
            pltpu.VMEM((slots, 128), F32),
            pltpu.VMEM((tile, 128), F32),
            pltpu.VMEM((tile, 128), F32),
            pltpu.SemaphoreType.DMA((3, 2, 8)),
        ],
        compiler_params=params(dimension_semantics=("arbitrary", "arbitrary")),
        name="attend_back",
    )(*operands)
    return outs if upper else (outs[0], None)


def block_spans(total_rows):
    return [(offset, min(512, total_rows - offset)) for offset in range(0, total_rows, 512)]


def rotate(field, cosine, sine_table):
    half_dim = field.shape[-1] // 2
    first_half = field[..., :half_dim]
    second_half = field[..., half_dim:]
    return jnp.concatenate(
        [
            first_half * cosine - second_half * sine_table,
            second_half * cosine + first_half * sine_table,
        ],
        axis=-1,
    )


def allowed(query_pos, key_pos, lengths):
    causal = key_pos[None, None, :] <= query_pos[None, :, None]
    inside = key_pos[None, None, :] < lengths[:, None, None]
    return (causal & inside)[:, None, :, :]


def attend_gathered(q_heads, k_flat, v_flat, lengths, positions, score_scale):
    seq_count, stretch_len, head_count, head_dim = q_heads.shape
    first_row = jnp.int32(0)
    k_piece = lax.all_gather(k_flat, "seq", axis=1, tiled=True)
    v_piece = lax.all_gather(v_flat, "seq", axis=1, tiled=True)
    running_max = jnp.full((seq_count, head_count, stretch_len), NEGATIVE, jnp.float32)
    row_total = jnp.zeros((seq_count, head_count, stretch_len), jnp.float32)
    weighted = jnp.zeros((seq_count, stretch_len, head_count, head_dim), jnp.float32)
    for offset, block_len in block_spans(k_piece.shape[1]):
        k_block = k_piece[:, offset : offset + block_len].reshape(
            seq_count, block_len, head_count, head_dim
        )
        v_block = (
            v_piece[:, offset : offset + block_len]
            .reshape(seq_count, block_len, head_count, head_dim)
            .astype(jnp.float32)
        )
        key_pos = first_row + offset + jnp.arange(block_len, dtype=jnp.int32)
        allowed_mask = allowed(positions, key_pos, lengths)
        logits = (
            jnp.einsum("sqhd,skhd->shqk", q_heads, k_block, preferred_element_type=jnp.float32)
            * score_scale
        )
        new_max = jnp.maximum(
            running_max, jnp.max(jnp.where(allowed_mask, logits, NEGATIVE), axis=-1)
        )
        probs = jnp.where(allowed_mask, jnp.exp(logits - new_max[..., None]), 0.0)
        rescale = jnp.exp(running_max - new_max)
        row_total = row_total * rescale + jnp.sum(probs, axis=-1)
        weighted = weighted * jnp.transpose(rescale, (0, 2, 1))[..., None] + jnp.einsum(
            "shqk,skhd->sqhd", probs, v_block, precision=PRECISE, preferred_element_type=jnp.float32
        )
        running_max = new_max
    running_max, row_total, weighted = (running_max, row_total, weighted)
    attended = weighted / jnp.transpose(row_total, (0, 2, 1))[..., None]
    return (attended, running_max + jnp.log(row_total))


def attend_back_gathered(
    q_heads,
    k_heads,
    v_heads,
    q_flat,
    k_flat,
    v_flat,
    grad_heads,
    grad_flat,
    log_total,
    delta_rows,
    lengths,
    positions,
    score_scale,
):
    seq_count, stretch_len, head_count, head_dim = q_heads.shape
    zeros_heads = jnp.zeros((seq_count, stretch_len, head_count, head_dim), jnp.float32)
    carry = zeros_heads
    first_row = jnp.int32(0)
    k_piece = lax.all_gather(k_flat, "seq", axis=1, tiled=True)
    v_piece = lax.all_gather(v_flat, "seq", axis=1, tiled=True)
    for offset, block_len in block_spans(k_piece.shape[1]):
        k_block = k_piece[:, offset : offset + block_len].reshape(
            seq_count, block_len, head_count, head_dim
        )
        v_block = v_piece[:, offset : offset + block_len].reshape(
            seq_count, block_len, head_count, head_dim
        )
        key_pos = first_row + offset + jnp.arange(block_len, dtype=jnp.int32)
        allowed_mask = allowed(positions, key_pos, lengths)
        logits = (
            jnp.einsum("sqhd,skhd->shqk", q_heads, k_block, preferred_element_type=jnp.float32)
            * score_scale
        )
        probs = jnp.where(allowed_mask, jnp.exp(logits - log_total[..., None]), 0.0)
        grad_probs = jnp.einsum(
            "sqhd,skhd->shqk", grad_heads, v_block, preferred_element_type=jnp.float32
        )
        grad_logits = (probs * (grad_probs - delta_rows[..., None])).astype(jnp.bfloat16)
        carry = (
            carry
            + jnp.einsum(
                "shqk,skhd->sqhd", grad_logits, k_block, preferred_element_type=jnp.float32
            )
            * score_scale
        )
    gathered_stats = (
        lax.all_gather(log_total, "seq", axis=2, tiled=True),
        lax.all_gather(delta_rows, "seq", axis=2, tiled=True),
    )
    first_row = jnp.int32(0)
    q_piece = lax.all_gather(q_flat, "seq", axis=1, tiled=True)
    g_piece = lax.all_gather(grad_flat, "seq", axis=1, tiled=True)
    grad_key = zeros_heads
    grad_value = zeros_heads
    for offset, block_len in block_spans(q_piece.shape[1]):
        q_block = q_piece[:, offset : offset + block_len].reshape(
            seq_count, block_len, head_count, head_dim
        )
        g_block = g_piece[:, offset : offset + block_len].reshape(
            seq_count, block_len, head_count, head_dim
        )
        query_pos = first_row + offset + jnp.arange(block_len, dtype=jnp.int32)
        allowed_mask = allowed(query_pos, positions, lengths)
        lse_block = lax.dynamic_slice_in_dim(gathered_stats[0], offset, block_len, 2)
        delta_block = lax.dynamic_slice_in_dim(gathered_stats[1], offset, block_len, 2)
        logits = (
            jnp.einsum("sqhd,skhd->shqk", q_block, k_heads, preferred_element_type=jnp.float32)
            * score_scale
        )
        probs = jnp.where(allowed_mask, jnp.exp(logits - lse_block[..., None]), 0.0)
        grad_value = grad_value + jnp.einsum(
            "shqk,sqhd->skhd",
            probs,
            g_block.astype(jnp.float32),
            precision=PRECISE,
            preferred_element_type=jnp.float32,
        )
        grad_probs = jnp.einsum(
            "sqhd,skhd->shqk", g_block, v_heads, preferred_element_type=jnp.float32
        )
        grad_logits = (probs * (grad_probs - delta_block[..., None])).astype(jnp.bfloat16)
        grad_key = (
            grad_key
            + jnp.einsum(
                "shqk,sqhd->skhd", grad_logits, q_block, preferred_element_type=jnp.float32
            )
            * score_scale
        )
    grad_key, grad_value = (grad_key, grad_value)
    return (carry, grad_key, grad_value)


def body(tokens, seq_lens, norm_attn, w_qkv, w_out, norm_ffn, w_gate, w_up, w_down, cotangent):
    seq_count, stretch_len, model_width = tokens.shape
    head_count = HEADS
    head_dim = model_width // head_count
    score_scale = head_dim ** (-0.5)
    lengths = seq_lens[0]
    positions = lax.axis_index("seq") * stretch_len + jnp.arange(stretch_len, dtype=jnp.int32)
    half_dim = head_dim // 2
    freqs = 10000.0 ** (-jnp.arange(half_dim, dtype=jnp.float32) / half_dim)
    angle = positions.astype(jnp.float32)[:, None] * freqs[None, :]
    cosine = jnp.cos(angle)[:, None, :]
    sine_table = jnp.sin(angle)[:, None, :]

    def heads_of(field):
        return field.reshape(seq_count, stretch_len, head_count, head_dim)

    def gather_layer(layer_index):
        return (
            lax.all_gather(norm_attn[layer_index], ("grp", "seq"), axis=0, tiled=True),
            lax.all_gather(w_qkv[layer_index], ("grp", "seq"), axis=0, tiled=True),
            lax.all_gather(w_out[layer_index], ("grp", "seq"), axis=0, tiled=True),
            lax.all_gather(norm_ffn[layer_index], ("grp", "seq"), axis=0, tiled=True),
            lax.all_gather(w_gate[layer_index], ("grp", "seq"), axis=0, tiled=True),
            lax.all_gather(w_up[layer_index], ("grp", "seq"), axis=0, tiled=True),
            lax.all_gather(w_down[layer_index], ("grp", "seq"), axis=0, tiled=True),
        )

    def gather_again(layer_index):
        return (
            lax.all_gather(norm_attn[layer_index], ("grp", "seq"), axis=0, tiled=True),
            lax.all_gather(w_qkv[layer_index], ("grp", "seq"), axis=0, tiled=True),
            lax.all_gather(w_out[layer_index], ("grp", "seq"), axis=0, tiled=True),
            lax.all_gather(norm_ffn[layer_index], ("grp", "seq"), axis=0, tiled=True),
            lax.all_gather(w_gate[layer_index], ("grp", "seq"), axis=0, tiled=True),
            lax.all_gather(w_up[layer_index], ("grp", "seq"), axis=0, tiled=True),
            lax.all_gather(w_down[layer_index], ("grp", "seq"), axis=0, tiled=True),
        )

    def forward_layer(inputs, params, first_value):
        gain_one, mat_qkv, mat_out, gain_two, mat_gate, mat_up, mat_down = params
        rms_one = lax.rsqrt(jnp.mean(inputs * inputs, axis=-1, keepdims=True) + EPSILON)
        normed = (inputs * rms_one * gain_one.astype(jnp.float32)).astype(jnp.bfloat16)
        projected = jnp.dot(normed, mat_qkv, preferred_element_type=jnp.float32)
        query_raw = projected[:, :model_width]
        key_raw = projected[:, model_width : 2 * model_width]
        value_raw = projected[:, 2 * model_width :]
        if first_value is None:
            values = value_raw.astype(jnp.bfloat16)
        else:
            values = (0.5 * value_raw + 0.5 * first_value.astype(jnp.float32)).astype(jnp.bfloat16)
        query_rot = rotate(heads_of(query_raw), cosine, sine_table).astype(jnp.bfloat16)
        key_rot = rotate(heads_of(key_raw), cosine, sine_table).astype(jnp.bfloat16)
        attended, log_total = attend_gathered(
            query_rot,
            key_rot.reshape(seq_count, stretch_len, model_width),
            values.reshape(seq_count, stretch_len, model_width),
            lengths,
            positions,
            score_scale,
        )
        attn_low = attended.reshape(-1, model_width).astype(jnp.bfloat16)
        middle = inputs + jnp.dot(attn_low, mat_out, preferred_element_type=jnp.float32)
        rms_two = lax.rsqrt(jnp.mean(middle * middle, axis=-1, keepdims=True) + EPSILON)
        normed_two = (middle * rms_two * gain_two.astype(jnp.float32)).astype(jnp.bfloat16)
        gate_pre = jnp.dot(normed_two, mat_gate, preferred_element_type=jnp.float32)
        up_pre = jnp.dot(normed_two, mat_up, preferred_element_type=jnp.float32)
        hidden = (jax.nn.silu(gate_pre) * up_pre).astype(jnp.bfloat16)
        result = middle + jnp.dot(hidden, mat_down, preferred_element_type=jnp.float32)
        kept = (
            inputs,
            rms_one,
            normed,
            query_rot,
            key_rot,
            values,
            attended,
            attn_low,
            log_total,
            middle,
            rms_two,
            normed_two,
            gate_pre,
            up_pre,
            hidden,
        )
        return (result, values, kept)

    def backward_layer(grad_in, params, kept, first_grad):
        gain_one, mat_qkv, mat_out, gain_two, mat_gate, mat_up, mat_down = params
        (
            inputs,
            rms_one,
            normed,
            query_rot,
            key_rot,
            values,
            attended,
            attn_low,
            log_total,
            middle,
            rms_two,
            normed_two,
            gate_pre,
            up_pre,
            hidden,
        ) = kept
        grad_low = grad_in.astype(jnp.bfloat16)
        grad_down = jnp.einsum("nf,nd->fd", hidden, grad_low, preferred_element_type=jnp.float32)
        grad_hidden = jnp.einsum(
            "nd,fd->nf", grad_low, mat_down, preferred_element_type=jnp.float32
        )
        sigma = jax.nn.sigmoid(gate_pre)
        grad_gate_pre = (grad_hidden * up_pre * sigma * (1.0 + gate_pre * (1.0 - sigma))).astype(
            jnp.bfloat16
        )
        grad_up_pre = (grad_hidden * gate_pre * sigma).astype(jnp.bfloat16)
        grad_gate = jnp.einsum(
            "nd,nf->df", normed_two, grad_gate_pre, preferred_element_type=jnp.float32
        )
        grad_up = jnp.einsum(
            "nd,nf->df", normed_two, grad_up_pre, preferred_element_type=jnp.float32
        )
        grad_normed_two = jnp.einsum(
            "nf,df->nd", grad_gate_pre, mat_gate, preferred_element_type=jnp.float32
        ) + jnp.einsum("nf,df->nd", grad_up_pre, mat_up, preferred_element_type=jnp.float32)
        scaled_two = middle * rms_two
        grad_gain_two = jnp.sum(grad_normed_two * scaled_two, axis=0)
        weighted_two = grad_normed_two * gain_two.astype(jnp.float32)
        grad_middle = grad_in + rms_two * (
            weighted_two - scaled_two * jnp.mean(weighted_two * scaled_two, axis=-1, keepdims=True)
        )
        grad_attn = grad_middle.astype(jnp.bfloat16)
        grad_out_mat = jnp.einsum(
            "nd,ne->de", attn_low, grad_attn, preferred_element_type=jnp.float32
        )
        grad_attended = jnp.einsum(
            "ne,de->nd", grad_attn, mat_out, preferred_element_type=jnp.float32
        ).astype(jnp.bfloat16)
        grad_heads = heads_of(grad_attended)
        delta_rows = jnp.transpose(
            jnp.sum(grad_heads.astype(jnp.float32) * attended, axis=-1), (0, 2, 1)
        )
        grad_query, grad_key, grad_value = attend_back_gathered(
            query_rot,
            key_rot,
            heads_of(values),
            query_rot.reshape(seq_count, stretch_len, model_width),
            key_rot.reshape(seq_count, stretch_len, model_width),
            values.reshape(seq_count, stretch_len, model_width),
            grad_heads,
            grad_attended.reshape(seq_count, stretch_len, model_width),
            log_total,
            delta_rows,
            lengths,
            positions,
            score_scale,
        )
        grad_query_raw = rotate(grad_query, cosine, -sine_table).reshape(-1, model_width)
        grad_key_raw = rotate(grad_key, cosine, -sine_table).reshape(-1, model_width)
        grad_value_flat = grad_value.reshape(-1, model_width)
        if first_grad is None:
            grad_value_raw = 0.5 * grad_value_flat
            passed = 0.5 * grad_value_flat
        else:
            grad_value_raw = grad_value_flat + first_grad
            passed = None
        grad_proj = jnp.concatenate([grad_query_raw, grad_key_raw, grad_value_raw], axis=-1).astype(
            jnp.bfloat16
        )
        grad_qkv = jnp.einsum("nd,ne->de", normed, grad_proj, preferred_element_type=jnp.float32)
        grad_normed = jnp.einsum(
            "ne,de->nd", grad_proj, mat_qkv, preferred_element_type=jnp.float32
        )
        scaled_one = inputs * rms_one
        grad_gain_one = jnp.sum(grad_normed * scaled_one, axis=0)
        weighted_one = grad_normed * gain_one.astype(jnp.float32)
        grad_inputs = grad_middle + rms_one * (
            weighted_one - scaled_one * jnp.mean(weighted_one * scaled_one, axis=-1, keepdims=True)
        )
        return (
            grad_inputs,
            (grad_gain_one, grad_qkv, grad_out_mat, grad_gain_two, grad_gate, grad_up, grad_down),
            passed,
        )

    def reduce_layer(grads):
        return (
            lax.psum_scatter(grads[0], ("grp", "seq"), scatter_dimension=0, tiled=True),
            lax.psum_scatter(grads[1], ("grp", "seq"), scatter_dimension=0, tiled=True),
            lax.psum_scatter(grads[2], ("grp", "seq"), scatter_dimension=0, tiled=True),
            lax.psum_scatter(grads[3], ("grp", "seq"), scatter_dimension=0, tiled=True),
            lax.psum_scatter(grads[4], ("grp", "seq"), scatter_dimension=0, tiled=True),
            lax.psum_scatter(grads[5], ("grp", "seq"), scatter_dimension=0, tiled=True),
            lax.psum_scatter(grads[6], ("grp", "seq"), scatter_dimension=0, tiled=True),
        )

    state_zero = tokens.astype(jnp.float32).reshape(-1, model_width)
    params_one = gather_layer(0)
    state_one, first_value, kept_one = forward_layer(state_zero, params_one, None)
    params_two = gather_layer(1)
    state_two, unused_value, kept_two = forward_layer(state_one, params_two, first_value)
    layer_out = state_two.astype(jnp.bfloat16).reshape(seq_count, stretch_len, model_width)
    valid_mask = (positions[None, :] < lengths[:, None]).astype(jnp.float32)
    grad_state = (cotangent.astype(jnp.float32) * valid_mask[:, :, None]).reshape(-1, model_width)
    params_two = gather_again(1)
    grad_mid, grads_two, passed = backward_layer(grad_state, params_two, kept_two, None)
    shards_two = reduce_layer(grads_two)
    params_one = gather_again(0)
    grad_inputs, grads_one, unused_grad = backward_layer(grad_mid, params_one, kept_one, passed)
    shards_one = reduce_layer(grads_one)
    stacked = tuple((jnp.stack([shards_one[member], shards_two[member]]) for member in range(7)))
    input_grad = grad_inputs.reshape(seq_count, stretch_len, model_width)
    return (
        layer_out,
        input_grad,
        stacked[0],
        stacked[1],
        stacked[2],
        stacked[3],
        stacked[4],
        stacked[5],
        stacked[6],
    )


def body_planes(
    tokens, seq_lens, norm_attn, w_qkv, w_out, norm_ffn, w_gate, w_up, w_down, cotangent
):
    seqs, stretch, width = tokens.shape
    y, c, z, x = (lax.axis_index(axis) for axis in ALL)
    lane = c * 4 + y * 2 + x
    where = jnp.stack([y, c, z, x]).astype(jnp.int32)
    rows = seqs * stretch

    def to_plane(field):
        field = jnp.transpose(field.reshape(seqs, 2, 8, 16, width), (2, 0, 1, 3, 4))
        field = lax.all_to_all(field, PLANE, 0, 0, tiled=True)
        field = lax.all_to_all(field.reshape((4, 2) + field.shape[1:]), "z", 0, 0, tiled=True)
        return jnp.transpose(field.reshape(8, seqs, 2, 16, width), (1, 0, 2, 3, 4)).reshape(rows, width)

    def from_plane(field):
        field = jnp.transpose(field.reshape(seqs, 8, 2, 16, width), (1, 0, 2, 3, 4))
        field = lax.all_to_all(field.reshape((4, 2) + field.shape[1:]), "z", 0, 0, tiled=True)
        field = lax.all_to_all(field.reshape(8, seqs, 2, 16, width), PLANE, 0, 0, tiled=True)
        return jnp.transpose(field, (1, 2, 0, 3, 4)).reshape(seqs, stretch, width)

    def gather_attn(layer):
        gain = jnp.stack([norm_attn[layer], norm_ffn[layer]], axis=1)
        gain = jnp.pad(gain, ((0, 0), (0, 126)))
        shard = jnp.concatenate([w_qkv[layer, :, : 2 * width], gain], axis=1)
        w_qk = gather_z_first(where, shard, "x", "y")
        shard = jnp.concatenate([w_qkv[layer, :, 2 * width :], w_out[layer]], axis=1)
        w_vo = gather_z_first(where, shard, "y", "x")
        gain = jnp.transpose(w_qk[:, 2 * width : 2 * width + 128])[:2].astype(F32)
        return w_qk, w_vo, gain

    def gather_ffn(layer):
        shard = jnp.concatenate([w_gate[layer], w_up[layer]], axis=1)
        w_gu = gather_z_first(where, shard, "y", "x")
        w_d = gather_x_first(where, w_down[layer])
        return w_gu, w_d

    route = []
    for sy in range(2):
        for sc in range(2):
            for sb in range(8):
                ty, tc, tx = (sb >> 1) & 1, sb >> 2, sb & 1
                route.append(((sy * 2 + sc) * 8 + sb, ((ty * 2 + tc) * 4 + 2 * sc + sy) * 2 + tx))
    lengths = lax.ppermute(seq_lens, ALL, route)[0]
    slots = stretch * 8
    half_dim = width // HEADS // 2
    freqs = 10000.0 ** (-jnp.arange(half_dim, dtype=F32) / half_dim)
    angle = jnp.arange(slots, dtype=F32)[:, None] * freqs[None, :]
    cosine, sine = jnp.cos(angle), jnp.sin(angle)
    cosine = jnp.concatenate([cosine] * 4, axis=1)
    sine = jnp.concatenate([-sine, sine] * 2, axis=1)

    def mine(table):
        own = lax.dynamic_index_in_dim(
            table.reshape(slots // 128, 8, 16, 128), lane, 1, keepdims=False
        )
        return jnp.concatenate([own.reshape(stretch, 128)] * seqs)

    my_cos, my_sin = mine(cosine), mine(sine)
    step = jnp.arange(stretch, dtype=jnp.int32)
    places = (step // 16) * 128 + lane * 16 + step % 16
    valid = (places[None, :] < lengths[:, None]).astype(F32).reshape(rows, 1)

    def exchange(field):
        return lax.all_to_all(field, PLANE, 0, 0, tiled=True)

    def forward_layer(inputs, layer, w_attn, w_ffn, first_value):
        w_qk, w_vo, gain_all = w_attn
        w_gu, w_d = w_ffn
        ffn = w_gu.shape[1] // 2
        rms_one = lax.rsqrt(jnp.mean(inputs * inputs, axis=-1, keepdims=True) + EPSILON)
        normed = (inputs * rms_one * gain_all[0]).astype(BF)
        parts = project_qkv(normed, w_qk, w_vo, my_cos, my_sin, first_value)
        pieces = exchange(parts).reshape(8, 3, seqs, stretch // 16, 16, 128)
        attended, lse = attend(lengths, pieces)
        attn_low = exchange(attended.reshape(8, rows, 128))
        attn_low = jnp.transpose(attn_low, (1, 0, 2)).reshape(rows, width)
        middle = inputs + jnp.dot(attn_low, w_vo[:, width:], preferred_element_type=F32)
        rms_two = lax.rsqrt(jnp.mean(middle * middle, axis=-1, keepdims=True) + EPSILON)
        normed_two = (middle * rms_two * gain_all[1]).astype(BF)
        gate = jnp.dot(normed_two, w_gu[:, :ffn], preferred_element_type=F32)
        up = jnp.dot(normed_two, w_gu[:, ffn:], preferred_element_type=F32)
        hidden = (jax.nn.silu(gate) * up).astype(BF)
        result = middle + jnp.dot(hidden, w_d, preferred_element_type=F32)
        kept = (
            inputs, rms_one, normed, pieces, attended, attn_low, lse, middle, rms_two,
            normed_two, gate, up, hidden,
        )
        return result, parts, kept

    def own_half(field):
        view = field.reshape(rows, 2, 2, -1)
        own = lax.dynamic_index_in_dim(view, c, 2, keepdims=False).reshape(rows, -1)
        other = lax.dynamic_index_in_dim(view, 1 - c, 2, keepdims=False).reshape(rows, -1)
        return own, swap(other, "c")

    def row_grad(left, right, right_near, tile):
        own, near = own_half(left)
        grad = weight_grad(own, near, right, right_near, tile)
        return grad.reshape(2, 4, 2, -1, grad.shape[1])

    def norm_back(grad_normed, source, rms, gain):
        scaled = source * rms
        grad_gain = jnp.sum(grad_normed * scaled, axis=0)
        weighted = grad_normed * gain
        grad = rms * (weighted - scaled * jnp.mean(weighted * scaled, axis=-1, keepdims=True))
        return grad, grad_gain

    def backward_layer(grad_in, layer, w_attn, w_ffn, kept, passed):
        w_qk, w_vo, gain_all = w_attn
        w_gu, w_d = w_ffn
        ffn = w_gu.shape[1] // 2
        (
            inputs, rms_one, normed, pieces, attended, attn_low, lse, middle, rms_two,
            normed_two, gate, up, hidden,
        ) = kept
        grad_low = grad_in.astype(BF)
        near_low = swap(grad_low, "c")
        grad_hidden = lax.dot_general(grad_low, w_d, NT, preferred_element_type=F32)
        sigma = jax.nn.sigmoid(gate)
        grad_gate = (grad_hidden * up * sigma * (1.0 + gate * (1.0 - sigma))).astype(BF)
        grad_up = (grad_hidden * gate * sigma).astype(BF)
        near_gate, near_up = swap(grad_gate, "c"), swap(grad_up, "c")
        down = reduce_rows(row_grad(hidden, grad_low, near_low, 512).reshape(2, 4, 2, -1, width), "yzx")
        gates = reduce_rows(row_grad(normed_two, grad_gate, near_gate, 256), "xyz")
        ups = reduce_rows(row_grad(normed_two, grad_up, near_up, 256), "yxz")
        grad_normed = lax.dot_general(
            grad_gate, w_gu[:, :ffn], NT, preferred_element_type=F32
        ) + lax.dot_general(grad_up, w_gu[:, ffn:], NT, preferred_element_type=F32)
        grad, gain_two = norm_back(grad_normed, middle, rms_two, gain_all[1])
        grad_middle = grad_in + grad
        grad_attn = grad_middle.astype(BF)
        near_attn = swap(grad_attn, "c")
        out = reduce_rows(row_grad(attn_low, grad_attn, near_attn, 512), "xyz")
        grad_o = lax.dot_general(
            grad_attn, w_vo[:, width:], NT, preferred_element_type=F32
        ).astype(BF)
        grad_o = jnp.transpose(grad_o.reshape(rows, 8, 128), (1, 0, 2))
        grad_o = exchange(grad_o).reshape(attended.shape)
        parts, passed = attend_back(
            lengths, pieces, attended, grad_o, lse, cosine, sine, passed
        )
        parts = exchange(parts.reshape(8, 3, rows, 128))
        grad_proj = jnp.transpose(parts, (2, 1, 0, 3)).reshape(rows, 3 * width)
        near_proj = swap(grad_proj, "c")
        half = 3 * width // 2
        left, near_left = own_half(normed)

        def qkv_grad(lo, order):
            grad = weight_grad(
                left, near_left, grad_proj[:, lo : lo + half], near_proj[:, lo : lo + half], 512
            )
            return reduce_rows(grad.reshape(2, 4, 2, -1, half), order)

        qkv = jnp.concatenate([qkv_grad(0, "yxz"), qkv_grad(half, "xyz")], axis=1)
        grad_normed = lax.dot_general(
            grad_proj[:, : 2 * width], w_qk[:, : 2 * width], NT, preferred_element_type=F32
        ) + lax.dot_general(
            grad_proj[:, 2 * width :], w_vo[:, :width], NT, preferred_element_type=F32
        )
        grad, gain_one = norm_back(grad_normed, inputs, rms_one, gain_all[0])
        return grad_middle + grad, (gain_one, qkv, out, gain_two, gates, ups, down), passed

    state = to_plane(tokens).astype(F32)
    attn_one = gather_attn(0)
    ffn_one = gather_ffn(0)
    attn_two = gather_attn(1)
    ffn_two = gather_ffn(1)
    grad = to_plane(cotangent).astype(F32) * valid
    middle, first_value, kept_one = forward_layer(state, 0, attn_one, ffn_one, None)
    final, _, kept_two = forward_layer(middle, 1, attn_two, ffn_two, first_value)
    layer_out = from_plane(final.astype(BF))
    grad, grads_two, passed = backward_layer(grad, 1, attn_two, ffn_two, kept_two, None)
    grad, grads_one, _ = backward_layer(grad, 0, attn_one, ffn_one, kept_one, passed)
    input_grad = from_plane(grad.astype(BF)).astype(F32)

    sums = jnp.stack([grads_one[0], grads_two[0], grads_one[3], grads_two[3]])
    sums = sums + swap(sums, "c")
    sums = sums + swap(sums, "x")
    sums = sums + swap(sums, "y")
    sums = sums + hop(sums, 1)
    sums = sums + hop(sums, 2)
    sums = sums.reshape(4, 32, width // 32)
    mine_sums = lax.dynamic_index_in_dim(
        sums, ((y * 2 + c) * 4 + z) * 2 + x, 1, keepdims=False
    )
    pairs = [jnp.stack([one, two]) for one, two in zip(grads_one, grads_two)]
    return (
        layer_out,
        input_grad,
        mine_sums[:2],
        pairs[1],
        pairs[2],
        mine_sums[2:],
        pairs[4],
        pairs[5],
        pairs[6],
    )


IN_SPECS = (
    ("grp", "seq", None),
    ("grp", None),
    (None, ("grp", "seq")),
    (None, ("grp", "seq"), None),
    (None, ("grp", "seq"), None),
    (None, ("grp", "seq")),
    (None, ("grp", "seq"), None),
    (None, ("grp", "seq"), None),
    (None, ("grp", "seq"), None),
    ("grp", "seq", None),
)
OUT_SPECS = (
    ("grp", "seq", None),
    ("grp", "seq", None),
    (None, ("grp", "seq")),
    (None, ("grp", "seq"), None),
    (None, ("grp", "seq"), None),
    (None, ("grp", "seq")),
    (None, ("grp", "seq"), None),
    (None, ("grp", "seq"), None),
    (None, ("grp", "seq"), None),
)


def solution(mesh):
    if mesh.shape["grp"] == 4 and mesh.shape["seq"] == 8:
        split = Mesh(mesh.devices.reshape(2, 2, 4, 2), ALL)
        names = {"grp": ("y", "c"), "seq": ("z", "x"), ("grp", "seq"): ALL, None: None}
        program = body_planes
    else:
        split = mesh
        names = {"grp": "grp", "seq": "seq", ("grp", "seq"): ("grp", "seq"), None: None}
        program = body

    def specs(table):
        return tuple(P(*(names[name] for name in row)) for row in table)

    return jax.shard_map(
        program,
        mesh=split,
        in_specs=specs(IN_SPECS),
        out_specs=specs(OUT_SPECS),
        check_vma=False,
    )
```

```python
import jax
import jax.numpy as jnp
from jax import lax
from jax.experimental import pallas as pl
from jax.experimental.pallas import tpu as pltpu
from jax.sharding import Mesh
from jax.sharding import PartitionSpec as P

HEADS = 16
EPSILON = 1e-06
NEGATIVE = -1e30
PRECISE = lax.Precision.HIGHEST
BF = jnp.bfloat16
F32 = jnp.float32
ALL = ("y", "c", "z", "x")
PLANE = ("c", "y", "x")
VMEM_BYTES = 50 * 1024 * 1024
ANY = pl.BlockSpec(memory_space=pl.ANY)
SMEM = pl.BlockSpec(memory_space=pltpu.SMEM)
NT = (((1,), (1,)), ((), ()))
TN = (((0,), (0,)), ((), ()))


def params(**more):
    return pltpu.CompilerParams(vmem_limit_bytes=VMEM_BYTES, **more)


def assemble(where, pieces, relative, with_x):
    rows, cols = pieces[0].shape[1:]
    count = len(pieces)
    lead = (2, 2, 4, 2) if with_x else (2, 2, 4)

    def kernel(where_ref, *rest):
        ins, out, held, sems = rest[:count], rest[count], rest[count + 1], rest[count + 2]
        y, c, z, x = (where_ref[n] for n in range(4))
        copies, puts = [], []
        for n in range(count):
            dy, dc, dx = relative[n]
            for dz in range(4):
                slot = (y ^ dy, c ^ dc, z ^ dz) + ((x ^ dx,) if with_x else ())
                spot = held.at[n, dz]
                copies.append(pltpu.make_async_copy(ins[n].at[dz], spot, sems.at[0, n, dz]))
                puts.append(pltpu.make_async_copy(spot, out.at[slot], sems.at[1, n, dz]))
        for copy in copies:
            copy.start()
        for copy, put in zip(copies, puts):
            copy.wait()
            put.start()
        for put in puts:
            put.wait()

    out = pl.pallas_call(
        kernel,
        in_specs=[SMEM] + [ANY] * count,
        out_specs=ANY,
        out_shape=jax.ShapeDtypeStruct(lead + (rows, cols), pieces[0].dtype),
        scratch_shapes=[
            pltpu.VMEM((count, 4, rows, cols), pieces[0].dtype),
            pltpu.SemaphoreType.DMA((2, count, 4)),
        ],
        compiler_params=params(),
        name="assemble",
    )(where, *pieces)
    return out.reshape(-1, cols)


def swap(value, axis):
    return lax.ppermute(value, axis, [(0, 1), (1, 0)])


def hop(value, offset):
    return lax.ppermute(value, "z", [(i, i ^ offset) for i in range(4)])


def gather_z_first(where, shard, first, second):
    stack = jnp.stack([shard] + [hop(shard, k) for k in (1, 2, 3)])
    near = swap(stack, first)
    ring = [((0, 0), stack), ((1, 0), near)]
    ring += [((0, 1), swap(stack, second)), ((1, 1), swap(near, second))]
    pieces, relative = [], []
    for (one, two), piece in ring:
        moved = {first: one, second: two}
        for dc, held in ((0, piece), (1, swap(piece, "c"))):
            pieces.append(held)
            relative.append((moved["y"], dc, moved["x"]))
    return assemble(where, pieces, relative, True)


def fence(*values):
    return lax.optimization_barrier(values)


class Reduction:
    def __init__(self, partial, order, names="zyx"):
        self.partial = partial
        self.order = order
        self.names = list(names)
        self.moved = None

    def send(self):
        axis, self.order = self.order[0], self.order[1:]
        dim = self.names.index(axis)
        self.names.pop(dim)
        here = lax.axis_index(axis)

        def block(slot):
            return lax.dynamic_index_in_dim(self.partial, slot, dim, keepdims=False)

        if axis == "z":
            self.moved = [hop(block(here ^ k), k) for k in (1, 2, 3)]
        else:
            self.moved = [swap(block(1 - here), axis)]
        self.partial = block(here)

    def add(self):
        total = self.partial.astype(F32)
        for part in self.moved:
            total = total + part.astype(F32)
        self.moved = None
        self.partial = total.astype(BF) if self.order else total


def send_all(reductions, *others):
    reductions = [r for r in reductions if r.order]
    held = fence(*[r.partial for r in reductions], *others)
    for reduction, partial in zip(reductions, held):
        reduction.partial = partial
        reduction.send()
    return held[len(reductions) :]


def add_all(reductions, *others):
    reductions = [r for r in reductions if r.moved is not None]
    flat = [part for r in reductions for part in r.moved]
    held = fence(*flat, *others)
    at = 0
    for reduction in reductions:
        count = len(reduction.moved)
        reduction.moved = list(held[at : at + count])
        at += count
        reduction.add()
    held = fence(*[r.partial for r in reductions], *held[at:])
    for reduction, partial in zip(reductions, held):
        reduction.partial = partial
    return held[len(reductions) :]


def turn(field, cosine, signed_sine):
    lane = lax.broadcasted_iota(jnp.int32, field.shape, 1)
    other = jnp.where(
        lane % 64 < 32, pltpu.roll(field, 96, axis=1), pltpu.roll(field, 32, axis=1)
    )
    return field * cosine + other * signed_sine


def project_qkv(normed, weights, cosine, signed_sine, first_value):
    rows, width = normed.shape
    devices = width // 128

    def kernel(normed_ref, w_q_ref, w_k_ref, w_v_ref, cos_ref, sin_ref, *rest):
        out_ref = rest[-1]
        step = pl.program_id(0)

        def product(w_ref):
            return jnp.dot(normed_ref[...], w_ref[...], preferred_element_type=F32)

        def turned(w_ref):
            field = product(w_ref)
            for n in range(devices):
                part = field[:, 128 * n : 128 * n + 128]
                out_ref[n, 0] = turn(part, cos_ref[...], sin_ref[...]).astype(BF)

        @pl.when(step == 0)
        def _():
            turned(w_q_ref)

        @pl.when(step == 1)
        def _():
            turned(w_k_ref)

        @pl.when(step == 2)
        def _():
            field = product(w_v_ref)
            for n in range(devices):
                part = field[:, 128 * n : 128 * n + 128]
                if first_value is not None:
                    part = 0.5 * part + 0.5 * rest[0][n, 0].astype(F32)
                out_ref[n, 0] = part.astype(BF)

    whole = lambda step: (0, 0)
    in_specs = [pl.BlockSpec((rows, width), whole)]
    for _, start in weights:
        in_specs.append(pl.BlockSpec((width, width), lambda step, start=start: (0, start)))
    in_specs += [pl.BlockSpec((rows, 128), whole)] * 2
    operands = [normed] + [array for array, _ in weights] + [cosine, signed_sine]
    if first_value is not None:
        in_specs.append(pl.BlockSpec((devices, 1, rows, 128), lambda step: (0, 2, 0, 0)))
        operands.append(first_value)
    return pl.pallas_call(
        kernel,
        grid=(3,),
        in_specs=in_specs,
        out_specs=pl.BlockSpec((devices, 1, rows, 128), lambda step: (0, step, 0, 0)),
        out_shape=jax.ShapeDtypeStruct((devices, 3, rows, 128), BF),
        compiler_params=params(dimension_semantics=("arbitrary",)),
        name="project_qkv",
    )(*operands)


def weight_grad(core, left_own, left_near, right_own, right_near, tile):
    rows, width = left_own.shape
    cols = right_own.shape[1]
    size = width // 4
    window = -(-size // 128) * 128
    slack = window - size

    def kernel(core_ref, lo, ln, ro, rn, out_ref, held, flipped, sems):
        @pl.when(pl.program_id(0) == 0)
        def _():
            copies = []
            for side, ref in enumerate((lo, ln)):
                for part in range(2):
                    start = 2 * part * size + core_ref[0] * (size - slack)
                    span = pl.ds(pl.multiple_of(start, 128), window)
                    copies.append(
                        pltpu.make_async_copy(
                            ref.at[:, span], held.at[side, part], sems.at[side, part]
                        )
                    )
            for copy in copies:
                copy.start()
            for copy in copies:
                copy.wait()
            for side in range(2):
                for part in range(2):
                    flipped[part, :, side * rows : side * rows + rows] = held[side, part].T

        for part in range(2):
            span = pl.ds(pl.multiple_of(core_ref[0] * slack, 16), size)
            left = flipped[part, span, :]
            total = jnp.dot(left[:, :rows], ro[...], preferred_element_type=F32)
            total += jnp.dot(left[:, rows:], rn[...], preferred_element_type=F32)
            out_ref[:, part] = total.astype(BF).reshape(4, size // 4, tile)

    block = pl.BlockSpec((rows, tile), lambda n: (0, n))
    return pl.pallas_call(
        kernel,
        grid=(cols // tile,),
        in_specs=[SMEM, ANY, ANY, block, block],
        out_specs=pl.BlockSpec((4, 2, size // 4, tile), lambda n: (0, 0, 0, n)),
        out_shape=jax.ShapeDtypeStruct((4, 2, size // 4, cols), BF),
        scratch_shapes=[
            pltpu.VMEM((2, 2, rows, window), BF),
            pltpu.VMEM((2, window, 2 * rows), BF),
            pltpu.SemaphoreType.DMA((2, 2)),
        ],
        compiler_params=params(dimension_semantics=("arbitrary",)),
        name="weight_grad",
    )(core, left_own, left_near, right_own, right_near)


def rows_of(block):
    return block.reshape(-1, 128)


def attend(length, pieces):
    tile = 256
    slots = pieces.shape[2] * 128
    tiles = slots // tile
    per = tile // 128

    def kernel(len_ref, piece_ref, out_ref, lse_ref, held, flipped, logit, sems):
        step = pl.program_id(0)

        @pl.when(step == 0)
        def _():
            copies = [
                pltpu.make_async_copy(
                    piece_ref.at[device], held.at[:, :, device], sems.at[device]
                )
                for device in range(8)
            ]
            for copy in copies:
                copy.start()
            for copy in copies:
                copy.wait()

        @pl.when(step == 0)
        def _():
            for block in range(tiles):
                key = rows_of(held[1, pl.ds(per * block, per)])
                flipped[block] = key.T

        used = len_ref[0]
        query = rows_of(held[0, pl.ds(per * step, per)]) * BF(0.125)
        lane = lax.broadcasted_iota(jnp.int32, (tile, 128), 1)
        low = lane < 64
        zero = jnp.zeros_like(query)
        queries = [jnp.where(low, query, zero), jnp.where(low, zero, query)]

        def score(block, tops, masked):
            key_t = flipped[block]
            result = []
            for head in range(2):
                field = jnp.dot(queries[head], key_t, preferred_element_type=F32)
                if masked:
                    query_pos = step * tile + lax.broadcasted_iota(jnp.int32, field.shape, 0)
                    key_pos = block * tile + lax.broadcasted_iota(jnp.int32, field.shape, 1)
                    seen = (key_pos <= query_pos) & (key_pos < used)
                    field = jnp.where(seen, field, NEGATIVE)
                logit[head, block] = field
                top = jnp.maximum(field[:, :128], field[:, 128:])
                result.append(jnp.maximum(tops[head], top))
            return tuple(result)

        full = jnp.minimum(step, used // tile)
        end = jnp.minimum(step + 1, (used + tile - 1) // tile)
        low_top = jnp.full((tile, 128), NEGATIVE, F32)
        tops = lax.fori_loop(0, full, lambda b, s: score(b, s, False), (low_top, low_top))
        tops = lax.fori_loop(full, end, lambda b, s: score(b, s, True), tops)
        tops = [jnp.max(top, axis=1, keepdims=True) for top in tops]
        wide = [jnp.broadcast_to(top, (tile, tile)) for top in tops]
        one = jnp.ones_like(query)

        def mix(block, sums):
            value = rows_of(held[2, pl.ds(per * block, per)])
            values = [jnp.where(low, value, one), jnp.where(low, one, value)]
            result = []
            for head in range(2):
                probs = jnp.exp(logit[head, block] - wide[head]).astype(BF)
                result.append(
                    sums[head] + jnp.dot(probs, values[head], preferred_element_type=F32)
                )
            return tuple(result)

        nothing = jnp.zeros((tile, 128), F32)
        sums = lax.fori_loop(0, end, mix, (nothing, nothing))
        totals = [sums[0][:, 64:65], sums[1][:, 0:1]]
        out = jnp.where(low, sums[0] / totals[0], sums[1] / totals[1])
        out = out.astype(BF).reshape(per, 8, 16, 128)
        for device in range(8):
            out_ref[device, pl.ds(per * step, per)] = out[:, device]
        level = jnp.where(low, tops[0] + jnp.log(totals[0]), tops[1] + jnp.log(totals[1])).T
        start = pl.multiple_of(step * tile, tile)
        lse_ref[0:1, pl.ds(start, tile)] = level[0:1]
        lse_ref[1:2, pl.ds(start, tile)] = level[64:65]

    return pl.pallas_call(
        kernel,
        grid=(tiles,),
        in_specs=[SMEM, ANY],
        out_specs=[
            pl.BlockSpec((8,) + pieces.shape[2:], lambda i: (0, 0, 0, 0)),
            pl.BlockSpec((8, slots), lambda i: (0, 0)),
        ],
        out_shape=[
            jax.ShapeDtypeStruct((8,) + pieces.shape[2:], BF),
            jax.ShapeDtypeStruct((8, slots), F32),
        ],
        scratch_shapes=[
            pltpu.VMEM((3, slots // 128, 8, 16, 128), BF),
            pltpu.VMEM((tiles, 128, tile), BF),
            pltpu.VMEM((2, tiles, tile, tile), F32),
            pltpu.SemaphoreType.DMA((8,)),
        ],
        compiler_params=params(dimension_semantics=("arbitrary",)),
        name="attend",
    )(length, pieces)


def attend_back(length, pieces, attended, grads, lse, cosine, signed_sine, passed):
    tile = 256
    slots = pieces.shape[2] * 128
    tiles = slots // tile
    per = tile // 128
    upper = passed is None

    def kernel(*refs):
        len_ref, piece_ref, att_ref, grad_ref, lse_ref, cos_ref, sin_ref = refs[:7]
        refs = refs[7:]
        if upper:
            passed_ref = None
            out_ref, give_ref = refs[:2]
            refs = refs[2:]
        else:
            passed_ref, out_ref = refs[:2]
            give_ref = None
            refs = refs[2:]
        held, att, grad, delta, level, query_acc, key_acc, value_acc, sems = refs
        step = pl.program_id(0)
        used = len_ref[0]

        @pl.when(step == 0)
        def _():
            copies = []
            for device in range(8):
                for n, (source, target) in enumerate(
                    (
                        (grad_ref.at[device], grad.at[:, device]),
                        (att_ref.at[device], att.at[:, device]),
                        (piece_ref.at[device], held.at[:, :, device]),
                    )
                ):
                    copies.append(pltpu.make_async_copy(source, target, sems.at[n, device]))
            for copy in copies:
                copy.start()
            for copy in copies:
                copy.wait()

        @pl.when(step == 0)
        def _():
            query_acc[...] = jnp.zeros_like(query_acc)
            line = lax.broadcasted_iota(jnp.int32, (8, 128), 0)
            lane = lax.broadcasted_iota(jnp.int32, (8, 128), 1)
            pick = jnp.where(line == lane // 64, 1.0, 0.0).astype(F32)
            for block in range(tiles):
                span = slice(tile * block, tile * block + tile)
                product = rows_of(grad[pl.ds(per * block, per)]).astype(F32) * rows_of(
                    att[pl.ds(per * block, per)]
                ).astype(F32)
                delta[:, span] = lax.dot_general(
                    pick, product, NT, precision=PRECISE, preferred_element_type=F32
                )
            place = lax.broadcasted_iota(jnp.int32, (8, slots), 1)
            level[...] = jnp.where(place < used, lse_ref[...], -NEGATIVE)

        key = rows_of(held[1, pl.ds(per * step, per)])
        value = rows_of(held[2, pl.ds(per * step, per)])
        lane = lax.broadcasted_iota(jnp.int32, (tile, 128), 1)
        low = lane < 64

        def head_part(field, head):
            keep = low if head == 0 else jnp.logical_not(low)
            return jnp.where(keep, field, jnp.zeros_like(field))

        scaled = key * BF(0.125)
        keys = [head_part(scaled, head) for head in range(2)]
        values = [head_part(value, head) for head in range(2)]
        key_acc[...] = jnp.zeros_like(key_acc)
        value_acc[...] = jnp.zeros_like(value_acc)

        def visit(block, masked):
            query = rows_of(held[0, pl.ds(per * block, per)])
            grad_out = rows_of(grad[pl.ds(per * block, per)])
            start = pl.multiple_of(block * tile, tile)
            spans = pl.ds(start, tile)
            query_sum = jnp.zeros((tile, 128), F32)
            key_sum = jnp.zeros((tile, 128), F32)
            value_sum = jnp.zeros((tile, 128), F32)
            for head in range(2):
                logits = lax.dot_general(keys[head], query, NT, preferred_element_type=F32)
                probs = jnp.exp(logits - level[head : head + 1, spans])
                if masked:
                    key_pos = lax.broadcasted_iota(jnp.int32, probs.shape, 0)
                    query_pos = lax.broadcasted_iota(jnp.int32, probs.shape, 1)
                    probs = jnp.where(key_pos <= query_pos, probs, 0.0)
                grad_probs = lax.dot_general(
                    values[head], grad_out, NT, preferred_element_type=F32
                )
                grad_logits = (probs * (grad_probs - delta[head : head + 1, spans])).astype(BF)
                value_sum += jnp.dot(
                    probs.astype(BF), head_part(grad_out, head), preferred_element_type=F32
                )
                key_sum += jnp.dot(
                    grad_logits, head_part(query, head), preferred_element_type=F32
                )
                query_sum += lax.dot_general(
                    grad_logits, keys[head], TN, preferred_element_type=F32
                )
            query_acc[spans, :] += query_sum
            key_acc[...] += key_sum
            value_acc[...] += value_sum

        end = (used + tile - 1) // tile

        @pl.when(step < end)
        def _():
            visit(step, True)

            def body(block, carry):
                visit(block, False)
                return carry

            lax.fori_loop(step + 1, end, body, 0)

        def put(member, block, field):
            field = field.astype(BF).reshape(per, 8, 16, 128)
            for device in range(8):
                out_ref[device, member, pl.ds(per * block, per)] = field[:, device]

        start = pl.multiple_of(step * tile, tile)
        spans = pl.ds(start, tile)
        key_grad = key_acc[...] * 0.125
        put(1, step, turn(key_grad, cos_ref[spans, :], -sin_ref[spans, :]))
        if upper:
            half = 0.5 * value_acc[...]
            give_ref[spans, :] = half
            put(2, step, half)
        else:
            put(2, step, value_acc[...] + passed_ref[spans, :])

        @pl.when(step == tiles - 1)
        def _():
            for block in range(tiles):
                part = slice(tile * block, tile * block + tile)
                put(0, block, turn(query_acc[part, :], cos_ref[part, :], -sin_ref[part, :]))

    flat = lambda i: (0, 0)
    table = pl.BlockSpec((slots, 128), flat)
    in_specs = [SMEM, ANY, ANY, ANY, pl.BlockSpec((8, slots), flat), table, table]
    operands = [length, pieces, attended, grads, lse, cosine, signed_sine]
    out_specs = [pl.BlockSpec(pieces.shape, lambda i: (0, 0, 0, 0, 0))]
    out_shape = [jax.ShapeDtypeStruct(pieces.shape, BF)]
    if upper:
        out_specs.append(table)
        out_shape.append(jax.ShapeDtypeStruct((slots, 128), F32))
    else:
        in_specs.append(table)
        operands.append(passed)
    outs = pl.pallas_call(
        kernel,
        grid=(tiles,),
        in_specs=in_specs,
        out_specs=out_specs,
        out_shape=out_shape,
        scratch_shapes=[
            pltpu.VMEM((3, slots // 128, 8, 16, 128), BF),
            pltpu.VMEM((slots // 128, 8, 16, 128), BF),
            pltpu.VMEM((slots // 128, 8, 16, 128), BF),
            pltpu.VMEM((8, slots), F32),
            pltpu.VMEM((8, slots), F32),
            pltpu.VMEM((slots, 128), F32),
            pltpu.VMEM((tile, 128), F32),
            pltpu.VMEM((tile, 128), F32),
            pltpu.SemaphoreType.DMA((3, 8)),
        ],
        compiler_params=params(dimension_semantics=("arbitrary",)),
        name="attend_back",
    )(*operands)
    return outs if upper else (outs[0], None)


def block_spans(total_rows):
    return [(offset, min(512, total_rows - offset)) for offset in range(0, total_rows, 512)]


def rotate(field, cosine, sine_table):
    half_dim = field.shape[-1] // 2
    first_half = field[..., :half_dim]
    second_half = field[..., half_dim:]
    return jnp.concatenate(
        [
            first_half * cosine - second_half * sine_table,
            second_half * cosine + first_half * sine_table,
        ],
        axis=-1,
    )


def allowed(query_pos, key_pos, lengths):
    causal = key_pos[None, None, :] <= query_pos[None, :, None]
    inside = key_pos[None, None, :] < lengths[:, None, None]
    return (causal & inside)[:, None, :, :]


def attend_gathered(q_heads, k_flat, v_flat, lengths, positions, score_scale):
    seq_count, stretch_len, head_count, head_dim = q_heads.shape
    first_row = jnp.int32(0)
    k_piece = lax.all_gather(k_flat, "seq", axis=1, tiled=True)
    v_piece = lax.all_gather(v_flat, "seq", axis=1, tiled=True)
    running_max = jnp.full((seq_count, head_count, stretch_len), NEGATIVE, jnp.float32)
    row_total = jnp.zeros((seq_count, head_count, stretch_len), jnp.float32)
    weighted = jnp.zeros((seq_count, stretch_len, head_count, head_dim), jnp.float32)
    for offset, block_len in block_spans(k_piece.shape[1]):
        k_block = k_piece[:, offset : offset + block_len].reshape(
            seq_count, block_len, head_count, head_dim
        )
        v_block = (
            v_piece[:, offset : offset + block_len]
            .reshape(seq_count, block_len, head_count, head_dim)
            .astype(jnp.float32)
        )
        key_pos = first_row + offset + jnp.arange(block_len, dtype=jnp.int32)
        allowed_mask = allowed(positions, key_pos, lengths)
        logits = (
            jnp.einsum("sqhd,skhd->shqk", q_heads, k_block, preferred_element_type=jnp.float32)
            * score_scale
        )
        new_max = jnp.maximum(
            running_max, jnp.max(jnp.where(allowed_mask, logits, NEGATIVE), axis=-1)
        )
        probs = jnp.where(allowed_mask, jnp.exp(logits - new_max[..., None]), 0.0)
        rescale = jnp.exp(running_max - new_max)
        row_total = row_total * rescale + jnp.sum(probs, axis=-1)
        weighted = weighted * jnp.transpose(rescale, (0, 2, 1))[..., None] + jnp.einsum(
            "shqk,skhd->sqhd", probs, v_block, precision=PRECISE, preferred_element_type=jnp.float32
        )
        running_max = new_max
    running_max, row_total, weighted = (running_max, row_total, weighted)
    attended = weighted / jnp.transpose(row_total, (0, 2, 1))[..., None]
    return (attended, running_max + jnp.log(row_total))


def attend_back_gathered(
    q_heads,
    k_heads,
    v_heads,
    q_flat,
    k_flat,
    v_flat,
    grad_heads,
    grad_flat,
    log_total,
    delta_rows,
    lengths,
    positions,
    score_scale,
):
    seq_count, stretch_len, head_count, head_dim = q_heads.shape
    zeros_heads = jnp.zeros((seq_count, stretch_len, head_count, head_dim), jnp.float32)
    carry = zeros_heads
    first_row = jnp.int32(0)
    k_piece = lax.all_gather(k_flat, "seq", axis=1, tiled=True)
    v_piece = lax.all_gather(v_flat, "seq", axis=1, tiled=True)
    for offset, block_len in block_spans(k_piece.shape[1]):
        k_block = k_piece[:, offset : offset + block_len].reshape(
            seq_count, block_len, head_count, head_dim
        )
        v_block = v_piece[:, offset : offset + block_len].reshape(
            seq_count, block_len, head_count, head_dim
        )
        key_pos = first_row + offset + jnp.arange(block_len, dtype=jnp.int32)
        allowed_mask = allowed(positions, key_pos, lengths)
        logits = (
            jnp.einsum("sqhd,skhd->shqk", q_heads, k_block, preferred_element_type=jnp.float32)
            * score_scale
        )
        probs = jnp.where(allowed_mask, jnp.exp(logits - log_total[..., None]), 0.0)
        grad_probs = jnp.einsum(
            "sqhd,skhd->shqk", grad_heads, v_block, preferred_element_type=jnp.float32
        )
        grad_logits = (probs * (grad_probs - delta_rows[..., None])).astype(jnp.bfloat16)
        carry = (
            carry
            + jnp.einsum(
                "shqk,skhd->sqhd", grad_logits, k_block, preferred_element_type=jnp.float32
            )
            * score_scale
        )
    gathered_stats = (
        lax.all_gather(log_total, "seq", axis=2, tiled=True),
        lax.all_gather(delta_rows, "seq", axis=2, tiled=True),
    )
    first_row = jnp.int32(0)
    q_piece = lax.all_gather(q_flat, "seq", axis=1, tiled=True)
    g_piece = lax.all_gather(grad_flat, "seq", axis=1, tiled=True)
    grad_key = zeros_heads
    grad_value = zeros_heads
    for offset, block_len in block_spans(q_piece.shape[1]):
        q_block = q_piece[:, offset : offset + block_len].reshape(
            seq_count, block_len, head_count, head_dim
        )
        g_block = g_piece[:, offset : offset + block_len].reshape(
            seq_count, block_len, head_count, head_dim
        )
        query_pos = first_row + offset + jnp.arange(block_len, dtype=jnp.int32)
        allowed_mask = allowed(query_pos, positions, lengths)
        lse_block = lax.dynamic_slice_in_dim(gathered_stats[0], offset, block_len, 2)
        delta_block = lax.dynamic_slice_in_dim(gathered_stats[1], offset, block_len, 2)
        logits = (
            jnp.einsum("sqhd,skhd->shqk", q_block, k_heads, preferred_element_type=jnp.float32)
            * score_scale
        )
        probs = jnp.where(allowed_mask, jnp.exp(logits - lse_block[..., None]), 0.0)
        grad_value = grad_value + jnp.einsum(
            "shqk,sqhd->skhd",
            probs,
            g_block.astype(jnp.float32),
            precision=PRECISE,
            preferred_element_type=jnp.float32,
        )
        grad_probs = jnp.einsum(
            "sqhd,skhd->shqk", g_block, v_heads, preferred_element_type=jnp.float32
        )
        grad_logits = (probs * (grad_probs - delta_block[..., None])).astype(jnp.bfloat16)
        grad_key = (
            grad_key
            + jnp.einsum(
                "shqk,sqhd->skhd", grad_logits, q_block, preferred_element_type=jnp.float32
            )
            * score_scale
        )
    grad_key, grad_value = (grad_key, grad_value)
    return (carry, grad_key, grad_value)


def body(tokens, seq_lens, norm_attn, w_qkv, w_out, norm_ffn, w_gate, w_up, w_down, cotangent):
    seq_count, stretch_len, model_width = tokens.shape
    head_count = HEADS
    head_dim = model_width // head_count
    score_scale = head_dim ** (-0.5)
    lengths = seq_lens[0]
    positions = lax.axis_index("seq") * stretch_len + jnp.arange(stretch_len, dtype=jnp.int32)
    half_dim = head_dim // 2
    freqs = 10000.0 ** (-jnp.arange(half_dim, dtype=jnp.float32) / half_dim)
    angle = positions.astype(jnp.float32)[:, None] * freqs[None, :]
    cosine = jnp.cos(angle)[:, None, :]
    sine_table = jnp.sin(angle)[:, None, :]

    def heads_of(field):
        return field.reshape(seq_count, stretch_len, head_count, head_dim)

    def gather_layer(layer_index):
        return (
            lax.all_gather(norm_attn[layer_index], ("grp", "seq"), axis=0, tiled=True),
            lax.all_gather(w_qkv[layer_index], ("grp", "seq"), axis=0, tiled=True),
            lax.all_gather(w_out[layer_index], ("grp", "seq"), axis=0, tiled=True),
            lax.all_gather(norm_ffn[layer_index], ("grp", "seq"), axis=0, tiled=True),
            lax.all_gather(w_gate[layer_index], ("grp", "seq"), axis=0, tiled=True),
            lax.all_gather(w_up[layer_index], ("grp", "seq"), axis=0, tiled=True),
            lax.all_gather(w_down[layer_index], ("grp", "seq"), axis=0, tiled=True),
        )

    def gather_again(layer_index):
        return (
            lax.all_gather(norm_attn[layer_index], ("grp", "seq"), axis=0, tiled=True),
            lax.all_gather(w_qkv[layer_index], ("grp", "seq"), axis=0, tiled=True),
            lax.all_gather(w_out[layer_index], ("grp", "seq"), axis=0, tiled=True),
            lax.all_gather(norm_ffn[layer_index], ("grp", "seq"), axis=0, tiled=True),
            lax.all_gather(w_gate[layer_index], ("grp", "seq"), axis=0, tiled=True),
            lax.all_gather(w_up[layer_index], ("grp", "seq"), axis=0, tiled=True),
            lax.all_gather(w_down[layer_index], ("grp", "seq"), axis=0, tiled=True),
        )

    def forward_layer(inputs, params, first_value):
        gain_one, mat_qkv, mat_out, gain_two, mat_gate, mat_up, mat_down = params
        rms_one = lax.rsqrt(jnp.mean(inputs * inputs, axis=-1, keepdims=True) + EPSILON)
        normed = (inputs * rms_one * gain_one.astype(jnp.float32)).astype(jnp.bfloat16)
        projected = jnp.dot(normed, mat_qkv, preferred_element_type=jnp.float32)
        query_raw = projected[:, :model_width]
        key_raw = projected[:, model_width : 2 * model_width]
        value_raw = projected[:, 2 * model_width :]
        if first_value is None:
            values = value_raw.astype(jnp.bfloat16)
        else:
            values = (0.5 * value_raw + 0.5 * first_value.astype(jnp.float32)).astype(jnp.bfloat16)
        query_rot = rotate(heads_of(query_raw), cosine, sine_table).astype(jnp.bfloat16)
        key_rot = rotate(heads_of(key_raw), cosine, sine_table).astype(jnp.bfloat16)
        attended, log_total = attend_gathered(
            query_rot,
            key_rot.reshape(seq_count, stretch_len, model_width),
            values.reshape(seq_count, stretch_len, model_width),
            lengths,
            positions,
            score_scale,
        )
        attn_low = attended.reshape(-1, model_width).astype(jnp.bfloat16)
        middle = inputs + jnp.dot(attn_low, mat_out, preferred_element_type=jnp.float32)
        rms_two = lax.rsqrt(jnp.mean(middle * middle, axis=-1, keepdims=True) + EPSILON)
        normed_two = (middle * rms_two * gain_two.astype(jnp.float32)).astype(jnp.bfloat16)
        gate_pre = jnp.dot(normed_two, mat_gate, preferred_element_type=jnp.float32)
        up_pre = jnp.dot(normed_two, mat_up, preferred_element_type=jnp.float32)
        hidden = (jax.nn.silu(gate_pre) * up_pre).astype(jnp.bfloat16)
        result = middle + jnp.dot(hidden, mat_down, preferred_element_type=jnp.float32)
        kept = (
            inputs,
            rms_one,
            normed,
            query_rot,
            key_rot,
            values,
            attended,
            attn_low,
            log_total,
            middle,
            rms_two,
            normed_two,
            gate_pre,
            up_pre,
            hidden,
        )
        return (result, values, kept)

    def backward_layer(grad_in, params, kept, first_grad):
        gain_one, mat_qkv, mat_out, gain_two, mat_gate, mat_up, mat_down = params
        (
            inputs,
            rms_one,
            normed,
            query_rot,
            key_rot,
            values,
            attended,
            attn_low,
            log_total,
            middle,
            rms_two,
            normed_two,
            gate_pre,
            up_pre,
            hidden,
        ) = kept
        grad_low = grad_in.astype(jnp.bfloat16)
        grad_down = jnp.einsum("nf,nd->fd", hidden, grad_low, preferred_element_type=jnp.float32)
        grad_hidden = jnp.einsum(
            "nd,fd->nf", grad_low, mat_down, preferred_element_type=jnp.float32
        )
        sigma = jax.nn.sigmoid(gate_pre)
        grad_gate_pre = (grad_hidden * up_pre * sigma * (1.0 + gate_pre * (1.0 - sigma))).astype(
            jnp.bfloat16
        )
        grad_up_pre = (grad_hidden * gate_pre * sigma).astype(jnp.bfloat16)
        grad_gate = jnp.einsum(
            "nd,nf->df", normed_two, grad_gate_pre, preferred_element_type=jnp.float32
        )
        grad_up = jnp.einsum(
            "nd,nf->df", normed_two, grad_up_pre, preferred_element_type=jnp.float32
        )
        grad_normed_two = jnp.einsum(
            "nf,df->nd", grad_gate_pre, mat_gate, preferred_element_type=jnp.float32
        ) + jnp.einsum("nf,df->nd", grad_up_pre, mat_up, preferred_element_type=jnp.float32)
        scaled_two = middle * rms_two
        grad_gain_two = jnp.sum(grad_normed_two * scaled_two, axis=0)
        weighted_two = grad_normed_two * gain_two.astype(jnp.float32)
        grad_middle = grad_in + rms_two * (
            weighted_two - scaled_two * jnp.mean(weighted_two * scaled_two, axis=-1, keepdims=True)
        )
        grad_attn = grad_middle.astype(jnp.bfloat16)
        grad_out_mat = jnp.einsum(
            "nd,ne->de", attn_low, grad_attn, preferred_element_type=jnp.float32
        )
        grad_attended = jnp.einsum(
            "ne,de->nd", grad_attn, mat_out, preferred_element_type=jnp.float32
        ).astype(jnp.bfloat16)
        grad_heads = heads_of(grad_attended)
        delta_rows = jnp.transpose(
            jnp.sum(grad_heads.astype(jnp.float32) * attended, axis=-1), (0, 2, 1)
        )
        grad_query, grad_key, grad_value = attend_back_gathered(
            query_rot,
            key_rot,
            heads_of(values),
            query_rot.reshape(seq_count, stretch_len, model_width),
            key_rot.reshape(seq_count, stretch_len, model_width),
            values.reshape(seq_count, stretch_len, model_width),
            grad_heads,
            grad_attended.reshape(seq_count, stretch_len, model_width),
            log_total,
            delta_rows,
            lengths,
            positions,
            score_scale,
        )
        grad_query_raw = rotate(grad_query, cosine, -sine_table).reshape(-1, model_width)
        grad_key_raw = rotate(grad_key, cosine, -sine_table).reshape(-1, model_width)
        grad_value_flat = grad_value.reshape(-1, model_width)
        if first_grad is None:
            grad_value_raw = 0.5 * grad_value_flat
            passed = 0.5 * grad_value_flat
        else:
            grad_value_raw = grad_value_flat + first_grad
            passed = None
        grad_proj = jnp.concatenate([grad_query_raw, grad_key_raw, grad_value_raw], axis=-1).astype(
            jnp.bfloat16
        )
        grad_qkv = jnp.einsum("nd,ne->de", normed, grad_proj, preferred_element_type=jnp.float32)
        grad_normed = jnp.einsum(
            "ne,de->nd", grad_proj, mat_qkv, preferred_element_type=jnp.float32
        )
        scaled_one = inputs * rms_one
        grad_gain_one = jnp.sum(grad_normed * scaled_one, axis=0)
        weighted_one = grad_normed * gain_one.astype(jnp.float32)
        grad_inputs = grad_middle + rms_one * (
            weighted_one - scaled_one * jnp.mean(weighted_one * scaled_one, axis=-1, keepdims=True)
        )
        return (
            grad_inputs,
            (grad_gain_one, grad_qkv, grad_out_mat, grad_gain_two, grad_gate, grad_up, grad_down),
            passed,
        )

    def reduce_layer(grads):
        return (
            lax.psum_scatter(grads[0], ("grp", "seq"), scatter_dimension=0, tiled=True),
            lax.psum_scatter(grads[1], ("grp", "seq"), scatter_dimension=0, tiled=True),
            lax.psum_scatter(grads[2], ("grp", "seq"), scatter_dimension=0, tiled=True),
            lax.psum_scatter(grads[3], ("grp", "seq"), scatter_dimension=0, tiled=True),
            lax.psum_scatter(grads[4], ("grp", "seq"), scatter_dimension=0, tiled=True),
            lax.psum_scatter(grads[5], ("grp", "seq"), scatter_dimension=0, tiled=True),
            lax.psum_scatter(grads[6], ("grp", "seq"), scatter_dimension=0, tiled=True),
        )

    state_zero = tokens.astype(jnp.float32).reshape(-1, model_width)
    params_one = gather_layer(0)
    state_one, first_value, kept_one = forward_layer(state_zero, params_one, None)
    params_two = gather_layer(1)
    state_two, unused_value, kept_two = forward_layer(state_one, params_two, first_value)
    layer_out = state_two.astype(jnp.bfloat16).reshape(seq_count, stretch_len, model_width)
    valid_mask = (positions[None, :] < lengths[:, None]).astype(jnp.float32)
    grad_state = (cotangent.astype(jnp.float32) * valid_mask[:, :, None]).reshape(-1, model_width)
    params_two = gather_again(1)
    grad_mid, grads_two, passed = backward_layer(grad_state, params_two, kept_two, None)
    shards_two = reduce_layer(grads_two)
    params_one = gather_again(0)
    grad_inputs, grads_one, unused_grad = backward_layer(grad_mid, params_one, kept_one, passed)
    shards_one = reduce_layer(grads_one)
    stacked = tuple((jnp.stack([shards_one[member], shards_two[member]]) for member in range(7)))
    input_grad = grad_inputs.reshape(seq_count, stretch_len, model_width)
    return (
        layer_out,
        input_grad,
        stacked[0],
        stacked[1],
        stacked[2],
        stacked[3],
        stacked[4],
        stacked[5],
        stacked[6],
    )


def body_planes(
    tokens, seq_lens, norm_attn, w_qkv, w_out, norm_ffn, w_gate, w_up, w_down, cotangent
):
    seqs, stretch, width = tokens.shape
    y, c, z, x = (lax.axis_index(axis) for axis in ALL)
    lane = c * 4 + y * 2 + x
    where = jnp.stack([y, c, z, x]).astype(jnp.int32)
    rows = seqs * stretch
    ffn = w_gate.shape[2]

    def exchange(field):
        return lax.all_to_all(field, PLANE, 0, 0, tiled=True)

    def exchange_z(field):
        shape = field.shape
        moved = lax.all_to_all(field.reshape((4, 2) + shape[1:]), "z", 0, 0, tiled=True)
        return moved.reshape(shape)

    def cut_blocks(field):
        field = field.reshape(seqs, 2, 8, 16, width)
        return jnp.transpose(field, (2, 0, 1, 3, 4))

    def join_stripes(field):
        return jnp.transpose(field, (1, 0, 2, 3, 4)).reshape(rows, width)

    def cut_stripes(field):
        return jnp.transpose(field.reshape(seqs, 8, 2, 16, width), (1, 0, 2, 3, 4))

    def join_blocks(field):
        return jnp.transpose(field, (1, 2, 0, 3, 4)).reshape(seqs, stretch, width)

    def gather_all(shard):
        return lax.all_gather(shard, ALL, axis=0, tiled=True)

    def gain_shard(layer):
        gain = jnp.stack([norm_attn[layer], norm_ffn[layer]], axis=1)
        return jnp.pad(gain, ((0, 0), (0, 126)))

    def gains(columns):
        return jnp.transpose(columns)[:2].astype(F32)

    def gather_ffn(layer, *after):
        cuts = [w_gate[layer], w_up[layer], pack(w_down[layer])]
        if layer == 0:
            cuts.append(w_out[layer])
        shard = jnp.concatenate(cuts, axis=1)
        if after:
            shard, *_ = fence(shard, *after)
        gathered = gather_all(shard)
        packed = gathered[:, 2 * ffn : 2 * ffn + 3 * width]
        w_d = unpack(packed.reshape(32, -1, 3 * width)).reshape(-1, width)
        return gathered, w_d

    def pack(rows_of_down):
        tall = w_qkv.shape[1]
        spare = 3 * tall - rows_of_down.shape[-2]
        lead = [(0, 0)] * (rows_of_down.ndim - 2)
        padded = jnp.pad(rows_of_down, lead + [(0, spare), (0, 0)])
        cuts = [padded[..., n * tall : n * tall + tall, :] for n in range(3)]
        return jnp.concatenate(cuts, axis=-1)

    def unpack(packed):
        cols = packed.shape[-1] // 3
        cuts = [packed[..., n * cols : n * cols + cols] for n in range(3)]
        return jnp.concatenate(cuts, axis=-2)[..., : w_down.shape[1], :]

    def gather_first():
        shard = w_qkv[0]
        first = jnp.concatenate([shard[:, :width], gain_shard(0)], axis=1)
        w_q = gather_z_first(where, first, "x", "y")
        w_k = gather_z_first(where, shard[:, width : 2 * width], "y", "x")
        w_v = gather_z_first(where, shard[:, 2 * width :], "x", "y")
        weights = [(w_q, 0), (w_k, 0), (w_v, 0)]
        return weights, [w_q[:, :width], w_k, w_v], gains(w_q[:, width:])

    def gather_second(*after):
        shard = jnp.concatenate([w_qkv[1], w_out[1], gain_shard(1)], axis=1)
        shard, *_ = fence(shard, *after)
        whole = gather_all(shard)
        weights = [(whole, 0), (whole, 1), (whole, 2)]
        turned = [whole[:, : 3 * width]]
        return weights, turned, whole[:, 3 * width : 4 * width], gains(whole[:, 4 * width :])

    here = z * 2 + x
    routes = []
    for k in range(8):
        route = []
        for sy in range(2):
            for sc in range(2):
                for sb in range(8):
                    to = sb ^ k
                    target = (((to >> 1) & 1) * 2 + (to >> 2)) * 4 + 2 * sc + sy
                    route.append(((sy * 2 + sc) * 8 + sb, target * 2 + (to & 1)))
        routes.append(route)
    lengths = lax.ppermute(seq_lens, ALL, routes[0])[0]
    length = [lengths[n : n + 1] for n in range(2)]
    slots = stretch * 8
    half_dim = width // HEADS // 2
    freqs = 10000.0 ** (-jnp.arange(half_dim, dtype=F32) / half_dim)
    angle = jnp.arange(slots, dtype=F32)[:, None] * freqs[None, :]
    cosine, sine = jnp.cos(angle), jnp.sin(angle)
    cosine = jnp.concatenate([cosine] * 4, axis=1)
    sine = jnp.concatenate([-sine, sine] * 2, axis=1)

    def mine(table):
        own = lax.dynamic_index_in_dim(
            table.reshape(slots // 128, 8, 16, 128), lane, 1, keepdims=False
        )
        return own.reshape(stretch, 128)

    my_cos, my_sin = mine(cosine), mine(sine)
    step = jnp.arange(stretch, dtype=jnp.int32)
    places = (step // 16) * 128 + lane * 16 + step % 16
    valid = (places[None, :] < lengths[:, None]).astype(F32).reshape(rows, 1)

    def halves(field):
        return field[:stretch], field[stretch:]

    def forward_attention(inputs, weights, gain, first_value, *after):
        rms_one = lax.rsqrt(jnp.mean(inputs * inputs, axis=-1, keepdims=True) + EPSILON)
        normed = (inputs * rms_one * gain[0]).astype(BF)
        top, bottom = halves(normed)
        parts_a = project_qkv(top, weights, my_cos, my_sin, first_value and first_value[0])
        parts_b = project_qkv(bottom, weights, my_cos, my_sin, first_value and first_value[1])
        shape = (8, 3, stretch // 16, 16, 128)
        pieces_a = exchange(parts_a)
        pieces_a, sent_b = fence(pieces_a, parts_b)
        pieces_a = pieces_a.reshape(shape)
        pieces_b = exchange(sent_b)
        attended_a, lse_a = attend(length[0], pieces_a)
        attended_a, pieces_b, *_ = fence(attended_a, pieces_b, *after)
        pieces_b = pieces_b.reshape(shape)
        low_a = exchange(attended_a.reshape(8, stretch, 128))
        attended_b, lse_b = attend(length[1], pieces_b)
        low_a, sent_b = fence(low_a, attended_b)
        low_b = exchange(sent_b.reshape(8, stretch, 128))
        attn_low = jnp.concatenate(
            [jnp.transpose(low, (1, 0, 2)).reshape(stretch, width) for low in (low_a, low_b)]
        )
        kept = (
            inputs, rms_one, normed, (pieces_a, pieces_b), (attended_a, attended_b), attn_low,
            (lse_a, lse_b),
        )
        return attn_low, (parts_a, parts_b), kept

    def forward_ffn(inputs, attn_low, w_o, w_ffn, gain):
        w_gu, w_d = w_ffn
        middle = inputs + jnp.dot(attn_low, w_o, preferred_element_type=F32)
        rms_two = lax.rsqrt(jnp.mean(middle * middle, axis=-1, keepdims=True) + EPSILON)
        normed_two = (middle * rms_two * gain[1]).astype(BF)
        gate = jnp.dot(normed_two, w_gu[:, :ffn], preferred_element_type=F32)
        up = jnp.dot(normed_two, w_gu[:, ffn : 2 * ffn], preferred_element_type=F32)
        hidden = (jax.nn.silu(gate) * up).astype(BF)
        result = middle + jnp.dot(hidden, w_d, preferred_element_type=F32)
        return result, (middle, rms_two, normed_two, gate, up, hidden)

    def near(field):
        return swap(field, "c")

    def norm_back(grad_normed, source, rms, gain):
        scaled = source * rms
        weighted = grad_normed * gain
        return rms * (weighted - scaled * jnp.mean(weighted * scaled, axis=-1, keepdims=True))

    def chip_grad(left, right, tile):
        grad = weight_grad(core, left[0], left[1], right[0], right[1], tile)
        return grad.reshape(4, 2, 2, -1, grad.shape[-1])

    def start_sum(left, right, tile, order):
        return Reduction(chip_grad(left, right, tile), order)

    def dots(grads, weights):
        total = None
        for grad, weight in zip(grads, weights):
            part = lax.dot_general(grad, weight, NT, preferred_element_type=F32)
            total = part if total is None else total + part
        return total

    def qkv_sums(one, proj):
        half = 3 * width // 2
        sums = []
        for lo, order in ((0, "yxz"), (half, "xyz")):
            right = (proj[0][:, lo : lo + half], proj[1][:, lo : lo + half])
            sums.append(start_sum(one, right, 512, order))
        return sums

    def ffn_grads(two, gates, ups, hid, low):
        grads = [chip_grad(two, gates, 256), chip_grad(two, ups, 256)]
        return jnp.concatenate(grads + [pack(chip_grad(hid, low, 512))], axis=-1)

    def backward_layer(grad_in, w_attn, w_ffn, kept, passed, pending, upper_sum, beside):
        w_turned, w_o, gain = w_attn
        w_gu, w_d = w_ffn
        (
            inputs, rms_one, normed, pieces, attended, attn_low, lse, middle, rms_two,
            normed_two, gate, up, hidden,
        ) = kept
        grad_low = grad_in.astype(BF)
        low = (grad_low, near(grad_low))
        hid = (hidden, near(hidden))
        two = (normed_two, near(normed_two))
        att = (attn_low, near(attn_low))
        one = (normed, near(normed))
        grad_hidden = lax.dot_general(grad_low, w_d, NT, preferred_element_type=F32)
        sigma = jax.nn.sigmoid(gate)
        grad_gate = (grad_hidden * up * sigma * (1.0 + gate * (1.0 - sigma))).astype(BF)
        grad_up = (grad_hidden * gate * sigma).astype(BF)
        gates = (grad_gate, near(grad_gate))
        ups = (grad_up, near(grad_up))
        if upper_sum is not None:
            summed = ffn_grads(two, gates, ups, hid, low)
            summed, grad_gate, grad_up = add_all(pending, summed, grad_gate, grad_up)
            summed, grad_gate, grad_up = send_all(pending, summed, grad_gate, grad_up)
            summed = lax.psum_scatter(summed, "z", scatter_dimension=0, tiled=True)[0]
        grad_normed = dots([grad_gate, grad_up], [w_gu[:, :ffn], w_gu[:, ffn : 2 * ffn]])
        grad_middle = grad_in + norm_back(grad_normed, middle, rms_two, gain[1])
        grad_attn = grad_middle.astype(BF)
        mid = (grad_attn, near(grad_attn))
        grad_o = lax.dot_general(grad_attn, w_o, NT, preferred_element_type=F32).astype(BF)
        grad_o = jnp.transpose(grad_o.reshape(rows, 8, 128), (1, 0, 2))
        grad_o, beside = fence(grad_o, beside)

        if upper_sum is None:
            held = fence(grad_o, *two, *gates, *ups, *hid, *low)
            grad_o, two, gates, ups = held[0], held[1:3], held[3:5], held[5:7]
            hid, low = held[7:9], held[9:11]
            grad_o = exchange(grad_o)
            summed = ffn_grads(two, gates, ups, hid, low)
            summed, grad_o = fence(summed, grad_o)
            summed = lax.psum_scatter(summed, "z", scatter_dimension=0, tiled=True)[0]
        else:
            grad_o = exchange(grad_o)
        (grad_o,) = add_all(pending, grad_o)
        if upper_sum is not None:
            upper_sum, grad_o = fence(upper_sum, grad_o)
            half = upper_sum.shape[-1] // 2
            pending.append(Reduction(upper_sum[..., :half], "xy", "yx"))
            pending.append(Reduction(upper_sum[..., half:], "yx", "yx"))
        (grad_o,) = send_all(pending, grad_o)
        grad_o = grad_o.reshape(8, 2, stretch // 16, 16, 128)
        cos_sin = (cosine, sine)
        parts_a, pass_a = attend_back(
            length[0], pieces[0], attended[0], grad_o[:, 0], lse[0], *cos_sin, passed and passed[0]
        )
        parts_a, grad_b = fence(parts_a, grad_o[:, 1])
        if upper_sum is not None:
            parts_a, grad_b = add_all(pending[3:], parts_a, grad_b)
            parts_a, grad_b = send_all(pending[3:], parts_a, grad_b)
        moved_a = exchange(parts_a.reshape(8, 3, stretch, 128))
        parts_b, pass_b = attend_back(
            length[1], pieces[1], attended[1], grad_b, lse[1], *cos_sin, passed and passed[1]
        )
        moved_a, parts_b, *held = fence(moved_a, parts_b, *att, *mid)
        att, mid = held[:2], held[2:4]
        moved_b = exchange(parts_b.reshape(8, 3, stretch, 128))
        out = start_sum(att, mid, 512, "xyz")
        if upper_sum is not None:
            summed, moved_b = add_all(pending, summed, moved_b)
            half = summed.shape[-1] // 2
            summed = [
                Reduction(summed[..., :half], "xy", "yx"),
                Reduction(summed[..., half:], "yx", "yx"),
            ]
            (moved_b,) = send_all([out] + summed, moved_b)
        else:
            (moved_b,) = send_all([out], moved_b)
        grad_proj = jnp.concatenate(
            [
                jnp.transpose(moved, (2, 1, 0, 3)).reshape(stretch, 3 * width)
                for moved in (moved_a, moved_b)
            ]
        )
        proj = (grad_proj, near(grad_proj))
        cuts, at = [], 0
        for weight in w_turned:
            cuts.append(grad_proj[:, at : at + weight.shape[1]])
            at += weight.shape[1]
        grad_normed = dots(cuts, w_turned)
        grad = grad_middle + norm_back(grad_normed, inputs, rms_one, gain[0])
        return grad, summed, out, one + proj, (pass_a, pass_b), beside

    core = c.astype(jnp.int32).reshape(1)
    ffn_one = gather_ffn(0)
    state = join_stripes(exchange_z(exchange(cut_blocks(tokens)))).astype(F32)
    qkv_one, turned_one, gain_one = gather_first()
    low_one, first_value, kept_one = forward_attention(
        state, qkv_one, gain_one, None, ffn_one[0]
    )
    qkv_two, turned_two, out_two, gain_two = gather_second(ffn_one[0], kept_one[4][0])
    ffn_two = gather_ffn(1, low_one)
    out_one = ffn_one[0][:, 2 * ffn + 3 * width :]
    low_one, other = fence(low_one, cut_blocks(cotangent))
    other = [
        lax.ppermute(lax.dynamic_index_in_dim(other, here ^ k, 0, keepdims=False), ALL, routes[k])
        for k in range(8)
    ]
    middle, more = forward_ffn(state, low_one, out_one, ffn_one, gain_one)
    kept_one += more
    low_two, _, kept_two = forward_attention(middle, qkv_two, gain_two, first_value)
    final, more = forward_ffn(middle, low_two, out_two, ffn_two, gain_two)
    kept_two += more
    final, *other = fence(final, *other)
    grad = jnp.zeros((8, seqs, 2, 16, width), BF)
    for k in range(8):
        grad = lax.dynamic_update_index_in_dim(grad, other[k], lane ^ k, 0)
    grad = join_stripes(grad).astype(F32) * valid
    layer_out = exchange_z(cut_stripes(final.astype(BF)))
    grad, ffn_two_sum, out_sum, todo, passed, layer_out = backward_layer(
        grad, (turned_two, out_two, gain_two), ffn_two, kept_two, None, [], None, layer_out
    )
    grad, *todo = fence(grad, *todo)
    sums_two = [out_sum] + qkv_sums(todo[:2], todo[2:])
    grad, layer_out = send_all(sums_two[1:], grad, layer_out)
    layer_out = exchange(layer_out)
    grad, ffn_one_sum, out_sum, todo, _, layer_out = backward_layer(
        grad,
        (turned_one, out_one, gain_one),
        ffn_one,
        kept_one,
        passed,
        sums_two,
        ffn_two_sum,
        layer_out,
    )
    layer_out = join_blocks(layer_out)
    grad, *todo = fence(grad, *todo)
    input_grad = exchange_z(cut_stripes(grad.astype(BF)))
    last = qkv_sums(todo[:2], todo[2:])
    (input_grad,) = send_all(last, input_grad)
    input_grad = exchange(input_grad)
    rest = ffn_one_sum + [out_sum]
    add_all(rest, *[r.partial for r in last])
    send_all(rest)
    for _ in range(2):
        add_all(last)
        send_all(last)
        add_all(rest, *[r.partial for r in last])
        send_all(rest)
    add_all(last + rest)
    input_grad = join_blocks(input_grad).astype(F32)
    sums_one = [out_sum] + last
    sums_two, late, lower = sums_two[:3], sums_two[3:], ffn_one_sum

    out_grad, qkv_grad, gate_grad, up_grad, down_grad = [], [], [], [], []
    for sums, halves_of in ((sums_one, lower), (sums_two, late)):
        out_grad.append(sums[0].partial)
        qkv_grad.append(jnp.concatenate([sums[1].partial, sums[2].partial], axis=1))
        field = jnp.concatenate([r.partial for r in halves_of], axis=1)
        gate_grad.append(field[:, :ffn])
        up_grad.append(field[:, ffn : 2 * ffn])
        down_grad.append(unpack(field[:, 2 * ffn :]))

    def gain_grad(pairs, gain):
        total = sum(jnp.sum(w.astype(F32) * grad, axis=1) for w, grad in pairs)
        return total / gain.astype(F32)

    attn_gain = [gain_grad([(w_qkv[n], qkv_grad[n])], norm_attn[n]) for n in range(2)]
    ffn_gain = [
        gain_grad([(w_gate[n], gate_grad[n]), (w_up[n], up_grad[n])], norm_ffn[n])
        for n in range(2)
    ]
    return (
        layer_out,
        input_grad,
        jnp.stack(attn_gain),
        jnp.stack(qkv_grad),
        jnp.stack(out_grad),
        jnp.stack(ffn_gain),
        jnp.stack(gate_grad),
        jnp.stack(up_grad),
        jnp.stack(down_grad),
    )


IN_SPECS = (
    ("grp", "seq", None),
    ("grp", None),
    (None, ("grp", "seq")),
    (None, ("grp", "seq"), None),
    (None, ("grp", "seq"), None),
    (None, ("grp", "seq")),
    (None, ("grp", "seq"), None),
    (None, ("grp", "seq"), None),
    (None, ("grp", "seq"), None),
    ("grp", "seq", None),
)
OUT_SPECS = (
    ("grp", "seq", None),
    ("grp", "seq", None),
    (None, ("grp", "seq")),
    (None, ("grp", "seq"), None),
    (None, ("grp", "seq"), None),
    (None, ("grp", "seq")),
    (None, ("grp", "seq"), None),
    (None, ("grp", "seq"), None),
    (None, ("grp", "seq"), None),
)


def solution(mesh):
    if mesh.shape["grp"] == 4 and mesh.shape["seq"] == 8:
        split = Mesh(mesh.devices.reshape(2, 2, 4, 2), ALL)
        names = {"grp": ("y", "c"), "seq": ("z", "x"), ("grp", "seq"): ALL, None: None}
        program = body_planes
    else:
        split = mesh
        names = {"grp": "grp", "seq": "seq", ("grp", "seq"): ("grp", "seq"), None: None}
        program = body

    def specs(table):
        return tuple(P(*(names[name] for name in row)) for row in table)

    return jax.shard_map(
        program,
        mesh=split,
        in_specs=specs(IN_SPECS),
        out_specs=specs(OUT_SPECS),
        check_vma=False,
    )
```

```python
import jax
import jax.numpy as jnp
from jax import lax
from jax.experimental import pallas as pl
from jax.experimental.pallas import tpu as pltpu
from jax.sharding import Mesh
from jax.sharding import PartitionSpec as P

HEADS = 16
EPSILON = 1e-06
NEGATIVE = -1e30
PRECISE = lax.Precision.HIGHEST
BF = jnp.bfloat16
F32 = jnp.float32
ALL = ("y", "c", "z", "x")
PLANE = ("c", "y", "x")
VMEM_BYTES = 50 * 1024 * 1024
ANY = pl.BlockSpec(memory_space=pl.ANY)
SMEM = pl.BlockSpec(memory_space=pltpu.SMEM)
NT = (((1,), (1,)), ((), ()))
TN = (((0,), (0,)), ((), ()))


def params(**more):
    return pltpu.CompilerParams(vmem_limit_bytes=VMEM_BYTES, **more)


def assemble(where, pieces, relative, with_x):
    rows, cols = pieces[0].shape[1:]
    count = len(pieces)
    lead = (2, 2, 4, 2) if with_x else (2, 2, 4)

    def kernel(where_ref, *rest):
        ins, out, held, sems = rest[:count], rest[count], rest[count + 1], rest[count + 2]
        y, c, z, x = (where_ref[n] for n in range(4))
        copies, puts = [], []
        for n in range(count):
            dy, dc, dx = relative[n]
            for dz in range(4):
                slot = (y ^ dy, c ^ dc, z ^ dz) + ((x ^ dx,) if with_x else ())
                spot = held.at[n, dz]
                copies.append(pltpu.make_async_copy(ins[n].at[dz], spot, sems.at[0, n, dz]))
                puts.append(pltpu.make_async_copy(spot, out.at[slot], sems.at[1, n, dz]))
        for copy in copies:
            copy.start()
        for copy, put in zip(copies, puts):
            copy.wait()
            put.start()
        for put in puts:
            put.wait()

    out = pl.pallas_call(
        kernel,
        in_specs=[SMEM] + [ANY] * count,
        out_specs=ANY,
        out_shape=jax.ShapeDtypeStruct(lead + (rows, cols), pieces[0].dtype),
        scratch_shapes=[
            pltpu.VMEM((count, 4, rows, cols), pieces[0].dtype),
            pltpu.SemaphoreType.DMA((2, count, 4)),
        ],
        compiler_params=params(),
        name="assemble",
    )(where, *pieces)
    return out.reshape(-1, cols)


def swap(value, axis):
    return lax.ppermute(value, axis, [(0, 1), (1, 0)])


def hop(value, offset):
    return lax.ppermute(value, "z", [(i, i ^ offset) for i in range(4)])


def gather_z_first(where, shard, first, second):
    stack = jnp.stack([shard] + [hop(shard, k) for k in (1, 2, 3)])
    near = swap(stack, first)
    ring = [((0, 0), stack), ((1, 0), near)]
    ring += [((0, 1), swap(stack, second)), ((1, 1), swap(near, second))]
    pieces, relative = [], []
    for (one, two), piece in ring:
        moved = {first: one, second: two}
        for dc, held in ((0, piece), (1, swap(piece, "c"))):
            pieces.append(held)
            relative.append((moved["y"], dc, moved["x"]))
    return assemble(where, pieces, relative, True)


def fence(*values):
    return lax.optimization_barrier(values)


class Reduction:
    def __init__(self, partial, order, names="zyx"):
        self.partial = partial
        self.order = order
        self.names = list(names)
        self.moved = None

    def send(self):
        axis, self.order = self.order[0], self.order[1:]
        dim = self.names.index(axis)
        self.names.pop(dim)
        here = lax.axis_index(axis)

        def block(slot):
            return lax.dynamic_index_in_dim(self.partial, slot, dim, keepdims=False)

        if axis == "z":
            self.moved = [hop(block(here ^ k), k) for k in (1, 2, 3)]
        else:
            self.moved = [swap(block(1 - here), axis)]
        self.partial = block(here)

    def add(self):
        total = self.partial.astype(F32)
        for part in self.moved:
            total = total + part.astype(F32)
        self.moved = None
        self.partial = total.astype(BF) if self.order else total


def send_all(reductions, *others):
    reductions = [r for r in reductions if r.order]
    held = fence(*[r.partial for r in reductions], *others)
    for reduction, partial in zip(reductions, held):
        reduction.partial = partial
        reduction.send()
    return held[len(reductions) :]


def add_all(reductions, *others):
    reductions = [r for r in reductions if r.moved is not None]
    flat = [part for r in reductions for part in r.moved]
    held = fence(*flat, *others)
    at = 0
    for reduction in reductions:
        count = len(reduction.moved)
        reduction.moved = list(held[at : at + count])
        at += count
        reduction.add()
    held = fence(*[r.partial for r in reductions], *held[at:])
    for reduction, partial in zip(reductions, held):
        reduction.partial = partial
    return held[len(reductions) :]


def turn(field, cosine, signed_sine):
    lane = lax.broadcasted_iota(jnp.int32, field.shape, 1)
    other = jnp.where(
        lane % 64 < 32, pltpu.roll(field, 96, axis=1), pltpu.roll(field, 32, axis=1)
    )
    return field * cosine + other * signed_sine


def project_qkv(normed, weights, cosine, signed_sine, first_value):
    rows, width = normed.shape
    devices = width // 128

    def kernel(normed_ref, w_q_ref, w_k_ref, w_v_ref, cos_ref, sin_ref, *rest):
        out_ref = rest[-1]
        step = pl.program_id(0)

        def product(w_ref):
            return jnp.dot(normed_ref[...], w_ref[...], preferred_element_type=F32)

        def turned(w_ref):
            field = product(w_ref)
            for n in range(devices):
                part = field[:, 128 * n : 128 * n + 128]
                out_ref[n, 0] = turn(part, cos_ref[...], sin_ref[...]).astype(BF)

        @pl.when(step == 0)
        def _():
            turned(w_q_ref)

        @pl.when(step == 1)
        def _():
            turned(w_k_ref)

        @pl.when(step == 2)
        def _():
            field = product(w_v_ref)
            for n in range(devices):
                part = field[:, 128 * n : 128 * n + 128]
                if first_value is not None:
                    part = 0.5 * part + 0.5 * rest[0][n, 0].astype(F32)
                out_ref[n, 0] = part.astype(BF)

    whole = lambda step: (0, 0)
    in_specs = [pl.BlockSpec((rows, width), whole)]
    for _, start in weights:
        in_specs.append(pl.BlockSpec((width, width), lambda step, start=start: (0, start)))
    in_specs += [pl.BlockSpec((rows, 128), whole)] * 2
    operands = [normed] + [array for array, _ in weights] + [cosine, signed_sine]
    if first_value is not None:
        in_specs.append(pl.BlockSpec((devices, 1, rows, 128), lambda step: (0, 2, 0, 0)))
        operands.append(first_value)
    return pl.pallas_call(
        kernel,
        grid=(3,),
        in_specs=in_specs,
        out_specs=pl.BlockSpec((devices, 1, rows, 128), lambda step: (0, step, 0, 0)),
        out_shape=jax.ShapeDtypeStruct((devices, 3, rows, 128), BF),
        compiler_params=params(dimension_semantics=("arbitrary",)),
        name="project_qkv",
    )(*operands)


def weight_grads(core, groups, chunks):
    rows = groups[0][0][0].shape[0]
    operands, scratch, plans = [], [], []
    widths, count = {}, 0
    for (left, rights), places in zip(groups, chunks):
        size = left[0].shape[1] // 4
        window = -(-size // 128) * 128
        plan = {"size": size, "window": window, "left": len(operands), "held": len(scratch)}
        operands += list(left)
        scratch.append(pltpu.VMEM((2, 2 * rows, window), BF))
        plan["rights"] = []
        for right, parts in zip(rights, places):
            cols = right[0].shape[1]
            plan["rights"].append((len(operands), len(scratch), parts))
            operands += list(right)
            scratch.append(pltpu.VMEM((2 * rows, cols), BF))
            for _, span, result, at in parts:
                count += 1
                spread = span if size == window else 3 * span
                widths[result] = max(widths.get(result, 0), at + spread)
        plans.append(plan)
    shapes = [(4, 2, 64, widths[n]) for n in range(len(widths))]
    first_stage = len(scratch)
    scratch += [pltpu.VMEM(shape, BF) for shape in shapes]
    scratch += [
        pltpu.SemaphoreType.DMA((len(operands), 2)),
        pltpu.SemaphoreType.DMA((count,)),
    ]
    inputs, results = len(operands), len(shapes)

    def put_thirds(stage, part, total, at, span, size):
        for z in range(4):
            for x in range(2):
                low = z * (size // 4) + x * (size // 8)
                for third in range(3):
                    first, last = low + 32 * third, low + min(32 * third + 32, size // 8)
                    piece = total[first:last]
                    missing = 32 - piece.shape[0]
                    if missing:
                        piece = jnp.concatenate([piece, jnp.zeros((missing, span), F32)])
                    lane = at + third * span
                    stage[z, part, 32 * x : 32 * x + 32, lane : lane + span] = piece.astype(BF)

    def kernel(core_ref, *refs):
        ins, outs, work = refs[:inputs], refs[inputs : inputs + results], refs[inputs + results :]
        stages = work[first_stage : first_stage + results]
        in_sems, out_sems = work[-2:]
        loads = []
        for plan in plans:
            held, size, window = work[plan["held"]], plan["size"], plan["window"]
            slack = window - size
            left = []
            for side in range(2):
                for part in range(2):
                    start = 2 * part * size + core_ref[0] * (size - slack)
                    span = pl.ds(pl.multiple_of(start, 128), window)
                    at = plan["left"] + side
                    left.append(
                        pltpu.make_async_copy(
                            ins[at].at[:, span],
                            held.at[part, pl.ds(side * rows, rows)],
                            in_sems.at[at, part],
                        )
                    )
            rights = []
            for at, spot, _ in plan["rights"]:
                rights.append(
                    [
                        pltpu.make_async_copy(
                            ins[at + side],
                            work[spot].at[pl.ds(side * rows, rows)],
                            in_sems.at[at + side, 0],
                        )
                        for side in range(2)
                    ]
                )
            loads.append((left, rights))
            for copy in left + [copy for pair in rights for copy in pair]:
                copy.start()
        puts = []
        for plan, (left, rights) in zip(plans, loads):
            size, window = plan["size"], plan["window"]
            held = work[plan["held"]]
            for copy in left:
                copy.wait()
            for pair, (_, spot, parts) in zip(rights, plan["rights"]):
                for copy in pair:
                    copy.wait()
                for first, span, result, at in parts:
                    right = work[spot][:, first : first + span]
                    stage = stages[result]
                    wide = span if size == window else 3 * span
                    for part in range(2):
                        total = lax.dot_general(
                            held[part], right, TN, preferred_element_type=F32
                        )
                        if size == window:
                            total = total.astype(BF).reshape(4, size // 4, span)
                            stage[:, part, :, at : at + span] = total
                        else:
                            own = jnp.where(core_ref[0] == 0, total[:size], total[window - size :])
                            put_thirds(stage, part, own, at, span, size)
                    lanes = pl.ds(at, wide)
                    put = pltpu.make_async_copy(
                        stage.at[:, :, :, lanes],
                        outs[result].at[:, :, :, lanes],
                        out_sems.at[len(puts)],
                    )
                    put.start()
                    puts.append(put)
        for put in puts:
            put.wait()

    return pl.pallas_call(
        kernel,
        in_specs=[SMEM] + [ANY] * inputs,
        out_specs=[ANY] * results,
        out_shape=[jax.ShapeDtypeStruct(shape, BF) for shape in shapes],
        scratch_shapes=scratch,
        compiler_params=params(),
        name="weight_grads",
    )(core, *operands)


def rows_of(block):
    return block.reshape(-1, 128)


def attend(length, pieces):
    tile = 256
    slots = pieces.shape[2] * 128
    tiles = slots // tile
    per = tile // 128

    def kernel(len_ref, piece_ref, out_ref, lse_ref, held, flipped, logit, sems):
        step = pl.program_id(0)

        @pl.when(step == 0)
        def _():
            copies = [
                pltpu.make_async_copy(
                    piece_ref.at[device], held.at[:, :, device], sems.at[device]
                )
                for device in range(8)
            ]
            for copy in copies:
                copy.start()
            for copy in copies:
                copy.wait()

        @pl.when(step == 0)
        def _():
            for block in range(tiles):
                key = rows_of(held[1, pl.ds(per * block, per)])
                flipped[block] = key.T

        used = len_ref[0]
        query = rows_of(held[0, pl.ds(per * step, per)]) * BF(0.125)
        lane = lax.broadcasted_iota(jnp.int32, (tile, 128), 1)
        low = lane < 64
        zero = jnp.zeros_like(query)
        queries = [jnp.where(low, query, zero), jnp.where(low, zero, query)]

        def score(block, tops, masked):
            key_t = flipped[block]
            result = []
            for head in range(2):
                field = jnp.dot(queries[head], key_t, preferred_element_type=F32)
                if masked:
                    query_pos = step * tile + lax.broadcasted_iota(jnp.int32, field.shape, 0)
                    key_pos = block * tile + lax.broadcasted_iota(jnp.int32, field.shape, 1)
                    seen = (key_pos <= query_pos) & (key_pos < used)
                    field = jnp.where(seen, field, NEGATIVE)
                logit[head, block] = field
                top = jnp.maximum(field[:, :128], field[:, 128:])
                result.append(jnp.maximum(tops[head], top))
            return tuple(result)

        full = jnp.minimum(step, used // tile)
        end = jnp.minimum(step + 1, (used + tile - 1) // tile)
        low_top = jnp.full((tile, 128), NEGATIVE, F32)
        tops = lax.fori_loop(0, full, lambda b, s: score(b, s, False), (low_top, low_top))
        tops = lax.fori_loop(full, end, lambda b, s: score(b, s, True), tops)
        tops = [jnp.max(top, axis=1, keepdims=True) for top in tops]
        wide = [jnp.broadcast_to(top, (tile, tile)) for top in tops]
        one = jnp.ones_like(query)

        def mix(block, sums):
            value = rows_of(held[2, pl.ds(per * block, per)])
            values = [jnp.where(low, value, one), jnp.where(low, one, value)]
            result = []
            for head in range(2):
                probs = jnp.exp(logit[head, block] - wide[head]).astype(BF)
                result.append(
                    sums[head] + jnp.dot(probs, values[head], preferred_element_type=F32)
                )
            return tuple(result)

        nothing = jnp.zeros((tile, 128), F32)
        sums = lax.fori_loop(0, end, mix, (nothing, nothing))
        totals = [sums[0][:, 64:65], sums[1][:, 0:1]]
        out = jnp.where(low, sums[0] / totals[0], sums[1] / totals[1])
        out = out.astype(BF).reshape(per, 8, 16, 128)
        for device in range(8):
            out_ref[device, pl.ds(per * step, per)] = out[:, device]
        level = jnp.where(low, tops[0] + jnp.log(totals[0]), tops[1] + jnp.log(totals[1])).T
        start = pl.multiple_of(step * tile, tile)
        lse_ref[0:1, pl.ds(start, tile)] = level[0:1]
        lse_ref[1:2, pl.ds(start, tile)] = level[64:65]

    return pl.pallas_call(
        kernel,
        grid=(tiles,),
        in_specs=[SMEM, ANY],
        out_specs=[
            pl.BlockSpec((8,) + pieces.shape[2:], lambda i: (0, 0, 0, 0)),
            pl.BlockSpec((8, slots), lambda i: (0, 0)),
        ],
        out_shape=[
            jax.ShapeDtypeStruct((8,) + pieces.shape[2:], BF),
            jax.ShapeDtypeStruct((8, slots), F32),
        ],
        scratch_shapes=[
            pltpu.VMEM((3, slots // 128, 8, 16, 128), BF),
            pltpu.VMEM((tiles, 128, tile), BF),
            pltpu.VMEM((2, tiles, tile, tile), F32),
            pltpu.SemaphoreType.DMA((8,)),
        ],
        compiler_params=params(dimension_semantics=("arbitrary",)),
        name="attend",
    )(length, pieces)


def attend_back(length, pieces, attended, grads, lse, cosine, signed_sine, passed):
    tile = 256
    slots = pieces.shape[2] * 128
    tiles = slots // tile
    per = tile // 128
    upper = passed is None

    def kernel(*refs):
        len_ref, piece_ref, att_ref, grad_ref, lse_ref, cos_ref, sin_ref = refs[:7]
        refs = refs[7:]
        if upper:
            passed_ref = None
            out_ref, give_ref = refs[:2]
            refs = refs[2:]
        else:
            passed_ref, out_ref = refs[:2]
            give_ref = None
            refs = refs[2:]
        held, att, grad, delta, level, query_acc, key_acc, value_acc, sems = refs
        step = pl.program_id(0)
        used = len_ref[0]

        @pl.when(step == 0)
        def _():
            copies = []
            for device in range(8):
                for n, (source, target) in enumerate(
                    (
                        (grad_ref.at[device], grad.at[:, device]),
                        (att_ref.at[device], att.at[:, device]),
                        (piece_ref.at[device], held.at[:, :, device]),
                    )
                ):
                    copies.append(pltpu.make_async_copy(source, target, sems.at[n, device]))
            for copy in copies:
                copy.start()
            for copy in copies:
                copy.wait()

        @pl.when(step == 0)
        def _():
            query_acc[...] = jnp.zeros_like(query_acc)
            line = lax.broadcasted_iota(jnp.int32, (8, 128), 0)
            lane = lax.broadcasted_iota(jnp.int32, (8, 128), 1)
            pick = jnp.where(line == lane // 64, 1.0, 0.0).astype(F32)
            for block in range(tiles):
                span = slice(tile * block, tile * block + tile)
                product = rows_of(grad[pl.ds(per * block, per)]).astype(F32) * rows_of(
                    att[pl.ds(per * block, per)]
                ).astype(F32)
                delta[:, span] = lax.dot_general(
                    pick, product, NT, precision=PRECISE, preferred_element_type=F32
                )
            place = lax.broadcasted_iota(jnp.int32, (8, slots), 1)
            level[...] = jnp.where(place < used, lse_ref[...], -NEGATIVE)

        key = rows_of(held[1, pl.ds(per * step, per)])
        value = rows_of(held[2, pl.ds(per * step, per)])
        lane = lax.broadcasted_iota(jnp.int32, (tile, 128), 1)
        low = lane < 64

        def head_part(field, head):
            keep = low if head == 0 else jnp.logical_not(low)
            return jnp.where(keep, field, jnp.zeros_like(field))

        scaled = key * BF(0.125)
        keys = [head_part(scaled, head) for head in range(2)]
        values = [head_part(value, head) for head in range(2)]
        key_acc[...] = jnp.zeros_like(key_acc)
        value_acc[...] = jnp.zeros_like(value_acc)

        def visit(block, masked):
            query = rows_of(held[0, pl.ds(per * block, per)])
            grad_out = rows_of(grad[pl.ds(per * block, per)])
            start = pl.multiple_of(block * tile, tile)
            spans = pl.ds(start, tile)
            query_sum = jnp.zeros((tile, 128), F32)
            key_sum = jnp.zeros((tile, 128), F32)
            value_sum = jnp.zeros((tile, 128), F32)
            for head in range(2):
                logits = lax.dot_general(keys[head], query, NT, preferred_element_type=F32)
                probs = jnp.exp(logits - level[head : head + 1, spans])
                if masked:
                    key_pos = lax.broadcasted_iota(jnp.int32, probs.shape, 0)
                    query_pos = lax.broadcasted_iota(jnp.int32, probs.shape, 1)
                    probs = jnp.where(key_pos <= query_pos, probs, 0.0)
                grad_probs = lax.dot_general(
                    values[head], grad_out, NT, preferred_element_type=F32
                )
                grad_logits = (probs * (grad_probs - delta[head : head + 1, spans])).astype(BF)
                value_sum += jnp.dot(
                    probs.astype(BF), head_part(grad_out, head), preferred_element_type=F32
                )
                key_sum += jnp.dot(
                    grad_logits, head_part(query, head), preferred_element_type=F32
                )
                query_sum += lax.dot_general(
                    grad_logits, keys[head], TN, preferred_element_type=F32
                )
            query_acc[spans, :] += query_sum
            key_acc[...] += key_sum
            value_acc[...] += value_sum

        end = (used + tile - 1) // tile

        @pl.when(step < end)
        def _():
            visit(step, True)

            def body(block, carry):
                visit(block, False)
                return carry

            lax.fori_loop(step + 1, end, body, 0)

        def put(member, block, field):
            field = field.astype(BF).reshape(per, 8, 16, 128)
            for device in range(8):
                out_ref[device, member, pl.ds(per * block, per)] = field[:, device]

        start = pl.multiple_of(step * tile, tile)
        spans = pl.ds(start, tile)
        key_grad = key_acc[...] * 0.125
        put(1, step, turn(key_grad, cos_ref[spans, :], -sin_ref[spans, :]))
        if upper:
            half = 0.5 * value_acc[...]
            give_ref[spans, :] = half
            put(2, step, half)
        else:
            put(2, step, value_acc[...] + passed_ref[spans, :])

        @pl.when(step == tiles - 1)
        def _():
            for block in range(tiles):
                part = slice(tile * block, tile * block + tile)
                put(0, block, turn(query_acc[part, :], cos_ref[part, :], -sin_ref[part, :]))

    flat = lambda i: (0, 0)
    table = pl.BlockSpec((slots, 128), flat)
    in_specs = [SMEM, ANY, ANY, ANY, pl.BlockSpec((8, slots), flat), table, table]
    operands = [length, pieces, attended, grads, lse, cosine, signed_sine]
    out_specs = [pl.BlockSpec(pieces.shape, lambda i: (0, 0, 0, 0, 0))]
    out_shape = [jax.ShapeDtypeStruct(pieces.shape, BF)]
    if upper:
        out_specs.append(table)
        out_shape.append(jax.ShapeDtypeStruct((slots, 128), F32))
    else:
        in_specs.append(table)
        operands.append(passed)
    outs = pl.pallas_call(
        kernel,
        grid=(tiles,),
        in_specs=in_specs,
        out_specs=out_specs,
        out_shape=out_shape,
        scratch_shapes=[
            pltpu.VMEM((3, slots // 128, 8, 16, 128), BF),
            pltpu.VMEM((slots // 128, 8, 16, 128), BF),
            pltpu.VMEM((slots // 128, 8, 16, 128), BF),
            pltpu.VMEM((8, slots), F32),
            pltpu.VMEM((8, slots), F32),
            pltpu.VMEM((slots, 128), F32),
            pltpu.VMEM((tile, 128), F32),
            pltpu.VMEM((tile, 128), F32),
            pltpu.SemaphoreType.DMA((3, 8)),
        ],
        compiler_params=params(dimension_semantics=("arbitrary",)),
        name="attend_back",
    )(*operands)
    return outs if upper else (outs[0], None)


def block_spans(total_rows):
    return [(offset, min(512, total_rows - offset)) for offset in range(0, total_rows, 512)]


def rotate(field, cosine, sine_table):
    half_dim = field.shape[-1] // 2
    first_half = field[..., :half_dim]
    second_half = field[..., half_dim:]
    return jnp.concatenate(
        [
            first_half * cosine - second_half * sine_table,
            second_half * cosine + first_half * sine_table,
        ],
        axis=-1,
    )


def allowed(query_pos, key_pos, lengths):
    causal = key_pos[None, None, :] <= query_pos[None, :, None]
    inside = key_pos[None, None, :] < lengths[:, None, None]
    return (causal & inside)[:, None, :, :]


def attend_gathered(q_heads, k_flat, v_flat, lengths, positions, score_scale):
    seq_count, stretch_len, head_count, head_dim = q_heads.shape
    first_row = jnp.int32(0)
    k_piece = lax.all_gather(k_flat, "seq", axis=1, tiled=True)
    v_piece = lax.all_gather(v_flat, "seq", axis=1, tiled=True)
    running_max = jnp.full((seq_count, head_count, stretch_len), NEGATIVE, jnp.float32)
    row_total = jnp.zeros((seq_count, head_count, stretch_len), jnp.float32)
    weighted = jnp.zeros((seq_count, stretch_len, head_count, head_dim), jnp.float32)
    for offset, block_len in block_spans(k_piece.shape[1]):
        k_block = k_piece[:, offset : offset + block_len].reshape(
            seq_count, block_len, head_count, head_dim
        )
        v_block = (
            v_piece[:, offset : offset + block_len]
            .reshape(seq_count, block_len, head_count, head_dim)
            .astype(jnp.float32)
        )
        key_pos = first_row + offset + jnp.arange(block_len, dtype=jnp.int32)
        allowed_mask = allowed(positions, key_pos, lengths)
        logits = (
            jnp.einsum("sqhd,skhd->shqk", q_heads, k_block, preferred_element_type=jnp.float32)
            * score_scale
        )
        new_max = jnp.maximum(
            running_max, jnp.max(jnp.where(allowed_mask, logits, NEGATIVE), axis=-1)
        )
        probs = jnp.where(allowed_mask, jnp.exp(logits - new_max[..., None]), 0.0)
        rescale = jnp.exp(running_max - new_max)
        row_total = row_total * rescale + jnp.sum(probs, axis=-1)
        weighted = weighted * jnp.transpose(rescale, (0, 2, 1))[..., None] + jnp.einsum(
            "shqk,skhd->sqhd", probs, v_block, precision=PRECISE, preferred_element_type=jnp.float32
        )
        running_max = new_max
    running_max, row_total, weighted = (running_max, row_total, weighted)
    attended = weighted / jnp.transpose(row_total, (0, 2, 1))[..., None]
    return (attended, running_max + jnp.log(row_total))


def attend_back_gathered(
    q_heads,
    k_heads,
    v_heads,
    q_flat,
    k_flat,
    v_flat,
    grad_heads,
    grad_flat,
    log_total,
    delta_rows,
    lengths,
    positions,
    score_scale,
):
    seq_count, stretch_len, head_count, head_dim = q_heads.shape
    zeros_heads = jnp.zeros((seq_count, stretch_len, head_count, head_dim), jnp.float32)
    carry = zeros_heads
    first_row = jnp.int32(0)
    k_piece = lax.all_gather(k_flat, "seq", axis=1, tiled=True)
    v_piece = lax.all_gather(v_flat, "seq", axis=1, tiled=True)
    for offset, block_len in block_spans(k_piece.shape[1]):
        k_block = k_piece[:, offset : offset + block_len].reshape(
            seq_count, block_len, head_count, head_dim
        )
        v_block = v_piece[:, offset : offset + block_len].reshape(
            seq_count, block_len, head_count, head_dim
        )
        key_pos = first_row + offset + jnp.arange(block_len, dtype=jnp.int32)
        allowed_mask = allowed(positions, key_pos, lengths)
        logits = (
            jnp.einsum("sqhd,skhd->shqk", q_heads, k_block, preferred_element_type=jnp.float32)
            * score_scale
        )
        probs = jnp.where(allowed_mask, jnp.exp(logits - log_total[..., None]), 0.0)
        grad_probs = jnp.einsum(
            "sqhd,skhd->shqk", grad_heads, v_block, preferred_element_type=jnp.float32
        )
        grad_logits = (probs * (grad_probs - delta_rows[..., None])).astype(jnp.bfloat16)
        carry = (
            carry
            + jnp.einsum(
                "shqk,skhd->sqhd", grad_logits, k_block, preferred_element_type=jnp.float32
            )
            * score_scale
        )
    gathered_stats = (
        lax.all_gather(log_total, "seq", axis=2, tiled=True),
        lax.all_gather(delta_rows, "seq", axis=2, tiled=True),
    )
    first_row = jnp.int32(0)
    q_piece = lax.all_gather(q_flat, "seq", axis=1, tiled=True)
    g_piece = lax.all_gather(grad_flat, "seq", axis=1, tiled=True)
    grad_key = zeros_heads
    grad_value = zeros_heads
    for offset, block_len in block_spans(q_piece.shape[1]):
        q_block = q_piece[:, offset : offset + block_len].reshape(
            seq_count, block_len, head_count, head_dim
        )
        g_block = g_piece[:, offset : offset + block_len].reshape(
            seq_count, block_len, head_count, head_dim
        )
        query_pos = first_row + offset + jnp.arange(block_len, dtype=jnp.int32)
        allowed_mask = allowed(query_pos, positions, lengths)
        lse_block = lax.dynamic_slice_in_dim(gathered_stats[0], offset, block_len, 2)
        delta_block = lax.dynamic_slice_in_dim(gathered_stats[1], offset, block_len, 2)
        logits = (
            jnp.einsum("sqhd,skhd->shqk", q_block, k_heads, preferred_element_type=jnp.float32)
            * score_scale
        )
        probs = jnp.where(allowed_mask, jnp.exp(logits - lse_block[..., None]), 0.0)
        grad_value = grad_value + jnp.einsum(
            "shqk,sqhd->skhd",
            probs,
            g_block.astype(jnp.float32),
            precision=PRECISE,
            preferred_element_type=jnp.float32,
        )
        grad_probs = jnp.einsum(
            "sqhd,skhd->shqk", g_block, v_heads, preferred_element_type=jnp.float32
        )
        grad_logits = (probs * (grad_probs - delta_block[..., None])).astype(jnp.bfloat16)
        grad_key = (
            grad_key
            + jnp.einsum(
                "shqk,sqhd->skhd", grad_logits, q_block, preferred_element_type=jnp.float32
            )
            * score_scale
        )
    grad_key, grad_value = (grad_key, grad_value)
    return (carry, grad_key, grad_value)


def body(tokens, seq_lens, norm_attn, w_qkv, w_out, norm_ffn, w_gate, w_up, w_down, cotangent):
    seq_count, stretch_len, model_width = tokens.shape
    head_count = HEADS
    head_dim = model_width // head_count
    score_scale = head_dim ** (-0.5)
    lengths = seq_lens[0]
    positions = lax.axis_index("seq") * stretch_len + jnp.arange(stretch_len, dtype=jnp.int32)
    half_dim = head_dim // 2
    freqs = 10000.0 ** (-jnp.arange(half_dim, dtype=jnp.float32) / half_dim)
    angle = positions.astype(jnp.float32)[:, None] * freqs[None, :]
    cosine = jnp.cos(angle)[:, None, :]
    sine_table = jnp.sin(angle)[:, None, :]

    def heads_of(field):
        return field.reshape(seq_count, stretch_len, head_count, head_dim)

    def gather_layer(layer_index):
        return (
            lax.all_gather(norm_attn[layer_index], ("grp", "seq"), axis=0, tiled=True),
            lax.all_gather(w_qkv[layer_index], ("grp", "seq"), axis=0, tiled=True),
            lax.all_gather(w_out[layer_index], ("grp", "seq"), axis=0, tiled=True),
            lax.all_gather(norm_ffn[layer_index], ("grp", "seq"), axis=0, tiled=True),
            lax.all_gather(w_gate[layer_index], ("grp", "seq"), axis=0, tiled=True),
            lax.all_gather(w_up[layer_index], ("grp", "seq"), axis=0, tiled=True),
            lax.all_gather(w_down[layer_index], ("grp", "seq"), axis=0, tiled=True),
        )

    def gather_again(layer_index):
        return (
            lax.all_gather(norm_attn[layer_index], ("grp", "seq"), axis=0, tiled=True),
            lax.all_gather(w_qkv[layer_index], ("grp", "seq"), axis=0, tiled=True),
            lax.all_gather(w_out[layer_index], ("grp", "seq"), axis=0, tiled=True),
            lax.all_gather(norm_ffn[layer_index], ("grp", "seq"), axis=0, tiled=True),
            lax.all_gather(w_gate[layer_index], ("grp", "seq"), axis=0, tiled=True),
            lax.all_gather(w_up[layer_index], ("grp", "seq"), axis=0, tiled=True),
            lax.all_gather(w_down[layer_index], ("grp", "seq"), axis=0, tiled=True),
        )

    def forward_layer(inputs, params, first_value):
        gain_one, mat_qkv, mat_out, gain_two, mat_gate, mat_up, mat_down = params
        rms_one = lax.rsqrt(jnp.mean(inputs * inputs, axis=-1, keepdims=True) + EPSILON)
        normed = (inputs * rms_one * gain_one.astype(jnp.float32)).astype(jnp.bfloat16)
        projected = jnp.dot(normed, mat_qkv, preferred_element_type=jnp.float32)
        query_raw = projected[:, :model_width]
        key_raw = projected[:, model_width : 2 * model_width]
        value_raw = projected[:, 2 * model_width :]
        if first_value is None:
            values = value_raw.astype(jnp.bfloat16)
        else:
            values = (0.5 * value_raw + 0.5 * first_value.astype(jnp.float32)).astype(jnp.bfloat16)
        query_rot = rotate(heads_of(query_raw), cosine, sine_table).astype(jnp.bfloat16)
        key_rot = rotate(heads_of(key_raw), cosine, sine_table).astype(jnp.bfloat16)
        attended, log_total = attend_gathered(
            query_rot,
            key_rot.reshape(seq_count, stretch_len, model_width),
            values.reshape(seq_count, stretch_len, model_width),
            lengths,
            positions,
            score_scale,
        )
        attn_low = attended.reshape(-1, model_width).astype(jnp.bfloat16)
        middle = inputs + jnp.dot(attn_low, mat_out, preferred_element_type=jnp.float32)
        rms_two = lax.rsqrt(jnp.mean(middle * middle, axis=-1, keepdims=True) + EPSILON)
        normed_two = (middle * rms_two * gain_two.astype(jnp.float32)).astype(jnp.bfloat16)
        gate_pre = jnp.dot(normed_two, mat_gate, preferred_element_type=jnp.float32)
        up_pre = jnp.dot(normed_two, mat_up, preferred_element_type=jnp.float32)
        hidden = (jax.nn.silu(gate_pre) * up_pre).astype(jnp.bfloat16)
        result = middle + jnp.dot(hidden, mat_down, preferred_element_type=jnp.float32)
        kept = (
            inputs,
            rms_one,
            normed,
            query_rot,
            key_rot,
            values,
            attended,
            attn_low,
            log_total,
            middle,
            rms_two,
            normed_two,
            gate_pre,
            up_pre,
            hidden,
        )
        return (result, values, kept)

    def backward_layer(grad_in, params, kept, first_grad):
        gain_one, mat_qkv, mat_out, gain_two, mat_gate, mat_up, mat_down = params
        (
            inputs,
            rms_one,
            normed,
            query_rot,
            key_rot,
            values,
            attended,
            attn_low,
            log_total,
            middle,
            rms_two,
            normed_two,
            gate_pre,
            up_pre,
            hidden,
        ) = kept
        grad_low = grad_in.astype(jnp.bfloat16)
        grad_down = jnp.einsum("nf,nd->fd", hidden, grad_low, preferred_element_type=jnp.float32)
        grad_hidden = jnp.einsum(
            "nd,fd->nf", grad_low, mat_down, preferred_element_type=jnp.float32
        )
        sigma = jax.nn.sigmoid(gate_pre)
        grad_gate_pre = (grad_hidden * up_pre * sigma * (1.0 + gate_pre * (1.0 - sigma))).astype(
            jnp.bfloat16
        )
        grad_up_pre = (grad_hidden * gate_pre * sigma).astype(jnp.bfloat16)
        grad_gate = jnp.einsum(
            "nd,nf->df", normed_two, grad_gate_pre, preferred_element_type=jnp.float32
        )
        grad_up = jnp.einsum(
            "nd,nf->df", normed_two, grad_up_pre, preferred_element_type=jnp.float32
        )
        grad_normed_two = jnp.einsum(
            "nf,df->nd", grad_gate_pre, mat_gate, preferred_element_type=jnp.float32
        ) + jnp.einsum("nf,df->nd", grad_up_pre, mat_up, preferred_element_type=jnp.float32)
        scaled_two = middle * rms_two
        grad_gain_two = jnp.sum(grad_normed_two * scaled_two, axis=0)
        weighted_two = grad_normed_two * gain_two.astype(jnp.float32)
        grad_middle = grad_in + rms_two * (
            weighted_two - scaled_two * jnp.mean(weighted_two * scaled_two, axis=-1, keepdims=True)
        )
        grad_attn = grad_middle.astype(jnp.bfloat16)
        grad_out_mat = jnp.einsum(
            "nd,ne->de", attn_low, grad_attn, preferred_element_type=jnp.float32
        )
        grad_attended = jnp.einsum(
            "ne,de->nd", grad_attn, mat_out, preferred_element_type=jnp.float32
        ).astype(jnp.bfloat16)
        grad_heads = heads_of(grad_attended)
        delta_rows = jnp.transpose(
            jnp.sum(grad_heads.astype(jnp.float32) * attended, axis=-1), (0, 2, 1)
        )
        grad_query, grad_key, grad_value = attend_back_gathered(
            query_rot,
            key_rot,
            heads_of(values),
            query_rot.reshape(seq_count, stretch_len, model_width),
            key_rot.reshape(seq_count, stretch_len, model_width),
            values.reshape(seq_count, stretch_len, model_width),
            grad_heads,
            grad_attended.reshape(seq_count, stretch_len, model_width),
            log_total,
            delta_rows,
            lengths,
            positions,
            score_scale,
        )
        grad_query_raw = rotate(grad_query, cosine, -sine_table).reshape(-1, model_width)
        grad_key_raw = rotate(grad_key, cosine, -sine_table).reshape(-1, model_width)
        grad_value_flat = grad_value.reshape(-1, model_width)
        if first_grad is None:
            grad_value_raw = 0.5 * grad_value_flat
            passed = 0.5 * grad_value_flat
        else:
            grad_value_raw = grad_value_flat + first_grad
            passed = None
        grad_proj = jnp.concatenate([grad_query_raw, grad_key_raw, grad_value_raw], axis=-1).astype(
            jnp.bfloat16
        )
        grad_qkv = jnp.einsum("nd,ne->de", normed, grad_proj, preferred_element_type=jnp.float32)
        grad_normed = jnp.einsum(
            "ne,de->nd", grad_proj, mat_qkv, preferred_element_type=jnp.float32
        )
        scaled_one = inputs * rms_one
        grad_gain_one = jnp.sum(grad_normed * scaled_one, axis=0)
        weighted_one = grad_normed * gain_one.astype(jnp.float32)
        grad_inputs = grad_middle + rms_one * (
            weighted_one - scaled_one * jnp.mean(weighted_one * scaled_one, axis=-1, keepdims=True)
        )
        return (
            grad_inputs,
            (grad_gain_one, grad_qkv, grad_out_mat, grad_gain_two, grad_gate, grad_up, grad_down),
            passed,
        )

    def reduce_layer(grads):
        return (
            lax.psum_scatter(grads[0], ("grp", "seq"), scatter_dimension=0, tiled=True),
            lax.psum_scatter(grads[1], ("grp", "seq"), scatter_dimension=0, tiled=True),
            lax.psum_scatter(grads[2], ("grp", "seq"), scatter_dimension=0, tiled=True),
            lax.psum_scatter(grads[3], ("grp", "seq"), scatter_dimension=0, tiled=True),
            lax.psum_scatter(grads[4], ("grp", "seq"), scatter_dimension=0, tiled=True),
            lax.psum_scatter(grads[5], ("grp", "seq"), scatter_dimension=0, tiled=True),
            lax.psum_scatter(grads[6], ("grp", "seq"), scatter_dimension=0, tiled=True),
        )

    state_zero = tokens.astype(jnp.float32).reshape(-1, model_width)
    params_one = gather_layer(0)
    state_one, first_value, kept_one = forward_layer(state_zero, params_one, None)
    params_two = gather_layer(1)
    state_two, unused_value, kept_two = forward_layer(state_one, params_two, first_value)
    layer_out = state_two.astype(jnp.bfloat16).reshape(seq_count, stretch_len, model_width)
    valid_mask = (positions[None, :] < lengths[:, None]).astype(jnp.float32)
    grad_state = (cotangent.astype(jnp.float32) * valid_mask[:, :, None]).reshape(-1, model_width)
    params_two = gather_again(1)
    grad_mid, grads_two, passed = backward_layer(grad_state, params_two, kept_two, None)
    shards_two = reduce_layer(grads_two)
    params_one = gather_again(0)
    grad_inputs, grads_one, unused_grad = backward_layer(grad_mid, params_one, kept_one, passed)
    shards_one = reduce_layer(grads_one)
    stacked = tuple((jnp.stack([shards_one[member], shards_two[member]]) for member in range(7)))
    input_grad = grad_inputs.reshape(seq_count, stretch_len, model_width)
    return (
        layer_out,
        input_grad,
        stacked[0],
        stacked[1],
        stacked[2],
        stacked[3],
        stacked[4],
        stacked[5],
        stacked[6],
    )


def body_planes(
    tokens, seq_lens, norm_attn, w_qkv, w_out, norm_ffn, w_gate, w_up, w_down, cotangent
):
    seqs, stretch, width = tokens.shape
    y, c, z, x = (lax.axis_index(axis) for axis in ALL)
    lane = c * 4 + y * 2 + x
    where = jnp.stack([y, c, z, x]).astype(jnp.int32)
    rows = seqs * stretch
    ffn = w_gate.shape[2]

    def exchange(field):
        return lax.all_to_all(field, PLANE, 0, 0, tiled=True)

    def exchange_z(field):
        shape = field.shape
        moved = lax.all_to_all(field.reshape((4, 2) + shape[1:]), "z", 0, 0, tiled=True)
        return moved.reshape(shape)

    def cut_blocks(field):
        field = field.reshape(seqs, 2, 8, 16, width)
        return jnp.transpose(field, (2, 0, 1, 3, 4))

    def join_stripes(field):
        return jnp.transpose(field, (1, 0, 2, 3, 4)).reshape(rows, width)

    def cut_stripes(field):
        return jnp.transpose(field.reshape(seqs, 8, 2, 16, width), (1, 0, 2, 3, 4))

    def join_blocks(field):
        return jnp.transpose(field, (1, 2, 0, 3, 4)).reshape(seqs, stretch, width)

    def gather_all(shard):
        return lax.all_gather(shard, ALL, axis=0, tiled=True)

    def gain_shard(layer):
        gain = jnp.stack([norm_attn[layer], norm_ffn[layer]], axis=1)
        return jnp.pad(gain, ((0, 0), (0, 126)))

    def gains(columns):
        return jnp.transpose(columns)[:2].astype(F32)

    def gather_ffn(layer, *after):
        cuts = [w_gate[layer], w_up[layer], pack(w_down[layer])]
        if layer == 0:
            cuts.append(w_out[layer])
        shard = jnp.concatenate(cuts, axis=1)
        if after:
            shard, *_ = fence(shard, *after)
        gathered = gather_all(shard)
        packed = gathered[:, 2 * ffn : 2 * ffn + 3 * width]
        w_d = unpack(packed.reshape(32, -1, 3 * width)).reshape(-1, width)
        return gathered, w_d

    def pack(rows_of_down):
        tall = w_qkv.shape[1]
        spare = 3 * tall - rows_of_down.shape[-2]
        lead = [(0, 0)] * (rows_of_down.ndim - 2)
        padded = jnp.pad(rows_of_down, lead + [(0, spare), (0, 0)])
        cuts = [padded[..., n * tall : n * tall + tall, :] for n in range(3)]
        return jnp.concatenate(cuts, axis=-1)

    def unpack(packed):
        cols = packed.shape[-1] // 3
        cuts = [packed[..., n * cols : n * cols + cols] for n in range(3)]
        return jnp.concatenate(cuts, axis=-2)[..., : w_down.shape[1], :]

    def gather_first():
        shard = w_qkv[0]
        first = jnp.concatenate([shard[:, :width], gain_shard(0)], axis=1)
        w_q = gather_z_first(where, first, "x", "y")
        w_k = gather_z_first(where, shard[:, width : 2 * width], "y", "x")
        w_v = gather_z_first(where, shard[:, 2 * width :], "x", "y")
        weights = [(w_q, 0), (w_k, 0), (w_v, 0)]
        return weights, [w_q[:, :width], w_k, w_v], gains(w_q[:, width:])

    def gather_second(*after):
        shard = jnp.concatenate([w_qkv[1], w_out[1], gain_shard(1)], axis=1)
        shard, *_ = fence(shard, *after)
        whole = gather_all(shard)
        weights = [(whole, 0), (whole, 1), (whole, 2)]
        turned = [whole[:, : 3 * width]]
        return weights, turned, whole[:, 3 * width : 4 * width], gains(whole[:, 4 * width :])

    here = z * 2 + x
    routes = []
    for k in range(8):
        route = []
        for sy in range(2):
            for sc in range(2):
                for sb in range(8):
                    to = sb ^ k
                    target = (((to >> 1) & 1) * 2 + (to >> 2)) * 4 + 2 * sc + sy
                    route.append(((sy * 2 + sc) * 8 + sb, target * 2 + (to & 1)))
        routes.append(route)
    lengths = lax.ppermute(seq_lens, ALL, routes[0])[0]
    length = [lengths[n : n + 1] for n in range(2)]
    slots = stretch * 8
    half_dim = width // HEADS // 2
    freqs = 10000.0 ** (-jnp.arange(half_dim, dtype=F32) / half_dim)
    angle = jnp.arange(slots, dtype=F32)[:, None] * freqs[None, :]
    cosine, sine = jnp.cos(angle), jnp.sin(angle)
    cosine = jnp.concatenate([cosine] * 4, axis=1)
    sine = jnp.concatenate([-sine, sine] * 2, axis=1)

    def mine(table):
        own = lax.dynamic_index_in_dim(
            table.reshape(slots // 128, 8, 16, 128), lane, 1, keepdims=False
        )
        return own.reshape(stretch, 128)

    my_cos, my_sin = mine(cosine), mine(sine)
    step = jnp.arange(stretch, dtype=jnp.int32)
    places = (step // 16) * 128 + lane * 16 + step % 16
    valid = (places[None, :] < lengths[:, None]).astype(F32).reshape(rows, 1)

    def halves(field):
        return field[:stretch], field[stretch:]

    def forward_attention(inputs, weights, gain, first_value, *after):
        rms_one = lax.rsqrt(jnp.mean(inputs * inputs, axis=-1, keepdims=True) + EPSILON)
        normed = (inputs * rms_one * gain[0]).astype(BF)
        top, bottom = halves(normed)
        parts_a = project_qkv(top, weights, my_cos, my_sin, first_value and first_value[0])
        parts_b = project_qkv(bottom, weights, my_cos, my_sin, first_value and first_value[1])
        shape = (8, 3, stretch // 16, 16, 128)
        pieces_a = exchange(parts_a)
        pieces_a, sent_b = fence(pieces_a, parts_b)
        pieces_a = pieces_a.reshape(shape)
        pieces_b = exchange(sent_b)
        attended_a, lse_a = attend(length[0], pieces_a)
        attended_a, pieces_b, *_ = fence(attended_a, pieces_b, *after)
        pieces_b = pieces_b.reshape(shape)
        low_a = exchange(attended_a.reshape(8, stretch, 128))
        attended_b, lse_b = attend(length[1], pieces_b)
        low_a, sent_b = fence(low_a, attended_b)
        low_b = exchange(sent_b.reshape(8, stretch, 128))
        attn_low = jnp.concatenate(
            [jnp.transpose(low, (1, 0, 2)).reshape(stretch, width) for low in (low_a, low_b)]
        )
        kept = (
            inputs, rms_one, normed, (pieces_a, pieces_b), (attended_a, attended_b), attn_low,
            (lse_a, lse_b),
        )
        return attn_low, (parts_a, parts_b), kept

    def forward_ffn(inputs, attn_low, w_o, w_ffn, gain):
        w_gu, w_d = w_ffn
        middle = inputs + jnp.dot(attn_low, w_o, preferred_element_type=F32)
        rms_two = lax.rsqrt(jnp.mean(middle * middle, axis=-1, keepdims=True) + EPSILON)
        normed_two = (middle * rms_two * gain[1]).astype(BF)
        gate = jnp.dot(normed_two, w_gu[:, :ffn], preferred_element_type=F32)
        up = jnp.dot(normed_two, w_gu[:, ffn : 2 * ffn], preferred_element_type=F32)
        hidden = (jax.nn.silu(gate) * up).astype(BF)
        result = middle + jnp.dot(hidden, w_d, preferred_element_type=F32)
        return result, (middle, rms_two, normed_two, gate, up, hidden)

    def near(field):
        return swap(field, "c")

    def norm_back(grad_normed, source, rms, gain):
        scaled = source * rms
        weighted = grad_normed * gain
        return rms * (weighted - scaled * jnp.mean(weighted * scaled, axis=-1, keepdims=True))

    def blocks_of(grad):
        return grad.reshape(4, 2, 2, 32, grad.shape[-1])

    def dots(grads, weights):
        total = None
        for grad, weight in zip(grads, weights):
            part = lax.dot_general(grad, weight, NT, preferred_element_type=F32)
            total = part if total is None else total + part
        return total

    def attn_grads(one, att, proj, mid, places):
        return weight_grads(core, [(one, [proj]), (att, [mid])], places)

    def sum_z(grad):
        flat = grad.reshape(4, 128, grad.shape[-1])
        flat = lax.psum_scatter(flat, "z", scatter_dimension=0, tiled=True)
        return flat.reshape(2, 2, 32, grad.shape[-1])

    def pair_sums(summed):
        half = summed.shape[-1] // 2
        return [
            Reduction(summed[..., :half], "xy", "yx"),
            Reduction(summed[..., half:], "yx", "yx"),
        ]

    def ffn_grads(two, gates, ups, hid, low):
        half = ffn // 2
        parts = [[(0, half, 0, 0), (half, half, 0, half)]]
        parts.append([(0, half, 0, ffn), (half, half, 0, ffn + half)])
        (grad,) = weight_grads(
            core, [(two, [gates, ups]), (hid, [low])], [parts, [[(0, width, 0, 2 * ffn)]]]
        )
        return grad

    def backward_layer(grad_in, w_attn, w_ffn, kept, passed, upper, beside):
        w_turned, w_o, gain = w_attn
        w_gu, w_d = w_ffn
        (
            inputs, rms_one, normed, pieces, attended, attn_low, lse, middle, rms_two,
            normed_two, gate, up, hidden,
        ) = kept
        grad_low = grad_in.astype(BF)
        low = (grad_low, near(grad_low))
        hid = (hidden, near(hidden))
        two = (normed_two, near(normed_two))
        att = (attn_low, near(attn_low))
        one = (normed, near(normed))
        grad_hidden = lax.dot_general(grad_low, w_d, NT, preferred_element_type=F32)
        sigma = jax.nn.sigmoid(gate)
        grad_gate = (grad_hidden * up * sigma * (1.0 + gate * (1.0 - sigma))).astype(BF)
        grad_up = (grad_hidden * gate * sigma).astype(BF)
        gates = (grad_gate, near(grad_gate))
        ups = (grad_up, near(grad_up))
        if upper is None:
            beside, grad_gate, grad_up, *gates = fence(beside, grad_gate, grad_up, *gates)
        summed = ffn_grads(two, gates, ups, hid, low)
        summed, grad_gate, grad_up = fence(summed, grad_gate, grad_up)
        summed = sum_z(summed)
        grad_normed = dots([grad_gate, grad_up], [w_gu[:, :ffn], w_gu[:, ffn : 2 * ffn]])
        grad_middle = grad_in + norm_back(grad_normed, middle, rms_two, gain[1])
        grad_attn = grad_middle.astype(BF)
        mid = (grad_attn, near(grad_attn))
        grad_o = lax.dot_general(grad_attn, w_o, NT, preferred_element_type=F32).astype(BF)
        grad_o = jnp.transpose(grad_o.reshape(rows, 8, 128), (1, 0, 2))
        if upper is not None:
            grad_o, beside = fence(grad_o, beside)

        grad_o = exchange(grad_o)
        ffn_pair = []
        if upper is not None:
            upper_ffn, upper_attn = upper
            upper_ffn, grad_o = fence(upper_ffn, grad_o)
            ffn_pair = pair_sums(upper_ffn)
            (grad_o,) = send_all(ffn_pair, grad_o)
        grad_o = grad_o.reshape(8, 2, stretch // 16, 16, 128)
        cos_sin = (cosine, sine)
        parts_a, pass_a = attend_back(
            length[0], pieces[0], attended[0], grad_o[:, 0], lse[0], *cos_sin, passed and passed[0]
        )
        parts_a, grad_b = fence(parts_a, grad_o[:, 1])
        if ffn_pair:
            parts_a, grad_b = add_all(ffn_pair, parts_a, grad_b)
            parts_a, grad_b = send_all(ffn_pair, parts_a, grad_b)
        moved_a = exchange(parts_a.reshape(8, 3, stretch, 128))
        parts_b, pass_b = attend_back(
            length[1], pieces[1], attended[1], grad_b, lse[1], *cos_sin, passed and passed[1]
        )
        moved_a, parts_b = fence(moved_a, parts_b)
        moved_b = exchange(parts_b.reshape(8, 3, stretch, 128))
        attn_pair = []
        if ffn_pair:
            (moved_b,) = add_all(ffn_pair, moved_b)
            upper_attn, moved_b = fence(upper_attn, moved_b)
            attn_pair = pair_sums(upper_attn)
            (moved_b,) = send_all(attn_pair, moved_b)
        grad_proj = jnp.concatenate(
            [
                jnp.transpose(moved, (2, 1, 0, 3)).reshape(stretch, 3 * width)
                for moved in (moved_a, moved_b)
            ]
        )
        proj = (grad_proj, near(grad_proj))
        cuts, at = [], 0
        for weight in w_turned:
            cuts.append(grad_proj[:, at : at + weight.shape[1]])
            at += weight.shape[1]
        grad_normed = dots(cuts, w_turned)
        grad = grad_middle + norm_back(grad_normed, inputs, rms_one, gain[0])
        todo = one + att + proj + mid
        return grad, summed, todo, (pass_a, pass_b), ffn_pair, attn_pair, beside

    core = c.astype(jnp.int32).reshape(1)
    ffn_one = gather_ffn(0)
    state = join_stripes(exchange_z(exchange(cut_blocks(tokens)))).astype(F32)
    qkv_one, turned_one, gain_one = gather_first()
    low_one, first_value, kept_one = forward_attention(
        state, qkv_one, gain_one, None, ffn_one[0]
    )
    qkv_two, turned_two, out_two, gain_two = gather_second(ffn_one[0], kept_one[4][0])
    ffn_two = gather_ffn(1, low_one)
    out_one = ffn_one[0][:, 2 * ffn + 3 * width :]
    low_one, other = fence(low_one, cut_blocks(cotangent))
    other = [
        lax.ppermute(lax.dynamic_index_in_dim(other, here ^ k, 0, keepdims=False), ALL, routes[k])
        for k in range(8)
    ]
    middle, more = forward_ffn(state, low_one, out_one, ffn_one, gain_one)
    kept_one += more
    low_two, _, kept_two = forward_attention(middle, qkv_two, gain_two, first_value)
    final, more = forward_ffn(middle, low_two, out_two, ffn_two, gain_two)
    kept_two += more
    final, *other = fence(final, *other)
    grad = jnp.zeros((8, seqs, 2, 16, width), BF)
    for k in range(8):
        grad = lax.dynamic_update_index_in_dim(grad, other[k], lane ^ k, 0)
    grad = join_stripes(grad).astype(F32) * valid
    layer_out = exchange_z(cut_stripes(final.astype(BF)))
    grad, ffn_two_sum, todo, passed, _, _, layer_out = backward_layer(
        grad, (turned_two, out_two, gain_two), ffn_two, kept_two, None, None, layer_out
    )
    grad, *todo = fence(grad, *todo)
    todo = [tuple(todo[n : n + 2]) for n in (0, 2, 4, 6)]
    (attn_two,) = attn_grads(*todo, [[[(0, 3 * width, 0, 0)]], [[(0, width, 0, 3 * width)]]])
    attn_two, grad, layer_out = fence(attn_two, grad, layer_out)
    attn_two = sum_z(attn_two)
    layer_out = exchange(layer_out)
    grad, ffn_one_sum, todo, _, ffn_pair_two, attn_pair_two, layer_out = backward_layer(
        grad,
        (turned_one, out_one, gain_one),
        ffn_one,
        kept_one,
        passed,
        (ffn_two_sum, attn_two),
        layer_out,
    )
    layer_out = join_blocks(layer_out)
    grad, *todo = fence(grad, *todo)
    todo = [tuple(todo[n : n + 2]) for n in (0, 2, 4, 6)]
    places = [[[(0, 2 * width, 0, 0), (2 * width, width, 1, 0)]], [[(0, width, 1, width)]]]
    attn_pair_one = [
        Reduction(part.reshape(4, 2, 2, 32, -1), order)
        for part, order in zip(attn_grads(*todo, places), ("yxz", "xyz"))
    ]
    (grad,) = send_all(attn_pair_one, grad)
    input_grad = cut_stripes(grad.astype(BF))
    add_all(attn_pair_two, *[r.partial for r in attn_pair_one])
    send_all(attn_pair_two)
    add_all(attn_pair_one, *[r.partial for r in attn_pair_two])
    send_all(attn_pair_one)
    mark = [r.partial for r in attn_pair_one]
    ffn_one_sum, input_grad, *mark = fence(ffn_one_sum, input_grad, *mark)
    ffn_pair_one = pair_sums(ffn_one_sum)
    (input_grad,) = send_all(ffn_pair_one, input_grad)
    input_grad = exchange_z(input_grad)
    add_all(attn_pair_one)
    send_all(attn_pair_one)
    (input_grad,) = add_all(ffn_pair_one, input_grad)
    (input_grad,) = send_all(ffn_pair_one, input_grad)
    input_grad = exchange(input_grad)
    add_all(attn_pair_two + ffn_pair_one)
    add_all(attn_pair_one)
    input_grad = join_blocks(input_grad).astype(F32)

    out_grad, qkv_grad, gate_grad, up_grad, down_grad = [], [], [], [], []
    for attn_pair, ffn_pair in ((attn_pair_one, ffn_pair_one), (attn_pair_two, ffn_pair_two)):
        field = jnp.concatenate([r.partial for r in attn_pair], axis=1)
        qkv_grad.append(field[:, : 3 * width])
        out_grad.append(field[:, 3 * width :])
        field = jnp.concatenate([r.partial for r in ffn_pair], axis=1)
        gate_grad.append(field[:, :ffn])
        up_grad.append(field[:, ffn : 2 * ffn])
        down_grad.append(unpack(field[:, 2 * ffn :]))

    def gain_grad(pairs, gain):
        total = sum(jnp.sum(w.astype(F32) * grad, axis=1) for w, grad in pairs)
        return total / gain.astype(F32)

    attn_gain = [gain_grad([(w_qkv[n], qkv_grad[n])], norm_attn[n]) for n in range(2)]
    ffn_gain = [
        gain_grad([(w_gate[n], gate_grad[n]), (w_up[n], up_grad[n])], norm_ffn[n])
        for n in range(2)
    ]
    return (
        layer_out,
        input_grad,
        jnp.stack(attn_gain),
        jnp.stack(qkv_grad),
        jnp.stack(out_grad),
        jnp.stack(ffn_gain),
        jnp.stack(gate_grad),
        jnp.stack(up_grad),
        jnp.stack(down_grad),
    )


IN_SPECS = (
    ("grp", "seq", None),
    ("grp", None),
    (None, ("grp", "seq")),
    (None, ("grp", "seq"), None),
    (None, ("grp", "seq"), None),
    (None, ("grp", "seq")),
    (None, ("grp", "seq"), None),
    (None, ("grp", "seq"), None),
    (None, ("grp", "seq"), None),
    ("grp", "seq", None),
)
OUT_SPECS = (
    ("grp", "seq", None),
    ("grp", "seq", None),
    (None, ("grp", "seq")),
    (None, ("grp", "seq"), None),
    (None, ("grp", "seq"), None),
    (None, ("grp", "seq")),
    (None, ("grp", "seq"), None),
    (None, ("grp", "seq"), None),
    (None, ("grp", "seq"), None),
)


def solution(mesh):
    if mesh.shape["grp"] == 4 and mesh.shape["seq"] == 8:
        split = Mesh(mesh.devices.reshape(2, 2, 4, 2), ALL)
        names = {"grp": ("y", "c"), "seq": ("z", "x"), ("grp", "seq"): ALL, None: None}
        program = body_planes
    else:
        split = mesh
        names = {"grp": "grp", "seq": "seq", ("grp", "seq"): ("grp", "seq"), None: None}
        program = body

    def specs(table):
        return tuple(P(*(names[name] for name in row)) for row in table)

    return jax.shard_map(
        program,
        mesh=split,
        in_specs=specs(IN_SPECS),
        out_specs=specs(OUT_SPECS),
        check_vma=False,
    )
```

```python
import jax
import jax.numpy as jnp
from jax import lax
from jax.experimental import pallas as pl
from jax.experimental.pallas import tpu as pltpu
from jax.sharding import Mesh
from jax.sharding import PartitionSpec as P

HEADS = 16
EPSILON = 1e-06
NEGATIVE = -1e30
PRECISE = lax.Precision.HIGHEST
BF = jnp.bfloat16
F32 = jnp.float32
ALL = ("y", "c", "z", "x")
PLANE = ("c", "y", "x")
VMEM_BYTES = 50 * 1024 * 1024
ANY = pl.BlockSpec(memory_space=pl.ANY)
SMEM = pl.BlockSpec(memory_space=pltpu.SMEM)
NT = (((1,), (1,)), ((), ()))
TN = (((0,), (0,)), ((), ()))


def params(**more):
    return pltpu.CompilerParams(vmem_limit_bytes=VMEM_BYTES, **more)


def assemble(where, sides, relatives):
    rows = sides[0][0].shape[1]
    widths = [side[0].shape[2] for side in sides]
    kind = sides[0][0].dtype
    flat = [piece for side in sides for piece in side]
    count = len(flat)

    def kernel(where_ref, *rest):
        ins, out, sems = rest[:count], rest[count], rest[-1]
        y, c, z, x = (where_ref[n] for n in range(4))
        copies, puts = [], []
        n, first = 0, 0
        for side, relative in enumerate(relatives):
            held = rest[count + 1 + side]
            lanes = pl.ds(first, widths[side])
            first += widths[side]
            for at, (dy, dc, dx) in enumerate(relative):
                for dz in range(4):
                    spot = held.at[at, dz]
                    target = out.at[y ^ dy, c ^ dc, z ^ dz, x ^ dx, :, lanes]
                    copies.append(pltpu.make_async_copy(ins[n].at[dz], spot, sems.at[0, n, dz]))
                    puts.append(pltpu.make_async_copy(spot, target, sems.at[1, n, dz]))
                n += 1
        for copy in copies:
            copy.start()
        for copy, put in zip(copies, puts):
            copy.wait()
            put.start()
        for put in puts:
            put.wait()

    out = pl.pallas_call(
        kernel,
        in_specs=[SMEM] + [ANY] * count,
        out_specs=ANY,
        out_shape=jax.ShapeDtypeStruct((2, 2, 4, 2, rows, sum(widths)), kind),
        scratch_shapes=[
            pltpu.VMEM((len(side), 4, rows, width), kind) for side, width in zip(sides, widths)
        ]
        + [pltpu.SemaphoreType.DMA((2, count, 4))],
        compiler_params=params(),
        name="assemble",
    )(where, *flat)
    return out.reshape(-1, sum(widths))


def swap(value, axis):
    return lax.ppermute(value, axis, [(0, 1), (1, 0)])


def hop(value, offset):
    return lax.ppermute(value, "z", [(i, i ^ offset) for i in range(4)])


def gather_z_first(where, shard, first, second):
    stack = jnp.stack([shard] + [hop(shard, k) for k in (1, 2, 3)])
    near = swap(stack, first)
    ring = [((0, 0), stack), ((1, 0), near)]
    ring += [((0, 1), swap(stack, second)), ((1, 1), swap(near, second))]
    pieces, relative = [], []
    for (one, two), piece in ring:
        moved = {first: one, second: two}
        for dc, held in ((0, piece), (1, swap(piece, "c"))):
            pieces.append(held)
            relative.append((moved["y"], dc, moved["x"]))
    return assemble(where, [pieces], [relative])


def fence(*values):
    return lax.optimization_barrier(values)


class Reduction:
    def __init__(self, partial, order, names="zyx"):
        self.partial = partial
        self.order = order
        self.names = list(names)
        self.moved = None

    def send(self):
        axis, self.order = self.order[0], self.order[1:]
        dim = self.names.index(axis)
        self.names.pop(dim)
        here = lax.axis_index(axis)

        def block(slot):
            return lax.dynamic_index_in_dim(self.partial, slot, dim, keepdims=False)

        if axis == "z":
            self.moved = [hop(block(here ^ k), k) for k in (1, 2, 3)]
        else:
            self.moved = [swap(block(1 - here), axis)]
        self.partial = block(here)

    def add(self):
        total = self.partial.astype(F32)
        for part in self.moved:
            total = total + part.astype(F32)
        self.moved = None
        self.partial = total.astype(BF) if self.order else total


def send_all(reductions, *others):
    reductions = [r for r in reductions if r.order]
    held = fence(*[r.partial for r in reductions], *others)
    for reduction, partial in zip(reductions, held):
        reduction.partial = partial
        reduction.send()
    return held[len(reductions) :]


def add_all(reductions, *others):
    reductions = [r for r in reductions if r.moved is not None]
    flat = [part for r in reductions for part in r.moved]
    held = fence(*flat, *others)
    at = 0
    for reduction in reductions:
        count = len(reduction.moved)
        reduction.moved = list(held[at : at + count])
        at += count
        reduction.add()
    held = fence(*[r.partial for r in reductions], *held[at:])
    for reduction, partial in zip(reductions, held):
        reduction.partial = partial
    return held[len(reductions) :]


def turn(field, cosine, signed_sine):
    lane = lax.broadcasted_iota(jnp.int32, field.shape, 1)
    other = jnp.where(
        lane % 64 < 32, pltpu.roll(field, 96, axis=1), pltpu.roll(field, 32, axis=1)
    )
    return field * cosine + other * signed_sine


def project_qkv(inputs, gain, weights, cosine, signed_sine, first_value):
    rows, width = inputs.shape
    devices = width // 128

    def kernel(in_ref, gain_ref, w_q_ref, w_k_ref, w_v_ref, cos_ref, sin_ref, *rest):
        out_ref, normed_ref = rest[-2:]
        step = pl.program_id(0)

        @pl.when(step == 0)
        def _():
            field = in_ref[...].astype(F32)
            rms = lax.rsqrt(jnp.mean(field * field, axis=1, keepdims=True) + EPSILON)
            normed_ref[...] = (field * rms * gain_ref[0:1, :]).astype(BF)

        def product(w_ref):
            return jnp.dot(normed_ref[...], w_ref[...], preferred_element_type=F32)

        def turned(w_ref):
            field = product(w_ref)
            for n in range(devices):
                part = field[:, 128 * n : 128 * n + 128]
                out_ref[n, 0] = turn(part, cos_ref[...], sin_ref[...]).astype(BF)

        @pl.when(step == 0)
        def _():
            turned(w_q_ref)

        @pl.when(step == 1)
        def _():
            turned(w_k_ref)

        @pl.when(step == 2)
        def _():
            field = product(w_v_ref)
            for n in range(devices):
                part = field[:, 128 * n : 128 * n + 128]
                if first_value is not None:
                    part = 0.5 * part + 0.5 * rest[0][n, 0].astype(F32)
                out_ref[n, 0] = part.astype(BF)

    whole = lambda step: (0, 0)
    in_specs = [pl.BlockSpec((rows, width), whole), pl.BlockSpec((2, width), whole)]
    for _, start in weights:
        in_specs.append(pl.BlockSpec((width, width), lambda step, start=start: (0, start)))
    in_specs += [pl.BlockSpec((rows, 128), whole)] * 2
    operands = [inputs, gain] + [array for array, _ in weights] + [cosine, signed_sine]
    if first_value is not None:
        in_specs.append(pl.BlockSpec((devices, 1, rows, 128), lambda step: (0, 2, 0, 0)))
        operands.append(first_value)
    return pl.pallas_call(
        kernel,
        grid=(3,),
        in_specs=in_specs,
        out_specs=[
            pl.BlockSpec((devices, 1, rows, 128), lambda step: (0, step, 0, 0)),
            pl.BlockSpec((rows, width), whole),
        ],
        out_shape=[
            jax.ShapeDtypeStruct((devices, 3, rows, 128), BF),
            jax.ShapeDtypeStruct((rows, width), BF),
        ],
        compiler_params=params(dimension_semantics=("arbitrary",)),
        name="project_qkv",
    )(*operands)


def forward_ffn(low, inputs, w_o, w_gu, w_d, gain, ffn, kept, first_row, total_rows):
    rows, width = inputs.shape
    devices = low.shape[0]
    half = ffn // 2
    w_o, out_column = w_o
    kinds = [
        ((total_rows, width), BF),
        ((total_rows, width), F32),
        ((total_rows, width), BF),
        ((total_rows, ffn), BF),
        ((total_rows, ffn), BF),
        ((total_rows, ffn), BF),
    ]
    count = len(kinds)

    def kernel(low_ref, in_ref, wo_ref, wgu_ref, wd_ref, gain_ref, *refs):
        if kept is not None:
            refs = refs[count:]
        outs, refs = refs[: count + 1], refs[count + 1 :]
        att, wo, wg, wu, wd, mid, norm, gates, ups, hids, result, sems, out_sems = refs
        spans = [slice(0, half), slice(half, ffn)]
        loads = [
            pltpu.make_async_copy(
                low_ref.at[n], att.at[:, pl.ds(128 * n, 128)], sems.at[n]
            )
            for n in range(devices)
        ]
        loads.append(
            pltpu.make_async_copy(wo_ref.at[:, pl.ds(out_column, width)], wo, sems.at[devices])
        )
        late = []
        for n in range(2):
            at = devices + 1 + 3 * n
            column = pl.ds(n * half, half)
            late.append(
                [
                    pltpu.make_async_copy(wgu_ref.at[:, column], wg.at[n], sems.at[at]),
                    pltpu.make_async_copy(
                        wgu_ref.at[:, pl.ds(ffn + n * half, half)], wu.at[n], sems.at[at + 1]
                    ),
                    pltpu.make_async_copy(wd_ref.at[column], wd.at[n], sems.at[at + 2]),
                ]
            )
        for copy in loads + late[0] + late[1]:
            copy.start()
        puts = []

        def put(source, target, index):
            copy = pltpu.make_async_copy(source, target, out_sems.at[len(puts)])
            copy.start()
            puts.append(copy)

        own = pl.ds(first_row, rows)
        for copy in loads:
            copy.wait()
        put(att, outs[0].at[own], 0)
        middle = in_ref[...] + jnp.dot(att[...], wo[...], preferred_element_type=F32)
        mid[...] = middle
        put(mid, outs[1].at[own], 1)
        rms = lax.rsqrt(jnp.mean(middle * middle, axis=1, keepdims=True) + EPSILON)
        normed = (middle * rms * gain_ref[1:2, :]).astype(BF)
        norm[...] = normed
        put(norm, outs[2].at[own], 2)
        total = middle
        for n in range(2):
            late[n][0].wait()
            gate = jnp.dot(norm[...], wg[n], preferred_element_type=F32)
            late[n][1].wait()
            up = jnp.dot(norm[...], wu[n], preferred_element_type=F32)
            hidden = (gate * jax.nn.sigmoid(gate) * up).astype(BF)
            gates[:, spans[n]] = gate.astype(BF)
            ups[:, spans[n]] = up.astype(BF)
            hids[:, spans[n]] = hidden
            late[n][2].wait()
            total = total + jnp.dot(hidden, wd[n], preferred_element_type=F32)
        put(gates, outs[3].at[own], 3)
        put(ups, outs[4].at[own], 4)
        put(hids, outs[5].at[own], 5)
        result[...] = total
        put(result, outs[6], 6)
        for copy in puts:
            copy.wait()

    vmem = pl.BlockSpec(memory_space=pltpu.VMEM)
    operands = [low, inputs, w_o, w_gu, w_d, gain]
    in_specs = [ANY, vmem, ANY, ANY, ANY, vmem]
    aliases = {}
    if kept is not None:
        aliases = {len(operands) + n: n for n in range(count)}
        operands += list(kept)
        in_specs += [ANY] * count
    outs = pl.pallas_call(
        kernel,
        in_specs=in_specs,
        out_specs=[ANY] * (count + 1),
        out_shape=[jax.ShapeDtypeStruct(*kind) for kind in kinds]
        + [jax.ShapeDtypeStruct((rows, width), F32)],
        scratch_shapes=[
            pltpu.VMEM((rows, width), BF),
            pltpu.VMEM((width, width), BF),
            pltpu.VMEM((2, width, half), BF),
            pltpu.VMEM((2, width, half), BF),
            pltpu.VMEM((2, half, width), BF),
            pltpu.VMEM((rows, width), F32),
            pltpu.VMEM((rows, width), BF),
            pltpu.VMEM((rows, ffn), BF),
            pltpu.VMEM((rows, ffn), BF),
            pltpu.VMEM((rows, ffn), BF),
            pltpu.VMEM((rows, width), F32),
            pltpu.SemaphoreType.DMA((devices + 7,)),
            pltpu.SemaphoreType.DMA((count + 1,)),
        ],
        input_output_aliases=aliases,
        compiler_params=params(),
        name="forward_ffn",
    )(*operands)
    return outs[count], outs[:count]


def weight_grads(core, groups, chunks):
    rows = groups[0][0][0].shape[0]
    operands, scratch, plans = [], [], []
    widths, count = {}, 0
    for (left, rights), places in zip(groups, chunks):
        size = left[0].shape[1] // 4
        window = -(-size // 128) * 128
        plan = {"size": size, "window": window, "left": len(operands), "held": len(scratch)}
        operands += list(left)
        scratch.append(pltpu.VMEM((2, 2 * rows, window), BF))
        plan["rights"] = []
        for right, parts in zip(rights, places):
            cols = right[0].shape[1]
            plan["rights"].append((len(operands), len(scratch), parts))
            operands += list(right)
            scratch.append(pltpu.VMEM((2 * rows, cols), BF))
            for _, span, result, at in parts:
                count += 1
                spread = span if size == window else 3 * span
                widths[result] = max(widths.get(result, 0), at + spread)
        plans.append(plan)
    shapes = [(4, 2, 64, widths[n]) for n in range(len(widths))]
    first_stage = len(scratch)
    scratch += [pltpu.VMEM(shape, BF) for shape in shapes]
    scratch += [
        pltpu.SemaphoreType.DMA((len(operands), 2)),
        pltpu.SemaphoreType.DMA((count,)),
    ]
    inputs, results = len(operands), len(shapes)

    def put_thirds(stage, part, total, at, span, size):
        for z in range(4):
            for x in range(2):
                low = z * (size // 4) + x * (size // 8)
                for third in range(3):
                    first, last = low + 32 * third, low + min(32 * third + 32, size // 8)
                    piece = total[first:last]
                    missing = 32 - piece.shape[0]
                    if missing:
                        piece = jnp.concatenate([piece, jnp.zeros((missing, span), F32)])
                    lane = at + third * span
                    stage[z, part, 32 * x : 32 * x + 32, lane : lane + span] = piece.astype(BF)

    def kernel(core_ref, *refs):
        ins, outs, work = refs[:inputs], refs[inputs : inputs + results], refs[inputs + results :]
        stages = work[first_stage : first_stage + results]
        in_sems, out_sems = work[-2:]
        loads = []
        for plan in plans:
            held, size, window = work[plan["held"]], plan["size"], plan["window"]
            slack = window - size
            left = []
            for side in range(2):
                for part in range(2):
                    start = 2 * part * size + core_ref[0] * (size - slack)
                    span = pl.ds(pl.multiple_of(start, 128), window)
                    at = plan["left"] + side
                    left.append(
                        pltpu.make_async_copy(
                            ins[at].at[:, span],
                            held.at[part, pl.ds(side * rows, rows)],
                            in_sems.at[at, part],
                        )
                    )
            rights = []
            for at, spot, _ in plan["rights"]:
                rights.append(
                    [
                        pltpu.make_async_copy(
                            ins[at + side],
                            work[spot].at[pl.ds(side * rows, rows)],
                            in_sems.at[at + side, 0],
                        )
                        for side in range(2)
                    ]
                )
            loads.append((left, rights))
            for copy in left + [copy for pair in rights for copy in pair]:
                copy.start()
        puts = []
        for plan, (left, rights) in zip(plans, loads):
            size, window = plan["size"], plan["window"]
            held = work[plan["held"]]
            for copy in left:
                copy.wait()
            for pair, (_, spot, parts) in zip(rights, plan["rights"]):
                for copy in pair:
                    copy.wait()
                for first, span, result, at in parts:
                    right = work[spot][:, first : first + span]
                    stage = stages[result]
                    wide = span if size == window else 3 * span
                    for part in range(2):
                        total = lax.dot_general(
                            held[part], right, TN, preferred_element_type=F32
                        )
                        if size == window:
                            total = total.astype(BF).reshape(4, size // 4, span)
                            stage[:, part, :, at : at + span] = total
                        else:
                            own = jnp.where(core_ref[0] == 0, total[:size], total[window - size :])
                            put_thirds(stage, part, own, at, span, size)
                    lanes = pl.ds(at, wide)
                    put = pltpu.make_async_copy(
                        stage.at[:, :, :, lanes],
                        outs[result].at[:, :, :, lanes],
                        out_sems.at[len(puts)],
                    )
                    put.start()
                    puts.append(put)
        for put in puts:
            put.wait()

    return pl.pallas_call(
        kernel,
        in_specs=[SMEM] + [ANY] * inputs,
        out_specs=[ANY] * results,
        out_shape=[jax.ShapeDtypeStruct(shape, BF) for shape in shapes],
        scratch_shapes=scratch,
        compiler_params=params(),
        name="weight_grads",
    )(core, *operands)


def rows_of(block):
    return block.reshape(-1, 128)


def attend(length, pieces):
    tile, wide_tile = 256, 512
    slots = pieces.shape[2] * 128
    tiles, steps = slots // tile, slots // wide_tile
    per, wide_per, ratio = tile // 128, wide_tile // 128, wide_tile // tile

    def kernel(len_ref, piece_ref, out_ref, lse_ref, held, flipped, logit, sems):
        step = pl.program_id(0)

        @pl.when(step == 0)
        def _():
            copies = [
                pltpu.make_async_copy(
                    piece_ref.at[device], held.at[:, :, device], sems.at[device]
                )
                for device in range(8)
            ]
            for copy in copies:
                copy.start()
            for copy in copies:
                copy.wait()

        @pl.when(step == 0)
        def _():
            for block in range(tiles):
                key = rows_of(held[1, pl.ds(per * block, per)])
                flipped[block] = key.T

        used = len_ref[0]
        query = rows_of(held[0, pl.ds(wide_per * step, wide_per)]) * BF(0.125)
        lane = lax.broadcasted_iota(jnp.int32, (wide_tile, 128), 1)
        low = lane < 64
        zero = jnp.zeros_like(query)
        queries = [jnp.where(low, query, zero), jnp.where(low, zero, query)]

        def score(block, tops, masked):
            key_t = flipped[block]
            result = []
            for head in range(2):
                field = jnp.dot(queries[head], key_t, preferred_element_type=F32)
                if masked:
                    query_pos = step * wide_tile + lax.broadcasted_iota(jnp.int32, field.shape, 0)
                    key_pos = block * tile + lax.broadcasted_iota(jnp.int32, field.shape, 1)
                    seen = (key_pos <= query_pos) & (key_pos < used)
                    field = jnp.where(seen, field, NEGATIVE)
                logit[head, block] = field
                top = jnp.maximum(field[:, :128], field[:, 128:])
                result.append(jnp.maximum(tops[head], top))
            return tuple(result)

        full = jnp.minimum(ratio * step, used // tile)
        end = jnp.minimum(ratio * step + ratio, (used + tile - 1) // tile)
        low_top = jnp.full((wide_tile, 128), NEGATIVE, F32)
        tops = lax.fori_loop(0, full, lambda b, s: score(b, s, False), (low_top, low_top))
        tops = lax.fori_loop(full, end, lambda b, s: score(b, s, True), tops)
        tops = [jnp.max(top, axis=1, keepdims=True) for top in tops]
        wide = [jnp.broadcast_to(top, (wide_tile, tile)) for top in tops]
        low_key = low[:tile]
        one = jnp.ones((tile, 128), BF)

        def mix(block, sums):
            value = rows_of(held[2, pl.ds(per * block, per)])
            values = [jnp.where(low_key, value, one), jnp.where(low_key, one, value)]
            result = []
            for head in range(2):
                probs = jnp.exp(logit[head, block] - wide[head]).astype(BF)
                result.append(
                    sums[head] + jnp.dot(probs, values[head], preferred_element_type=F32)
                )
            return tuple(result)

        nothing = jnp.zeros((wide_tile, 128), F32)
        sums = lax.fori_loop(0, end, mix, (nothing, nothing))
        totals = [sums[0][:, 64:65], sums[1][:, 0:1]]
        out = jnp.where(low, sums[0] / totals[0], sums[1] / totals[1])
        out = out.astype(BF).reshape(wide_per, 8, 16, 128)
        for device in range(8):
            out_ref[device, pl.ds(wide_per * step, wide_per)] = out[:, device]
        level = jnp.where(low, tops[0] + jnp.log(totals[0]), tops[1] + jnp.log(totals[1])).T
        start = pl.multiple_of(step * wide_tile, wide_tile)
        lse_ref[0:1, pl.ds(start, wide_tile)] = level[0:1]
        lse_ref[1:2, pl.ds(start, wide_tile)] = level[64:65]

    return pl.pallas_call(
        kernel,
        grid=(steps,),
        in_specs=[SMEM, ANY],
        out_specs=[
            pl.BlockSpec((8,) + pieces.shape[2:], lambda i: (0, 0, 0, 0)),
            pl.BlockSpec((8, slots), lambda i: (0, 0)),
        ],
        out_shape=[
            jax.ShapeDtypeStruct((8,) + pieces.shape[2:], BF),
            jax.ShapeDtypeStruct((8, slots), F32),
        ],
        scratch_shapes=[
            pltpu.VMEM((3, slots // 128, 8, 16, 128), BF),
            pltpu.VMEM((tiles, 128, tile), BF),
            pltpu.VMEM((2, tiles, wide_tile, tile), F32),
            pltpu.SemaphoreType.DMA((8,)),
        ],
        compiler_params=params(dimension_semantics=("arbitrary",)),
        name="attend",
    )(length, pieces)


def attend_back(length, pieces, attended, grads, lse, cosine, signed_sine, passed):
    tile, wide = 256, 512
    slots = pieces.shape[2] * 128
    tiles = slots // tile
    per, wide_per, ratio = tile // 128, wide // 128, wide // tile
    upper = passed is None

    def kernel(*refs):
        len_ref, piece_ref, att_ref, grad_ref, lse_ref, cos_ref, sin_ref = refs[:7]
        refs = refs[7:]
        if upper:
            passed_ref = None
            out_ref, give_ref = refs[:2]
            refs = refs[2:]
        else:
            passed_ref, out_ref = refs[:2]
            give_ref = None
            refs = refs[2:]
        held, att, grad, delta, level, query_acc, key_acc, value_acc, sems = refs
        step = pl.program_id(0)
        used = len_ref[0]

        @pl.when(step == 0)
        def _():
            copies = []
            for device in range(8):
                for n, (source, target) in enumerate(
                    (
                        (grad_ref.at[device], grad.at[:, device]),
                        (att_ref.at[device], att.at[:, device]),
                        (piece_ref.at[device], held.at[:, :, device]),
                    )
                ):
                    copies.append(pltpu.make_async_copy(source, target, sems.at[n, device]))
            for copy in copies:
                copy.start()
            for copy in copies:
                copy.wait()

        @pl.when(step == 0)
        def _():
            query_acc[...] = jnp.zeros_like(query_acc)
            line = lax.broadcasted_iota(jnp.int32, (8, 128), 0)
            lane = lax.broadcasted_iota(jnp.int32, (8, 128), 1)
            pick = jnp.where(line == lane // 64, 1.0, 0.0).astype(F32)
            for block in range(tiles):
                span = slice(tile * block, tile * block + tile)
                product = rows_of(grad[pl.ds(per * block, per)]).astype(F32) * rows_of(
                    att[pl.ds(per * block, per)]
                ).astype(F32)
                delta[:, span] = lax.dot_general(
                    pick, product, NT, precision=PRECISE, preferred_element_type=F32
                )
            place = lax.broadcasted_iota(jnp.int32, (8, slots), 1)
            level[...] = jnp.where(place < used, lse_ref[...], -NEGATIVE)

        key = rows_of(held[1, pl.ds(wide_per * step, wide_per)])
        value = rows_of(held[2, pl.ds(wide_per * step, wide_per)])
        lane = lax.broadcasted_iota(jnp.int32, (wide, 128), 1)
        low = lane < 64

        def head_part(field, head):
            keep = low[: field.shape[0]]
            nothing = jnp.zeros_like(field)
            return jnp.where(keep, field, nothing) if head == 0 else jnp.where(keep, nothing, field)

        scaled = key * BF(0.125)
        keys = [head_part(scaled, head) for head in range(2)]
        values = [head_part(value, head) for head in range(2)]
        key_acc[...] = jnp.zeros_like(key_acc)
        value_acc[...] = jnp.zeros_like(value_acc)

        def visit(block, masked):
            query = rows_of(held[0, pl.ds(per * block, per)])
            grad_out = rows_of(grad[pl.ds(per * block, per)])
            start = pl.multiple_of(block * tile, tile)
            spans = pl.ds(start, tile)
            query_sum = jnp.zeros((tile, 128), F32)
            key_sum = jnp.zeros((wide, 128), F32)
            value_sum = jnp.zeros((wide, 128), F32)
            for head in range(2):
                logits = lax.dot_general(keys[head], query, NT, preferred_element_type=F32)
                probs = jnp.exp(logits - level[head : head + 1, spans])
                if masked:
                    key_pos = step * wide + lax.broadcasted_iota(jnp.int32, probs.shape, 0)
                    query_pos = block * tile + lax.broadcasted_iota(jnp.int32, probs.shape, 1)
                    probs = jnp.where(key_pos <= query_pos, probs, 0.0)
                grad_probs = lax.dot_general(
                    values[head], grad_out, NT, preferred_element_type=F32
                )
                grad_logits = (probs * (grad_probs - delta[head : head + 1, spans])).astype(BF)
                value_sum += jnp.dot(
                    probs.astype(BF), head_part(grad_out, head), preferred_element_type=F32
                )
                key_sum += jnp.dot(
                    grad_logits, head_part(query, head), preferred_element_type=F32
                )
                query_sum += lax.dot_general(
                    grad_logits, keys[head], TN, preferred_element_type=F32
                )
            query_acc[spans, :] += query_sum
            key_acc[...] += key_sum
            value_acc[...] += value_sum

        end = (used + tile - 1) // tile

        def body(block, carry, masked):
            visit(block, masked)
            return carry

        first = ratio * step
        lax.fori_loop(first, jnp.minimum(first + ratio, end), lambda b, s: body(b, s, True), 0)
        lax.fori_loop(first + ratio, end, lambda b, s: body(b, s, False), 0)

        def put(member, block, field):
            count = field.shape[0] // 128
            field = field.astype(BF).reshape(count, 8, 16, 128)
            for device in range(8):
                out_ref[device, member, pl.ds(count * block, count)] = field[:, device]

        start = pl.multiple_of(step * wide, wide)
        spans = pl.ds(start, wide)
        key_grad = key_acc[...] * 0.125
        put(1, step, turn(key_grad, cos_ref[spans, :], -sin_ref[spans, :]))
        if upper:
            half = 0.5 * value_acc[...]
            give_ref[spans, :] = half
            put(2, step, half)
        else:
            put(2, step, value_acc[...] + passed_ref[spans, :])

        @pl.when(step == slots // wide - 1)
        def _():
            for block in range(tiles):
                part = slice(tile * block, tile * block + tile)
                put(0, block, turn(query_acc[part, :], cos_ref[part, :], -sin_ref[part, :]))

    flat = lambda i: (0, 0)
    table = pl.BlockSpec((slots, 128), flat)
    in_specs = [SMEM, ANY, ANY, ANY, pl.BlockSpec((8, slots), flat), table, table]
    operands = [length, pieces, attended, grads, lse, cosine, signed_sine]
    out_specs = [pl.BlockSpec(pieces.shape, lambda i: (0, 0, 0, 0, 0))]
    out_shape = [jax.ShapeDtypeStruct(pieces.shape, BF)]
    if upper:
        out_specs.append(table)
        out_shape.append(jax.ShapeDtypeStruct((slots, 128), F32))
    else:
        in_specs.append(table)
        operands.append(passed)
    outs = pl.pallas_call(
        kernel,
        grid=(slots // wide,),
        in_specs=in_specs,
        out_specs=out_specs,
        out_shape=out_shape,
        scratch_shapes=[
            pltpu.VMEM((3, slots // 128, 8, 16, 128), BF),
            pltpu.VMEM((slots // 128, 8, 16, 128), BF),
            pltpu.VMEM((slots // 128, 8, 16, 128), BF),
            pltpu.VMEM((8, slots), F32),
            pltpu.VMEM((8, slots), F32),
            pltpu.VMEM((slots, 128), F32),
            pltpu.VMEM((wide, 128), F32),
            pltpu.VMEM((wide, 128), F32),
            pltpu.SemaphoreType.DMA((3, 8)),
        ],
        compiler_params=params(dimension_semantics=("arbitrary",)),
        name="attend_back",
    )(*operands)
    return outs if upper else (outs[0], None)


def block_spans(total_rows):
    return [(offset, min(512, total_rows - offset)) for offset in range(0, total_rows, 512)]


def rotate(field, cosine, sine_table):
    half_dim = field.shape[-1] // 2
    first_half = field[..., :half_dim]
    second_half = field[..., half_dim:]
    return jnp.concatenate(
        [
            first_half * cosine - second_half * sine_table,
            second_half * cosine + first_half * sine_table,
        ],
        axis=-1,
    )


def allowed(query_pos, key_pos, lengths):
    causal = key_pos[None, None, :] <= query_pos[None, :, None]
    inside = key_pos[None, None, :] < lengths[:, None, None]
    return (causal & inside)[:, None, :, :]


def attend_gathered(q_heads, k_flat, v_flat, lengths, positions, score_scale):
    seq_count, stretch_len, head_count, head_dim = q_heads.shape
    first_row = jnp.int32(0)
    k_piece = lax.all_gather(k_flat, "seq", axis=1, tiled=True)
    v_piece = lax.all_gather(v_flat, "seq", axis=1, tiled=True)
    running_max = jnp.full((seq_count, head_count, stretch_len), NEGATIVE, jnp.float32)
    row_total = jnp.zeros((seq_count, head_count, stretch_len), jnp.float32)
    weighted = jnp.zeros((seq_count, stretch_len, head_count, head_dim), jnp.float32)
    for offset, block_len in block_spans(k_piece.shape[1]):
        k_block = k_piece[:, offset : offset + block_len].reshape(
            seq_count, block_len, head_count, head_dim
        )
        v_block = (
            v_piece[:, offset : offset + block_len]
            .reshape(seq_count, block_len, head_count, head_dim)
            .astype(jnp.float32)
        )
        key_pos = first_row + offset + jnp.arange(block_len, dtype=jnp.int32)
        allowed_mask = allowed(positions, key_pos, lengths)
        logits = (
            jnp.einsum("sqhd,skhd->shqk", q_heads, k_block, preferred_element_type=jnp.float32)
            * score_scale
        )
        new_max = jnp.maximum(
            running_max, jnp.max(jnp.where(allowed_mask, logits, NEGATIVE), axis=-1)
        )
        probs = jnp.where(allowed_mask, jnp.exp(logits - new_max[..., None]), 0.0)
        rescale = jnp.exp(running_max - new_max)
        row_total = row_total * rescale + jnp.sum(probs, axis=-1)
        weighted = weighted * jnp.transpose(rescale, (0, 2, 1))[..., None] + jnp.einsum(
            "shqk,skhd->sqhd", probs, v_block, precision=PRECISE, preferred_element_type=jnp.float32
        )
        running_max = new_max
    running_max, row_total, weighted = (running_max, row_total, weighted)
    attended = weighted / jnp.transpose(row_total, (0, 2, 1))[..., None]
    return (attended, running_max + jnp.log(row_total))


def attend_back_gathered(
    q_heads,
    k_heads,
    v_heads,
    q_flat,
    k_flat,
    v_flat,
    grad_heads,
    grad_flat,
    log_total,
    delta_rows,
    lengths,
    positions,
    score_scale,
):
    seq_count, stretch_len, head_count, head_dim = q_heads.shape
    zeros_heads = jnp.zeros((seq_count, stretch_len, head_count, head_dim), jnp.float32)
    carry = zeros_heads
    first_row = jnp.int32(0)
    k_piece = lax.all_gather(k_flat, "seq", axis=1, tiled=True)
    v_piece = lax.all_gather(v_flat, "seq", axis=1, tiled=True)
    for offset, block_len in block_spans(k_piece.shape[1]):
        k_block = k_piece[:, offset : offset + block_len].reshape(
            seq_count, block_len, head_count, head_dim
        )
        v_block = v_piece[:, offset : offset + block_len].reshape(
            seq_count, block_len, head_count, head_dim
        )
        key_pos = first_row + offset + jnp.arange(block_len, dtype=jnp.int32)
        allowed_mask = allowed(positions, key_pos, lengths)
        logits = (
            jnp.einsum("sqhd,skhd->shqk", q_heads, k_block, preferred_element_type=jnp.float32)
            * score_scale
        )
        probs = jnp.where(allowed_mask, jnp.exp(logits - log_total[..., None]), 0.0)
        grad_probs = jnp.einsum(
            "sqhd,skhd->shqk", grad_heads, v_block, preferred_element_type=jnp.float32
        )
        grad_logits = (probs * (grad_probs - delta_rows[..., None])).astype(jnp.bfloat16)
        carry = (
            carry
            + jnp.einsum(
                "shqk,skhd->sqhd", grad_logits, k_block, preferred_element_type=jnp.float32
            )
            * score_scale
        )
    gathered_stats = (
        lax.all_gather(log_total, "seq", axis=2, tiled=True),
        lax.all_gather(delta_rows, "seq", axis=2, tiled=True),
    )
    first_row = jnp.int32(0)
    q_piece = lax.all_gather(q_flat, "seq", axis=1, tiled=True)
    g_piece = lax.all_gather(grad_flat, "seq", axis=1, tiled=True)
    grad_key = zeros_heads
    grad_value = zeros_heads
    for offset, block_len in block_spans(q_piece.shape[1]):
        q_block = q_piece[:, offset : offset + block_len].reshape(
            seq_count, block_len, head_count, head_dim
        )
        g_block = g_piece[:, offset : offset + block_len].reshape(
            seq_count, block_len, head_count, head_dim
        )
        query_pos = first_row + offset + jnp.arange(block_len, dtype=jnp.int32)
        allowed_mask = allowed(query_pos, positions, lengths)
        lse_block = lax.dynamic_slice_in_dim(gathered_stats[0], offset, block_len, 2)
        delta_block = lax.dynamic_slice_in_dim(gathered_stats[1], offset, block_len, 2)
        logits = (
            jnp.einsum("sqhd,skhd->shqk", q_block, k_heads, preferred_element_type=jnp.float32)
            * score_scale
        )
        probs = jnp.where(allowed_mask, jnp.exp(logits - lse_block[..., None]), 0.0)
        grad_value = grad_value + jnp.einsum(
            "shqk,sqhd->skhd",
            probs,
            g_block.astype(jnp.float32),
            precision=PRECISE,
            preferred_element_type=jnp.float32,
        )
        grad_probs = jnp.einsum(
            "sqhd,skhd->shqk", g_block, v_heads, preferred_element_type=jnp.float32
        )
        grad_logits = (probs * (grad_probs - delta_block[..., None])).astype(jnp.bfloat16)
        grad_key = (
            grad_key
            + jnp.einsum(
                "shqk,sqhd->skhd", grad_logits, q_block, preferred_element_type=jnp.float32
            )
            * score_scale
        )
    grad_key, grad_value = (grad_key, grad_value)
    return (carry, grad_key, grad_value)


def body(tokens, seq_lens, norm_attn, w_qkv, w_out, norm_ffn, w_gate, w_up, w_down, cotangent):
    seq_count, stretch_len, model_width = tokens.shape
    head_count = HEADS
    head_dim = model_width // head_count
    score_scale = head_dim ** (-0.5)
    lengths = seq_lens[0]
    positions = lax.axis_index("seq") * stretch_len + jnp.arange(stretch_len, dtype=jnp.int32)
    half_dim = head_dim // 2
    freqs = 10000.0 ** (-jnp.arange(half_dim, dtype=jnp.float32) / half_dim)
    angle = positions.astype(jnp.float32)[:, None] * freqs[None, :]
    cosine = jnp.cos(angle)[:, None, :]
    sine_table = jnp.sin(angle)[:, None, :]

    def heads_of(field):
        return field.reshape(seq_count, stretch_len, head_count, head_dim)

    def gather_layer(layer_index):
        return (
            lax.all_gather(norm_attn[layer_index], ("grp", "seq"), axis=0, tiled=True),
            lax.all_gather(w_qkv[layer_index], ("grp", "seq"), axis=0, tiled=True),
            lax.all_gather(w_out[layer_index], ("grp", "seq"), axis=0, tiled=True),
            lax.all_gather(norm_ffn[layer_index], ("grp", "seq"), axis=0, tiled=True),
            lax.all_gather(w_gate[layer_index], ("grp", "seq"), axis=0, tiled=True),
            lax.all_gather(w_up[layer_index], ("grp", "seq"), axis=0, tiled=True),
            lax.all_gather(w_down[layer_index], ("grp", "seq"), axis=0, tiled=True),
        )

    def gather_again(layer_index):
        return (
            lax.all_gather(norm_attn[layer_index], ("grp", "seq"), axis=0, tiled=True),
            lax.all_gather(w_qkv[layer_index], ("grp", "seq"), axis=0, tiled=True),
            lax.all_gather(w_out[layer_index], ("grp", "seq"), axis=0, tiled=True),
            lax.all_gather(norm_ffn[layer_index], ("grp", "seq"), axis=0, tiled=True),
            lax.all_gather(w_gate[layer_index], ("grp", "seq"), axis=0, tiled=True),
            lax.all_gather(w_up[layer_index], ("grp", "seq"), axis=0, tiled=True),
            lax.all_gather(w_down[layer_index], ("grp", "seq"), axis=0, tiled=True),
        )

    def forward_layer(inputs, params, first_value):
        gain_one, mat_qkv, mat_out, gain_two, mat_gate, mat_up, mat_down = params
        rms_one = lax.rsqrt(jnp.mean(inputs * inputs, axis=-1, keepdims=True) + EPSILON)
        normed = (inputs * rms_one * gain_one.astype(jnp.float32)).astype(jnp.bfloat16)
        projected = jnp.dot(normed, mat_qkv, preferred_element_type=jnp.float32)
        query_raw = projected[:, :model_width]
        key_raw = projected[:, model_width : 2 * model_width]
        value_raw = projected[:, 2 * model_width :]
        if first_value is None:
            values = value_raw.astype(jnp.bfloat16)
        else:
            values = (0.5 * value_raw + 0.5 * first_value.astype(jnp.float32)).astype(jnp.bfloat16)
        query_rot = rotate(heads_of(query_raw), cosine, sine_table).astype(jnp.bfloat16)
        key_rot = rotate(heads_of(key_raw), cosine, sine_table).astype(jnp.bfloat16)
        attended, log_total = attend_gathered(
            query_rot,
            key_rot.reshape(seq_count, stretch_len, model_width),
            values.reshape(seq_count, stretch_len, model_width),
            lengths,
            positions,
            score_scale,
        )
        attn_low = attended.reshape(-1, model_width).astype(jnp.bfloat16)
        middle = inputs + jnp.dot(attn_low, mat_out, preferred_element_type=jnp.float32)
        rms_two = lax.rsqrt(jnp.mean(middle * middle, axis=-1, keepdims=True) + EPSILON)
        normed_two = (middle * rms_two * gain_two.astype(jnp.float32)).astype(jnp.bfloat16)
        gate_pre = jnp.dot(normed_two, mat_gate, preferred_element_type=jnp.float32)
        up_pre = jnp.dot(normed_two, mat_up, preferred_element_type=jnp.float32)
        hidden = (jax.nn.silu(gate_pre) * up_pre).astype(jnp.bfloat16)
        result = middle + jnp.dot(hidden, mat_down, preferred_element_type=jnp.float32)
        kept = (
            inputs,
            rms_one,
            normed,
            query_rot,
            key_rot,
            values,
            attended,
            attn_low,
            log_total,
            middle,
            rms_two,
            normed_two,
            gate_pre,
            up_pre,
            hidden,
        )
        return (result, values, kept)

    def backward_layer(grad_in, params, kept, first_grad):
        gain_one, mat_qkv, mat_out, gain_two, mat_gate, mat_up, mat_down = params
        (
            inputs,
            rms_one,
            normed,
            query_rot,
            key_rot,
            values,
            attended,
            attn_low,
            log_total,
            middle,
            rms_two,
            normed_two,
            gate_pre,
            up_pre,
            hidden,
        ) = kept
        grad_low = grad_in.astype(jnp.bfloat16)
        grad_down = jnp.einsum("nf,nd->fd", hidden, grad_low, preferred_element_type=jnp.float32)
        grad_hidden = jnp.einsum(
            "nd,fd->nf", grad_low, mat_down, preferred_element_type=jnp.float32
        )
        sigma = jax.nn.sigmoid(gate_pre)
        grad_gate_pre = (grad_hidden * up_pre * sigma * (1.0 + gate_pre * (1.0 - sigma))).astype(
            jnp.bfloat16
        )
        grad_up_pre = (grad_hidden * gate_pre * sigma).astype(jnp.bfloat16)
        grad_gate = jnp.einsum(
            "nd,nf->df", normed_two, grad_gate_pre, preferred_element_type=jnp.float32
        )
        grad_up = jnp.einsum(
            "nd,nf->df", normed_two, grad_up_pre, preferred_element_type=jnp.float32
        )
        grad_normed_two = jnp.einsum(
            "nf,df->nd", grad_gate_pre, mat_gate, preferred_element_type=jnp.float32
        ) + jnp.einsum("nf,df->nd", grad_up_pre, mat_up, preferred_element_type=jnp.float32)
        scaled_two = middle * rms_two
        grad_gain_two = jnp.sum(grad_normed_two * scaled_two, axis=0)
        weighted_two = grad_normed_two * gain_two.astype(jnp.float32)
        grad_middle = grad_in + rms_two * (
            weighted_two - scaled_two * jnp.mean(weighted_two * scaled_two, axis=-1, keepdims=True)
        )
        grad_attn = grad_middle.astype(jnp.bfloat16)
        grad_out_mat = jnp.einsum(
            "nd,ne->de", attn_low, grad_attn, preferred_element_type=jnp.float32
        )
        grad_attended = jnp.einsum(
            "ne,de->nd", grad_attn, mat_out, preferred_element_type=jnp.float32
        ).astype(jnp.bfloat16)
        grad_heads = heads_of(grad_attended)
        delta_rows = jnp.transpose(
            jnp.sum(grad_heads.astype(jnp.float32) * attended, axis=-1), (0, 2, 1)
        )
        grad_query, grad_key, grad_value = attend_back_gathered(
            query_rot,
            key_rot,
            heads_of(values),
            query_rot.reshape(seq_count, stretch_len, model_width),
            key_rot.reshape(seq_count, stretch_len, model_width),
            values.reshape(seq_count, stretch_len, model_width),
            grad_heads,
            grad_attended.reshape(seq_count, stretch_len, model_width),
            log_total,
            delta_rows,
            lengths,
            positions,
            score_scale,
        )
        grad_query_raw = rotate(grad_query, cosine, -sine_table).reshape(-1, model_width)
        grad_key_raw = rotate(grad_key, cosine, -sine_table).reshape(-1, model_width)
        grad_value_flat = grad_value.reshape(-1, model_width)
        if first_grad is None:
            grad_value_raw = 0.5 * grad_value_flat
            passed = 0.5 * grad_value_flat
        else:
            grad_value_raw = grad_value_flat + first_grad
            passed = None
        grad_proj = jnp.concatenate([grad_query_raw, grad_key_raw, grad_value_raw], axis=-1).astype(
            jnp.bfloat16
        )
        grad_qkv = jnp.einsum("nd,ne->de", normed, grad_proj, preferred_element_type=jnp.float32)
        grad_normed = jnp.einsum(
            "ne,de->nd", grad_proj, mat_qkv, preferred_element_type=jnp.float32
        )
        scaled_one = inputs * rms_one
        grad_gain_one = jnp.sum(grad_normed * scaled_one, axis=0)
        weighted_one = grad_normed * gain_one.astype(jnp.float32)
        grad_inputs = grad_middle + rms_one * (
            weighted_one - scaled_one * jnp.mean(weighted_one * scaled_one, axis=-1, keepdims=True)
        )
        return (
            grad_inputs,
            (grad_gain_one, grad_qkv, grad_out_mat, grad_gain_two, grad_gate, grad_up, grad_down),
            passed,
        )

    def reduce_layer(grads):
        return (
            lax.psum_scatter(grads[0], ("grp", "seq"), scatter_dimension=0, tiled=True),
            lax.psum_scatter(grads[1], ("grp", "seq"), scatter_dimension=0, tiled=True),
            lax.psum_scatter(grads[2], ("grp", "seq"), scatter_dimension=0, tiled=True),
            lax.psum_scatter(grads[3], ("grp", "seq"), scatter_dimension=0, tiled=True),
            lax.psum_scatter(grads[4], ("grp", "seq"), scatter_dimension=0, tiled=True),
            lax.psum_scatter(grads[5], ("grp", "seq"), scatter_dimension=0, tiled=True),
            lax.psum_scatter(grads[6], ("grp", "seq"), scatter_dimension=0, tiled=True),
        )

    state_zero = tokens.astype(jnp.float32).reshape(-1, model_width)
    params_one = gather_layer(0)
    state_one, first_value, kept_one = forward_layer(state_zero, params_one, None)
    params_two = gather_layer(1)
    state_two, unused_value, kept_two = forward_layer(state_one, params_two, first_value)
    layer_out = state_two.astype(jnp.bfloat16).reshape(seq_count, stretch_len, model_width)
    valid_mask = (positions[None, :] < lengths[:, None]).astype(jnp.float32)
    grad_state = (cotangent.astype(jnp.float32) * valid_mask[:, :, None]).reshape(-1, model_width)
    params_two = gather_again(1)
    grad_mid, grads_two, passed = backward_layer(grad_state, params_two, kept_two, None)
    shards_two = reduce_layer(grads_two)
    params_one = gather_again(0)
    grad_inputs, grads_one, unused_grad = backward_layer(grad_mid, params_one, kept_one, passed)
    shards_one = reduce_layer(grads_one)
    stacked = tuple((jnp.stack([shards_one[member], shards_two[member]]) for member in range(7)))
    input_grad = grad_inputs.reshape(seq_count, stretch_len, model_width)
    return (
        layer_out,
        input_grad,
        stacked[0],
        stacked[1],
        stacked[2],
        stacked[3],
        stacked[4],
        stacked[5],
        stacked[6],
    )


def body_planes(
    tokens, seq_lens, norm_attn, w_qkv, w_out, norm_ffn, w_gate, w_up, w_down, cotangent
):
    seqs, stretch, width = tokens.shape
    y, c, z, x = (lax.axis_index(axis) for axis in ALL)
    lane = c * 4 + y * 2 + x
    where = jnp.stack([y, c, z, x]).astype(jnp.int32)
    rows = seqs * stretch
    ffn = w_gate.shape[2]

    def exchange(field):
        return lax.all_to_all(field, PLANE, 0, 0, tiled=True)

    def exchange_z(field):
        shape = field.shape
        moved = lax.all_to_all(field.reshape((4, 2) + shape[1:]), "z", 0, 0, tiled=True)
        return moved.reshape(shape)

    def cut_blocks(field):
        field = field.reshape(seqs, 2, 8, 16, width)
        return jnp.transpose(field, (2, 0, 1, 3, 4))

    def join_stripes(field):
        return jnp.transpose(field, (1, 0, 2, 3, 4)).reshape(rows, width)

    def cut_stripes(field):
        return jnp.transpose(field.reshape(seqs, 8, 2, 16, width), (1, 0, 2, 3, 4))

    def join_blocks(field):
        return jnp.transpose(field, (1, 2, 0, 3, 4)).reshape(seqs, stretch, width)

    def gather_all(shard):
        return lax.all_gather(shard, ALL, axis=0, tiled=True)

    def gain_shard(layer):
        gain = jnp.stack([norm_attn[layer], norm_ffn[layer]], axis=1)
        return jnp.pad(gain, ((0, 0), (0, 126)))

    def gains(columns):
        return jnp.transpose(columns)[:2].astype(F32)

    def gather_ffn(layer, *after):
        cuts = [w_gate[layer], w_up[layer], pack(w_down[layer])]
        if layer == 0:
            cuts.append(w_out[layer])
        shard = jnp.concatenate(cuts, axis=1)
        if after:
            shard, *_ = fence(shard, *after)
        gathered = gather_all(shard)
        packed = gathered[:, 2 * ffn : 2 * ffn + 3 * width]
        w_d = unpack(packed.reshape(32, -1, 3 * width)).reshape(-1, width)
        return gathered, w_d

    def pack(rows_of_down):
        tall = w_qkv.shape[1]
        spare = 3 * tall - rows_of_down.shape[-2]
        lead = [(0, 0)] * (rows_of_down.ndim - 2)
        padded = jnp.pad(rows_of_down, lead + [(0, spare), (0, 0)])
        cuts = [padded[..., n * tall : n * tall + tall, :] for n in range(3)]
        return jnp.concatenate(cuts, axis=-1)

    def unpack(packed):
        cols = packed.shape[-1] // 3
        cuts = [packed[..., n * cols : n * cols + cols] for n in range(3)]
        return jnp.concatenate(cuts, axis=-2)[..., : w_down.shape[1], :]

    def gather_first():
        shard = w_qkv[0]
        first = jnp.concatenate([shard[:, :width], gain_shard(0)], axis=1)
        w_q = gather_z_first(where, first, "x", "y")
        w_k = gather_z_first(where, shard[:, width : 2 * width], "y", "x")
        w_v = gather_z_first(where, shard[:, 2 * width :], "x", "y")
        weights = [(w_q, 0), (w_k, 0), (w_v, 0)]
        return weights, [w_q[:, :width], w_k, w_v], gains(w_q[:, width:])

    def second_weights(whole):
        weights = [(whole, 0), (whole, 1), (whole, 2)]
        turned = [whole[:, : 3 * width]]
        return weights, turned, (whole, 3 * width), gains(whole[:, 4 * width :])

    here = z * 2 + x
    routes = []
    for k in range(8):
        route = []
        for sy in range(2):
            for sc in range(2):
                for sb in range(8):
                    to = sb ^ k
                    target = (((to >> 1) & 1) * 2 + (to >> 2)) * 4 + 2 * sc + sy
                    route.append(((sy * 2 + sc) * 8 + sb, target * 2 + (to & 1)))
        routes.append(route)
    lengths = lax.ppermute(seq_lens, ALL, routes[0])[0]
    length = [lengths[n : n + 1] for n in range(2)]
    slots = stretch * 8
    half_dim = width // HEADS // 2
    freqs = 10000.0 ** (-jnp.arange(half_dim, dtype=F32) / half_dim)
    angle = jnp.arange(slots, dtype=F32)[:, None] * freqs[None, :]
    cosine, sine = jnp.cos(angle), jnp.sin(angle)
    cosine = jnp.concatenate([cosine] * 4, axis=1)
    sine = jnp.concatenate([-sine, sine] * 2, axis=1)

    def mine(table):
        own = lax.dynamic_index_in_dim(
            table.reshape(slots // 128, 8, 16, 128), lane, 1, keepdims=False
        )
        return own.reshape(stretch, 128)

    my_cos, my_sin = mine(cosine), mine(sine)
    step = jnp.arange(stretch, dtype=jnp.int32)
    places = (step // 16) * 128 + lane * 16 + step % 16
    valid = (places[None, :] < lengths[:, None]).astype(F32).reshape(rows, 1)

    shape = (8, 3, stretch // 16, 16, 128)

    def project(inputs, weights, gain, first_value):
        return project_qkv(inputs, gain, weights, my_cos, my_sin, first_value)

    def near(field):
        return swap(field, "c")

    def norm_back(grad_normed, source, gain):
        rms = lax.rsqrt(jnp.mean(source * source, axis=-1, keepdims=True) + EPSILON)
        scaled = source * rms
        weighted = grad_normed * gain
        return rms * (weighted - scaled * jnp.mean(weighted * scaled, axis=-1, keepdims=True))

    def blocks_of(grad):
        return grad.reshape(4, 2, 2, 32, grad.shape[-1])

    def dots(grads, weights):
        total = None
        for grad, weight in zip(grads, weights):
            part = lax.dot_general(grad, weight, NT, preferred_element_type=F32)
            total = part if total is None else total + part
        return total

    def attn_grads(one, att, proj, mid, places):
        return weight_grads(core, [(one, [proj]), (att, [mid])], places)

    def sum_z(grad):
        flat = grad.reshape(4, 128, grad.shape[-1])
        flat = lax.psum_scatter(flat, "z", scatter_dimension=0, tiled=True)
        return flat.reshape(2, 2, 32, grad.shape[-1])

    def pair_sums(summed):
        half = summed.shape[-1] // 2
        return [
            Reduction(summed[..., :half], "xy", "yx"),
            Reduction(summed[..., half:], "yx", "yx"),
        ]

    def ffn_grads(two, gates, ups, hid, low):
        half = ffn // 2
        parts = [[(0, half, 0, 0), (half, half, 0, half)]]
        parts.append([(0, half, 0, ffn), (half, half, 0, ffn + half)])
        (grad,) = weight_grads(
            core, [(two, [gates, ups]), (hid, [low])], [parts, [[(0, width, 0, 2 * ffn)]]]
        )
        return grad

    def backward_layer(grad_in, w_attn, w_ffn, kept, passed, upper, beside):
        w_turned, w_o, gain = w_attn
        w_o = w_o[0][:, w_o[1] : w_o[1] + width]
        w_gu, w_d = w_ffn
        inputs, normed, pieces, attended, lse, buffers = kept
        attn_low, middle, normed_two, gate, up, hidden = buffers
        inputs = jnp.concatenate(inputs).astype(F32)
        normed = jnp.concatenate(normed)
        gate, up = gate.astype(F32), up.astype(F32)
        grad_low = grad_in.astype(BF)
        low = (grad_low, near(grad_low))
        hid = (hidden, near(hidden))
        two = (normed_two, near(normed_two))
        att = (attn_low, near(attn_low))
        one = (normed, near(normed))
        grad_hidden = lax.dot_general(grad_low, w_d, NT, preferred_element_type=F32)
        sigma = jax.nn.sigmoid(gate)
        grad_gate = (grad_hidden * up * sigma * (1.0 + gate * (1.0 - sigma))).astype(BF)
        grad_up = (grad_hidden * gate * sigma).astype(BF)
        gates = (grad_gate, near(grad_gate))
        ups = (grad_up, near(grad_up))
        if upper is None:
            beside, grad_gate, grad_up, *gates = fence(beside, grad_gate, grad_up, *gates)
        summed = ffn_grads(two, gates, ups, hid, low)
        summed, grad_gate, grad_up = fence(summed, grad_gate, grad_up)
        summed = sum_z(summed)
        grad_normed = dots([grad_gate, grad_up], [w_gu[:, :ffn], w_gu[:, ffn : 2 * ffn]])
        grad_middle = grad_in + norm_back(grad_normed, middle, gain[1])
        grad_attn = grad_middle.astype(BF)
        mid = (grad_attn, near(grad_attn))
        grad_o = lax.dot_general(grad_attn, w_o, NT, preferred_element_type=F32).astype(BF)
        grad_o = jnp.transpose(grad_o.reshape(rows, 8, 128), (1, 0, 2))
        if upper is not None:
            grad_o, beside = fence(grad_o, beside)

        grad_o = exchange(grad_o)
        ffn_pair = []
        if upper is not None:
            upper_ffn, upper_attn = upper
            upper_ffn, grad_o = fence(upper_ffn, grad_o)
            ffn_pair = pair_sums(upper_ffn)
            (grad_o,) = send_all(ffn_pair, grad_o)
        grad_o = grad_o.reshape(8, 2, stretch // 16, 16, 128)
        cos_sin = (cosine, sine)
        parts_a, pass_a = attend_back(
            length[0], pieces[0], attended[0], grad_o[:, 0], lse[0], *cos_sin, passed and passed[0]
        )
        parts_a, grad_b = fence(parts_a, grad_o[:, 1])
        if ffn_pair:
            parts_a, grad_b = add_all(ffn_pair, parts_a, grad_b)
            parts_a, grad_b = send_all(ffn_pair, parts_a, grad_b)
        moved_a = exchange(parts_a.reshape(8, 3, stretch, 128))
        parts_b, pass_b = attend_back(
            length[1], pieces[1], attended[1], grad_b, lse[1], *cos_sin, passed and passed[1]
        )
        moved_a, parts_b = fence(moved_a, parts_b)
        moved_b = exchange(parts_b.reshape(8, 3, stretch, 128))
        attn_pair = []
        if ffn_pair:
            (moved_b,) = add_all(ffn_pair, moved_b)
            upper_attn, moved_b = fence(upper_attn, moved_b)
            attn_pair = pair_sums(upper_attn)
            (moved_b,) = send_all(attn_pair, moved_b)
        grad_proj = jnp.concatenate(
            [
                jnp.transpose(moved, (2, 1, 0, 3)).reshape(stretch, 3 * width)
                for moved in (moved_a, moved_b)
            ]
        )
        proj = (grad_proj, near(grad_proj))
        cuts, at = [], 0
        for weight in w_turned:
            cuts.append(grad_proj[:, at : at + weight.shape[1]])
            at += weight.shape[1]
        grad_normed = dots(cuts, w_turned)
        grad = grad_middle + norm_back(grad_normed, inputs, gain[0])
        todo = one + att + proj + mid
        return grad, summed, todo, (pass_a, pass_b), ffn_pair, attn_pair, beside

    core = c.astype(jnp.int32).reshape(1)
    ffn_one = gather_ffn(0)
    state = join_stripes(exchange_z(exchange(cut_blocks(tokens))))
    in_one = (state[:stretch], state[stretch:])
    qkv_one, turned_one, gain_one = gather_first()
    out_one = (ffn_one[0], 2 * ffn + 3 * width)

    shard = jnp.concatenate([w_qkv[1], w_out[1], gain_shard(1)], axis=1)
    parts_a, normed_a = project(in_one[0], qkv_one, gain_one, None)
    pieces_a = exchange(parts_a)
    parts_b, normed_b = project(in_one[1], qkv_one, gain_one, None)
    shard, pieces_a, sent_b = fence(shard, pieces_a, parts_b)
    hops = [hop(shard, k) for k in (1, 2, 3)]
    pieces_a = pieces_a.reshape(shape)
    pieces_b = exchange(sent_b)
    attended_a, lse_a = attend(length[0], pieces_a)
    attended_a, pieces_b, ffn_one, *hops = fence(attended_a, pieces_b, ffn_one, *hops)
    out_one = (ffn_one[0], out_one[1])
    stack = jnp.stack([shard] + hops)
    cut = stack.shape[2] // 256 * 128
    stacks = [stack[..., :cut], stack[..., cut:]]
    besides = [swap(stacks[0], "x"), swap(stacks[1], "y")]
    pieces_b = pieces_b.reshape(shape)
    low_a = exchange(attended_a.reshape(8, stretch, 128))
    attended_b, lse_b = attend(length[1], pieces_b)
    ffn_two = gather_ffn(1, attended_a)
    low_a, sent_b, besides = fence(low_a, attended_b, besides)
    rings = [
        [((0, 0), stacks[0]), ((0, 1), besides[0])],
        [((0, 0), stacks[1]), ((1, 0), besides[1])],
    ]
    for axis, ring in zip(("y", "x"), rings):
        for (dy, dx), piece in list(ring):
            place = (1, dx) if axis == "y" else (dy, 1)
            ring.append((place, swap(piece, axis)))
    low_b = exchange(sent_b.reshape(8, stretch, 128))
    rest = (ffn_one[0], ffn_one[1], gain_one, ffn)
    result_a, buffers = forward_ffn(
        low_a, in_one[0].astype(F32), out_one, *rest, None, 0, rows
    )
    held = fence(result_a, *[piece for ring in rings for _, piece in ring])
    result_a = held[0]
    rings = [
        [(place, piece) for (place, _), piece in zip(ring, held[1 + 4 * n : 5 + 4 * n])]
        for n, ring in enumerate(rings)
    ]
    rings = [
        [
            ((dy, dc, dx), swap(piece, "c") if dc else piece)
            for (dy, dx), piece in ring
            for dc in (0, 1)
        ]
        for ring in rings
    ]
    relative = [[place for place, _ in ring] for ring in rings]
    sides = [[piece for _, piece in ring] for ring in rings]
    whole = assemble(where, sides, relative)
    kept_one = (in_one, (normed_a, normed_b), (pieces_a, pieces_b), (attended_a, attended_b))
    kept_one += ((lse_a, lse_b),)
    qkv_two, turned_two, out_two, gain_two = second_weights(whole)

    next_a, normed_a = project(result_a, qkv_two, gain_two, parts_a)
    next_a, low_b = fence(next_a, low_b)
    pieces_a = exchange(next_a)
    result_b, buffers = forward_ffn(
        low_b, in_one[1].astype(F32), out_one, *rest, buffers, stretch, rows
    )
    kept_one += (buffers,)
    in_two = (result_a, result_b)
    next_b, normed_b = project(result_b, qkv_two, gain_two, parts_b)
    pieces_a, sent_b = fence(pieces_a, next_b)
    pieces_a = pieces_a.reshape(shape)
    pieces_b = exchange(sent_b)
    attended_a, lse_a = attend(length[0], pieces_a)
    attended_a, pieces_b, other = fence(attended_a, pieces_b, cut_blocks(cotangent))
    other = [
        lax.ppermute(lax.dynamic_index_in_dim(other, here ^ k, 0, keepdims=False), ALL, routes[k])
        for k in range(8)
    ]
    pieces_b = pieces_b.reshape(shape)
    low_a = exchange(attended_a.reshape(8, stretch, 128))
    attended_b, lse_b = attend(length[1], pieces_b)
    low_a, sent_b, *other = fence(low_a, attended_b, *other)
    low_b = exchange(sent_b.reshape(8, stretch, 128))
    rest = (ffn_two[0], ffn_two[1], gain_two, ffn)
    final_a, buffers = forward_ffn(low_a, result_a, out_two, *rest, None, 0, rows)
    final_a, low_b = fence(final_a, low_b)
    moved_a = exchange_z(final_a.astype(BF).reshape(8, 2, 16, width))
    final_b, buffers = forward_ffn(low_b, result_b, out_two, *rest, buffers, stretch, rows)
    kept_two = (in_two, (normed_a, normed_b), (pieces_a, pieces_b), (attended_a, attended_b))
    kept_two += ((lse_a, lse_b), buffers)
    moved_a, final_b, *other = fence(moved_a, final_b, *other)
    moved_b = exchange_z(final_b.astype(BF).reshape(8, 2, 16, width))
    grad = jnp.zeros((8, seqs, 2, 16, width), BF)
    for k in range(8):
        grad = lax.dynamic_update_index_in_dim(grad, other[k], lane ^ k, 0)
    grad = join_stripes(grad).astype(F32) * valid
    layer_out = jnp.stack([moved_a, moved_b], axis=1)
    grad, ffn_two_sum, todo, passed, _, _, layer_out = backward_layer(
        grad, (turned_two, out_two, gain_two), ffn_two, kept_two, None, None, layer_out
    )
    grad, *todo = fence(grad, *todo)
    todo = [tuple(todo[n : n + 2]) for n in (0, 2, 4, 6)]
    (attn_two,) = attn_grads(*todo, [[[(0, 3 * width, 0, 0)]], [[(0, width, 0, 3 * width)]]])
    attn_two, grad, layer_out = fence(attn_two, grad, layer_out)
    attn_two = sum_z(attn_two)
    layer_out = exchange(layer_out)
    grad, ffn_one_sum, todo, _, ffn_pair_two, attn_pair_two, layer_out = backward_layer(
        grad,
        (turned_one, out_one, gain_one),
        ffn_one,
        kept_one,
        passed,
        (ffn_two_sum, attn_two),
        layer_out,
    )
    layer_out = join_blocks(layer_out)
    grad, *todo = fence(grad, *todo)
    todo = [tuple(todo[n : n + 2]) for n in (0, 2, 4, 6)]
    places = [[[(0, 2 * width, 0, 0), (2 * width, width, 1, 0)]], [[(0, width, 1, width)]]]
    attn_pair_one = [
        Reduction(part.reshape(4, 2, 2, 32, -1), order)
        for part, order in zip(attn_grads(*todo, places), ("yxz", "xyz"))
    ]
    (grad,) = send_all(attn_pair_one, grad)
    input_grad = cut_stripes(grad.astype(BF))
    add_all(attn_pair_two, *[r.partial for r in attn_pair_one])
    send_all(attn_pair_two)
    add_all(attn_pair_one, *[r.partial for r in attn_pair_two])
    send_all(attn_pair_one)
    mark = [r.partial for r in attn_pair_one]
    ffn_one_sum, input_grad, *mark = fence(ffn_one_sum, input_grad, *mark)
    ffn_pair_one = pair_sums(ffn_one_sum)
    (input_grad,) = send_all(ffn_pair_one, input_grad)
    input_grad = exchange_z(input_grad)
    add_all(attn_pair_one)
    send_all(attn_pair_one)
    (input_grad,) = add_all(ffn_pair_one, input_grad)
    (input_grad,) = send_all(ffn_pair_one, input_grad)
    input_grad = exchange(input_grad)
    add_all(attn_pair_two + ffn_pair_one)
    add_all(attn_pair_one)
    input_grad = join_blocks(input_grad).astype(F32)

    out_grad, qkv_grad, gate_grad, up_grad, down_grad = [], [], [], [], []
    for attn_pair, ffn_pair in ((attn_pair_one, ffn_pair_one), (attn_pair_two, ffn_pair_two)):
        field = jnp.concatenate([r.partial for r in attn_pair], axis=1)
        qkv_grad.append(field[:, : 3 * width])
        out_grad.append(field[:, 3 * width :])
        field = jnp.concatenate([r.partial for r in ffn_pair], axis=1)
        gate_grad.append(field[:, :ffn])
        up_grad.append(field[:, ffn : 2 * ffn])
        down_grad.append(unpack(field[:, 2 * ffn :]))

    def gain_grad(pairs, gain):
        total = sum(jnp.sum(w.astype(F32) * grad, axis=1) for w, grad in pairs)
        return total / gain.astype(F32)

    attn_gain = [gain_grad([(w_qkv[n], qkv_grad[n])], norm_attn[n]) for n in range(2)]
    ffn_gain = [
        gain_grad([(w_gate[n], gate_grad[n]), (w_up[n], up_grad[n])], norm_ffn[n])
        for n in range(2)
    ]
    return (
        layer_out,
        input_grad,
        jnp.stack(attn_gain),
        jnp.stack(qkv_grad),
        jnp.stack(out_grad),
        jnp.stack(ffn_gain),
        jnp.stack(gate_grad),
        jnp.stack(up_grad),
        jnp.stack(down_grad),
    )


IN_SPECS = (
    ("grp", "seq", None),
    ("grp", None),
    (None, ("grp", "seq")),
    (None, ("grp", "seq"), None),
    (None, ("grp", "seq"), None),
    (None, ("grp", "seq")),
    (None, ("grp", "seq"), None),
    (None, ("grp", "seq"), None),
    (None, ("grp", "seq"), None),
    ("grp", "seq", None),
)
OUT_SPECS = (
    ("grp", "seq", None),
    ("grp", "seq", None),
    (None, ("grp", "seq")),
    (None, ("grp", "seq"), None),
    (None, ("grp", "seq"), None),
    (None, ("grp", "seq")),
    (None, ("grp", "seq"), None),
    (None, ("grp", "seq"), None),
    (None, ("grp", "seq"), None),
)


def solution(mesh):
    if mesh.shape["grp"] == 4 and mesh.shape["seq"] == 8:
        split = Mesh(mesh.devices.reshape(2, 2, 4, 2), ALL)
        names = {"grp": ("y", "c"), "seq": ("z", "x"), ("grp", "seq"): ALL, None: None}
        program = body_planes
    else:
        split = mesh
        names = {"grp": "grp", "seq": "seq", ("grp", "seq"): ("grp", "seq"), None: None}
        program = body

    def specs(table):
        return tuple(P(*(names[name] for name in row)) for row in table)

    return jax.shard_map(
        program,
        mesh=split,
        in_specs=specs(IN_SPECS),
        out_specs=specs(OUT_SPECS),
        check_vma=False,
    )
```

```python
import jax
import jax.numpy as jnp
from jax import lax
from jax.experimental import pallas as pl
from jax.experimental.pallas import tpu as pltpu
from jax.sharding import Mesh
from jax.sharding import PartitionSpec as P

HEADS = 16
EPSILON = 1e-06
NEGATIVE = -1e30
PRECISE = lax.Precision.HIGHEST
BF = jnp.bfloat16
F32 = jnp.float32
ALL = ("y", "c", "z", "x")
PLANE = ("c", "y", "x")
VMEM_BYTES = 50 * 1024 * 1024
ANY = pl.BlockSpec(memory_space=pl.ANY)
SMEM = pl.BlockSpec(memory_space=pltpu.SMEM)
NT = (((1,), (1,)), ((), ()))
TN = (((0,), (0,)), ((), ()))


def params(**more):
    return pltpu.CompilerParams(vmem_limit_bytes=VMEM_BYTES, **more)


def assemble(where, sides, relatives):
    rows = sides[0][0].shape[1]
    widths = [side[0].shape[2] for side in sides]
    kind = sides[0][0].dtype
    flat = [piece for side in sides for piece in side]
    count = len(flat)

    def kernel(where_ref, *rest):
        ins, out, sems = rest[:count], rest[count], rest[-1]
        y, c, z, x = (where_ref[n] for n in range(4))
        copies, puts = [], []
        n, first = 0, 0
        for side, relative in enumerate(relatives):
            held = rest[count + 1 + side]
            lanes = pl.ds(first, widths[side])
            first += widths[side]
            for at, (dy, dc, dx) in enumerate(relative):
                for dz in range(4):
                    spot = held.at[at, dz]
                    target = out.at[y ^ dy, c ^ dc, z ^ dz, x ^ dx, :, lanes]
                    copies.append(pltpu.make_async_copy(ins[n].at[dz], spot, sems.at[0, n, dz]))
                    puts.append(pltpu.make_async_copy(spot, target, sems.at[1, n, dz]))
                n += 1
        for copy in copies:
            copy.start()
        for copy, put in zip(copies, puts):
            copy.wait()
            put.start()
        for put in puts:
            put.wait()

    out = pl.pallas_call(
        kernel,
        in_specs=[SMEM] + [ANY] * count,
        out_specs=ANY,
        out_shape=jax.ShapeDtypeStruct((2, 2, 4, 2, rows, sum(widths)), kind),
        scratch_shapes=[
            pltpu.VMEM((len(side), 4, rows, width), kind) for side, width in zip(sides, widths)
        ]
        + [pltpu.SemaphoreType.DMA((2, count, 4))],
        compiler_params=params(),
        name="assemble",
    )(where, *flat)
    return out.reshape(-1, sum(widths))


def swap(value, axis):
    return lax.ppermute(value, axis, [(0, 1), (1, 0)])


def hop(value, offset):
    return lax.ppermute(value, "z", [(i, i ^ offset) for i in range(4)])


def gather_z_first(where, shard, first, second):
    stack = jnp.stack([shard] + [hop(shard, k) for k in (1, 2, 3)])
    near = swap(stack, first)
    ring = [((0, 0), stack), ((1, 0), near)]
    ring += [((0, 1), swap(stack, second)), ((1, 1), swap(near, second))]
    pieces, relative = [], []
    for (one, two), piece in ring:
        moved = {first: one, second: two}
        for dc, held in ((0, piece), (1, swap(piece, "c"))):
            pieces.append(held)
            relative.append((moved["y"], dc, moved["x"]))
    return assemble(where, [pieces], [relative])


def fence(*values):
    return lax.optimization_barrier(values)


class Reduction:
    def __init__(self, partial, order, names="zyx"):
        self.partial = partial
        self.order = order
        self.names = list(names)
        self.moved = None

    def send(self):
        axis, self.order = self.order[0], self.order[1:]
        dim = self.names.index(axis)
        self.names.pop(dim)
        here = lax.axis_index(axis)

        def block(slot):
            return lax.dynamic_index_in_dim(self.partial, slot, dim, keepdims=False)

        if axis == "z":
            self.moved = [hop(block(here ^ k), k) for k in (1, 2, 3)]
        else:
            self.moved = [swap(block(1 - here), axis)]
        self.partial = block(here)

    def add(self):
        total = self.partial.astype(F32)
        for part in self.moved:
            total = total + part.astype(F32)
        self.moved = None
        self.partial = total.astype(BF) if self.order else total


def send_all(reductions, *others):
    reductions = [r for r in reductions if r.order]
    held = fence(*[r.partial for r in reductions], *others)
    for reduction, partial in zip(reductions, held):
        reduction.partial = partial
        reduction.send()
    return held[len(reductions) :]


def add_all(reductions, *others):
    reductions = [r for r in reductions if r.moved is not None]
    flat = [part for r in reductions for part in r.moved]
    held = fence(*flat, *others)
    at = 0
    for reduction in reductions:
        count = len(reduction.moved)
        reduction.moved = list(held[at : at + count])
        at += count
        reduction.add()
    held = fence(*[r.partial for r in reductions], *held[at:])
    for reduction, partial in zip(reductions, held):
        reduction.partial = partial
    return held[len(reductions) :]


def turn(field, cosine, signed_sine):
    lane = lax.broadcasted_iota(jnp.int32, field.shape, 1)
    other = jnp.where(
        lane % 64 < 32, pltpu.roll(field, 96, axis=1), pltpu.roll(field, 32, axis=1)
    )
    return field * cosine + other * signed_sine


def project_qkv(inputs, gain, weights, cosine, signed_sine, first_value):
    rows, width = inputs.shape
    devices = width // 128

    def kernel(in_ref, gain_ref, w_q_ref, w_k_ref, w_v_ref, cos_ref, sin_ref, *rest):
        out_ref, normed_ref = rest[-2:]
        step = pl.program_id(0)

        @pl.when(step == 0)
        def _():
            field = in_ref[...].astype(F32)
            rms = lax.rsqrt(jnp.mean(field * field, axis=1, keepdims=True) + EPSILON)
            normed_ref[...] = (field * rms * gain_ref[0:1, :]).astype(BF)

        def product(w_ref):
            return jnp.dot(normed_ref[...], w_ref[...], preferred_element_type=F32)

        def turned(w_ref):
            field = product(w_ref)
            for n in range(devices):
                part = field[:, 128 * n : 128 * n + 128]
                out_ref[n, 0] = turn(part, cos_ref[...], sin_ref[...]).astype(BF)

        @pl.when(step == 0)
        def _():
            turned(w_q_ref)

        @pl.when(step == 1)
        def _():
            turned(w_k_ref)

        @pl.when(step == 2)
        def _():
            field = product(w_v_ref)
            for n in range(devices):
                part = field[:, 128 * n : 128 * n + 128]
                if first_value is not None:
                    part = 0.5 * part + 0.5 * rest[0][n, 0].astype(F32)
                out_ref[n, 0] = part.astype(BF)

    whole = lambda step: (0, 0)
    in_specs = [pl.BlockSpec((rows, width), whole), pl.BlockSpec((2, width), whole)]
    for _, start in weights:
        in_specs.append(pl.BlockSpec((width, width), lambda step, start=start: (0, start)))
    in_specs += [pl.BlockSpec((rows, 128), whole)] * 2
    operands = [inputs, gain] + [array for array, _ in weights] + [cosine, signed_sine]
    if first_value is not None:
        in_specs.append(pl.BlockSpec((devices, 1, rows, 128), lambda step: (0, 2, 0, 0)))
        operands.append(first_value)
    return pl.pallas_call(
        kernel,
        grid=(3,),
        in_specs=in_specs,
        out_specs=[
            pl.BlockSpec((devices, 1, rows, 128), lambda step: (0, step, 0, 0)),
            pl.BlockSpec((rows, width), whole),
        ],
        out_shape=[
            jax.ShapeDtypeStruct((devices, 3, rows, 128), BF),
            jax.ShapeDtypeStruct((rows, width), BF),
        ],
        compiler_params=params(dimension_semantics=("arbitrary",)),
        name="project_qkv",
    )(*operands)


def forward_ffn(low, inputs, w_o, w_gu, w_d, gain, ffn, kept, first_row, total_rows):
    rows, width = inputs.shape
    devices = low.shape[0]
    half = ffn // 2
    w_o, out_column = w_o
    kinds = [
        ((total_rows, width), BF),
        ((total_rows, width), F32),
        ((total_rows, width), BF),
        ((total_rows, ffn), BF),
        ((total_rows, ffn), BF),
        ((total_rows, ffn), BF),
    ]
    count = len(kinds)

    def kernel(low_ref, in_ref, wo_ref, wgu_ref, wd_ref, gain_ref, *refs):
        if kept is not None:
            refs = refs[count:]
        outs, refs = refs[: count + 1], refs[count + 1 :]
        att, wo, wg, wu, wd, mid, norm, gates, ups, hids, result, sems, out_sems = refs
        spans = [slice(0, half), slice(half, ffn)]
        loads = [
            pltpu.make_async_copy(
                low_ref.at[n], att.at[:, pl.ds(128 * n, 128)], sems.at[n]
            )
            for n in range(devices)
        ]
        loads.append(
            pltpu.make_async_copy(wo_ref.at[:, pl.ds(out_column, width)], wo, sems.at[devices])
        )
        late = []
        for n in range(2):
            at = devices + 1 + 3 * n
            column = pl.ds(n * half, half)
            late.append(
                [
                    pltpu.make_async_copy(wgu_ref.at[:, column], wg.at[n], sems.at[at]),
                    pltpu.make_async_copy(
                        wgu_ref.at[:, pl.ds(ffn + n * half, half)], wu.at[n], sems.at[at + 1]
                    ),
                    pltpu.make_async_copy(wd_ref.at[column], wd.at[n], sems.at[at + 2]),
                ]
            )
        for copy in loads + late[0] + late[1]:
            copy.start()
        puts = []

        def put(source, target, index):
            copy = pltpu.make_async_copy(source, target, out_sems.at[len(puts)])
            copy.start()
            puts.append(copy)

        own = pl.ds(first_row, rows)
        for copy in loads:
            copy.wait()
        put(att, outs[0].at[own], 0)
        middle = in_ref[...] + jnp.dot(att[...], wo[...], preferred_element_type=F32)
        mid[...] = middle
        put(mid, outs[1].at[own], 1)
        rms = lax.rsqrt(jnp.mean(middle * middle, axis=1, keepdims=True) + EPSILON)
        normed = (middle * rms * gain_ref[1:2, :]).astype(BF)
        norm[...] = normed
        put(norm, outs[2].at[own], 2)
        total = middle
        for n in range(2):
            late[n][0].wait()
            gate = jnp.dot(norm[...], wg[n], preferred_element_type=F32)
            late[n][1].wait()
            up = jnp.dot(norm[...], wu[n], preferred_element_type=F32)
            hidden = (gate * jax.nn.sigmoid(gate) * up).astype(BF)
            gates[:, spans[n]] = gate.astype(BF)
            ups[:, spans[n]] = up.astype(BF)
            hids[:, spans[n]] = hidden
            late[n][2].wait()
            total = total + jnp.dot(hidden, wd[n], preferred_element_type=F32)
        put(gates, outs[3].at[own], 3)
        put(ups, outs[4].at[own], 4)
        put(hids, outs[5].at[own], 5)
        result[...] = total
        put(result, outs[6], 6)
        for copy in puts:
            copy.wait()

    vmem = pl.BlockSpec(memory_space=pltpu.VMEM)
    operands = [low, inputs, w_o, w_gu, w_d, gain]
    in_specs = [ANY, vmem, ANY, ANY, ANY, vmem]
    aliases = {}
    if kept is not None:
        aliases = {len(operands) + n: n for n in range(count)}
        operands += list(kept)
        in_specs += [ANY] * count
    outs = pl.pallas_call(
        kernel,
        in_specs=in_specs,
        out_specs=[ANY] * (count + 1),
        out_shape=[jax.ShapeDtypeStruct(*kind) for kind in kinds]
        + [jax.ShapeDtypeStruct((rows, width), F32)],
        scratch_shapes=[
            pltpu.VMEM((rows, width), BF),
            pltpu.VMEM((width, width), BF),
            pltpu.VMEM((2, width, half), BF),
            pltpu.VMEM((2, width, half), BF),
            pltpu.VMEM((2, half, width), BF),
            pltpu.VMEM((rows, width), F32),
            pltpu.VMEM((rows, width), BF),
            pltpu.VMEM((rows, ffn), BF),
            pltpu.VMEM((rows, ffn), BF),
            pltpu.VMEM((rows, ffn), BF),
            pltpu.VMEM((rows, width), F32),
            pltpu.SemaphoreType.DMA((devices + 7,)),
            pltpu.SemaphoreType.DMA((count + 1,)),
        ],
        input_output_aliases=aliases,
        compiler_params=params(),
        name="forward_ffn",
    )(*operands)
    return outs[count], outs[:count]


def weight_grads(core, groups, chunks):
    rows = groups[0][0][0].shape[0]
    operands, scratch, plans = [], [], []
    widths, count = {}, 0
    for (left, rights), places in zip(groups, chunks):
        size = left[0].shape[1] // 4
        window = -(-size // 128) * 128
        plan = {"size": size, "window": window, "left": len(operands), "held": len(scratch)}
        operands += list(left)
        scratch.append(pltpu.VMEM((2, 2 * rows, window), BF))
        plan["rights"] = []
        for right, parts in zip(rights, places):
            cols = right[0].shape[1]
            plan["rights"].append((len(operands), len(scratch), parts))
            operands += list(right)
            scratch.append(pltpu.VMEM((2 * rows, cols), BF))
            for _, span, result, at in parts:
                count += 1
                spread = span if size == window else 3 * span
                widths[result] = max(widths.get(result, 0), at + spread)
        plans.append(plan)
    shapes = [(4, 2, 64, widths[n]) for n in range(len(widths))]
    first_stage = len(scratch)
    scratch += [pltpu.VMEM(shape, BF) for shape in shapes]
    scratch += [
        pltpu.SemaphoreType.DMA((len(operands), 2)),
        pltpu.SemaphoreType.DMA((count,)),
    ]
    inputs, results = len(operands), len(shapes)

    def put_thirds(stage, part, total, at, span, size):
        for z in range(4):
            for x in range(2):
                low = z * (size // 4) + x * (size // 8)
                for third in range(3):
                    first, last = low + 32 * third, low + min(32 * third + 32, size // 8)
                    piece = total[first:last]
                    missing = 32 - piece.shape[0]
                    if missing:
                        piece = jnp.concatenate([piece, jnp.zeros((missing, span), F32)])
                    lane = at + third * span
                    stage[z, part, 32 * x : 32 * x + 32, lane : lane + span] = piece.astype(BF)

    def kernel(core_ref, *refs):
        ins, outs, work = refs[:inputs], refs[inputs : inputs + results], refs[inputs + results :]
        stages = work[first_stage : first_stage + results]
        in_sems, out_sems = work[-2:]
        loads = []
        for plan in plans:
            held, size, window = work[plan["held"]], plan["size"], plan["window"]
            slack = window - size
            left = []
            for side in range(2):
                for part in range(2):
                    start = 2 * part * size + core_ref[0] * (size - slack)
                    span = pl.ds(pl.multiple_of(start, 128), window)
                    at = plan["left"] + side
                    left.append(
                        pltpu.make_async_copy(
                            ins[at].at[:, span],
                            held.at[part, pl.ds(side * rows, rows)],
                            in_sems.at[at, part],
                        )
                    )
            rights = []
            for at, spot, _ in plan["rights"]:
                rights.append(
                    [
                        pltpu.make_async_copy(
                            ins[at + side],
                            work[spot].at[pl.ds(side * rows, rows)],
                            in_sems.at[at + side, 0],
                        )
                        for side in range(2)
                    ]
                )
            loads.append((left, rights))
            for copy in left + [copy for pair in rights for copy in pair]:
                copy.start()
        puts = []
        for plan, (left, rights) in zip(plans, loads):
            size, window = plan["size"], plan["window"]
            held = work[plan["held"]]
            for copy in left:
                copy.wait()
            for pair, (_, spot, parts) in zip(rights, plan["rights"]):
                for copy in pair:
                    copy.wait()
                for first, span, result, at in parts:
                    right = work[spot][:, first : first + span]
                    stage = stages[result]
                    wide = span if size == window else 3 * span
                    for part in range(2):
                        total = lax.dot_general(
                            held[part], right, TN, preferred_element_type=F32
                        )
                        if size == window:
                            total = total.astype(BF).reshape(4, size // 4, span)
                            stage[:, part, :, at : at + span] = total
                        else:
                            own = jnp.where(core_ref[0] == 0, total[:size], total[window - size :])
                            put_thirds(stage, part, own, at, span, size)
                    lanes = pl.ds(at, wide)
                    put = pltpu.make_async_copy(
                        stage.at[:, :, :, lanes],
                        outs[result].at[:, :, :, lanes],
                        out_sems.at[len(puts)],
                    )
                    put.start()
                    puts.append(put)
        for put in puts:
            put.wait()

    return pl.pallas_call(
        kernel,
        in_specs=[SMEM] + [ANY] * inputs,
        out_specs=[ANY] * results,
        out_shape=[jax.ShapeDtypeStruct(shape, BF) for shape in shapes],
        scratch_shapes=scratch,
        compiler_params=params(),
        name="weight_grads",
    )(core, *operands)


def rows_of(block):
    return block.reshape(-1, 128)


def attend(length, pieces):
    tile, wide_tile = 256, 512
    slots = pieces.shape[2] * 128
    tiles, steps = slots // tile, slots // wide_tile
    per, wide_per, ratio = tile // 128, wide_tile // 128, wide_tile // tile

    def kernel(len_ref, piece_ref, out_ref, lse_ref, held, flipped, logit, sems):
        step = pl.program_id(0)

        @pl.when(step == 0)
        def _():
            copies = [
                pltpu.make_async_copy(
                    piece_ref.at[device], held.at[:, :, device], sems.at[device]
                )
                for device in range(8)
            ]
            for copy in copies:
                copy.start()
            for copy in copies:
                copy.wait()

        @pl.when(step == 0)
        def _():
            for block in range(tiles):
                key = rows_of(held[1, pl.ds(per * block, per)])
                flipped[block] = key.T

        used = len_ref[0]
        query = rows_of(held[0, pl.ds(wide_per * step, wide_per)]) * BF(0.125)
        lane = lax.broadcasted_iota(jnp.int32, (wide_tile, 128), 1)
        low = lane < 64
        zero = jnp.zeros_like(query)
        queries = [jnp.where(low, query, zero), jnp.where(low, zero, query)]

        def score(block, tops, masked):
            key_t = flipped[block]
            result = []
            for head in range(2):
                field = jnp.dot(queries[head], key_t, preferred_element_type=F32)
                if masked:
                    query_pos = step * wide_tile + lax.broadcasted_iota(jnp.int32, field.shape, 0)
                    key_pos = block * tile + lax.broadcasted_iota(jnp.int32, field.shape, 1)
                    seen = (key_pos <= query_pos) & (key_pos < used)
                    field = jnp.where(seen, field, NEGATIVE)
                logit[head, block] = field
                top = jnp.maximum(field[:, :128], field[:, 128:])
                result.append(jnp.maximum(tops[head], top))
            return tuple(result)

        full = jnp.minimum(ratio * step, used // tile)
        end = jnp.minimum(ratio * step + ratio, (used + tile - 1) // tile)
        low_top = jnp.full((wide_tile, 128), NEGATIVE, F32)
        tops = lax.fori_loop(0, full, lambda b, s: score(b, s, False), (low_top, low_top))
        tops = lax.fori_loop(full, end, lambda b, s: score(b, s, True), tops)
        tops = [jnp.max(top, axis=1, keepdims=True) for top in tops]
        wide = [jnp.broadcast_to(top, (wide_tile, tile)) for top in tops]
        low_key = low[:tile]
        one = jnp.ones((tile, 128), BF)

        def mix(block, sums):
            value = rows_of(held[2, pl.ds(per * block, per)])
            values = [jnp.where(low_key, value, one), jnp.where(low_key, one, value)]
            result = []
            for head in range(2):
                probs = jnp.exp(logit[head, block] - wide[head]).astype(BF)
                result.append(
                    sums[head] + jnp.dot(probs, values[head], preferred_element_type=F32)
                )
            return tuple(result)

        nothing = jnp.zeros((wide_tile, 128), F32)
        sums = lax.fori_loop(0, end, mix, (nothing, nothing))
        totals = [sums[0][:, 64:65], sums[1][:, 0:1]]
        out = jnp.where(low, sums[0] / totals[0], sums[1] / totals[1])
        out = out.astype(BF).reshape(wide_per, 8, 16, 128)
        for device in range(8):
            out_ref[device, pl.ds(wide_per * step, wide_per)] = out[:, device]
        level = jnp.where(low, tops[0] + jnp.log(totals[0]), tops[1] + jnp.log(totals[1])).T
        start = pl.multiple_of(step * wide_tile, wide_tile)
        lse_ref[0:1, pl.ds(start, wide_tile)] = level[0:1]
        lse_ref[1:2, pl.ds(start, wide_tile)] = level[64:65]

    return pl.pallas_call(
        kernel,
        grid=(steps,),
        in_specs=[SMEM, ANY],
        out_specs=[
            pl.BlockSpec((8,) + pieces.shape[2:], lambda i: (0, 0, 0, 0)),
            pl.BlockSpec((8, slots), lambda i: (0, 0)),
        ],
        out_shape=[
            jax.ShapeDtypeStruct((8,) + pieces.shape[2:], BF),
            jax.ShapeDtypeStruct((8, slots), F32),
        ],
        scratch_shapes=[
            pltpu.VMEM((3, slots // 128, 8, 16, 128), BF),
            pltpu.VMEM((tiles, 128, tile), BF),
            pltpu.VMEM((2, tiles, wide_tile, tile), F32),
            pltpu.SemaphoreType.DMA((8,)),
        ],
        compiler_params=params(dimension_semantics=("arbitrary",)),
        name="attend",
    )(length, pieces)


def attend_back(length, pieces, attended, grads, lse, cosine, signed_sine, passed):
    tile, wide = 256, 512
    slots = pieces.shape[2] * 128
    tiles = slots // tile
    per, wide_per, ratio = tile // 128, wide // 128, wide // tile
    upper = passed is None

    def kernel(*refs):
        len_ref, piece_ref, att_ref, grad_ref, lse_ref, cos_ref, sin_ref = refs[:7]
        refs = refs[7:]
        if upper:
            passed_ref = None
            out_ref, give_ref = refs[:2]
            refs = refs[2:]
        else:
            passed_ref, out_ref = refs[:2]
            give_ref = None
            refs = refs[2:]
        held, att, grad, delta, level, query_acc, key_acc, value_acc, sems = refs
        step = pl.program_id(0)
        used = len_ref[0]

        @pl.when(step == 0)
        def _():
            copies = []
            for device in range(8):
                for n, (source, target) in enumerate(
                    (
                        (grad_ref.at[device], grad.at[:, device]),
                        (att_ref.at[device], att.at[:, device]),
                        (piece_ref.at[device], held.at[:, :, device]),
                    )
                ):
                    copies.append(pltpu.make_async_copy(source, target, sems.at[n, device]))
            for copy in copies:
                copy.start()
            for copy in copies:
                copy.wait()

        @pl.when(step == 0)
        def _():
            query_acc[...] = jnp.zeros_like(query_acc)
            line = lax.broadcasted_iota(jnp.int32, (8, 128), 0)
            lane = lax.broadcasted_iota(jnp.int32, (8, 128), 1)
            pick = jnp.where(line == lane // 64, 1.0, 0.0).astype(F32)
            for block in range(tiles):
                span = slice(tile * block, tile * block + tile)
                product = rows_of(grad[pl.ds(per * block, per)]).astype(F32) * rows_of(
                    att[pl.ds(per * block, per)]
                ).astype(F32)
                delta[:, span] = lax.dot_general(
                    pick, product, NT, precision=PRECISE, preferred_element_type=F32
                )
            place = lax.broadcasted_iota(jnp.int32, (8, slots), 1)
            level[...] = jnp.where(place < used, lse_ref[...], -NEGATIVE)

        key = rows_of(held[1, pl.ds(wide_per * step, wide_per)])
        value = rows_of(held[2, pl.ds(wide_per * step, wide_per)])
        lane = lax.broadcasted_iota(jnp.int32, (wide, 128), 1)
        low = lane < 64

        def head_part(field, head):
            keep = low[: field.shape[0]]
            nothing = jnp.zeros_like(field)
            return jnp.where(keep, field, nothing) if head == 0 else jnp.where(keep, nothing, field)

        scaled = key * BF(0.125)
        keys = [head_part(scaled, head) for head in range(2)]
        values = [head_part(value, head) for head in range(2)]
        key_acc[...] = jnp.zeros_like(key_acc)
        value_acc[...] = jnp.zeros_like(value_acc)

        def visit(block, masked):
            query = rows_of(held[0, pl.ds(per * block, per)])
            grad_out = rows_of(grad[pl.ds(per * block, per)])
            start = pl.multiple_of(block * tile, tile)
            spans = pl.ds(start, tile)
            query_sum = jnp.zeros((tile, 128), F32)
            key_sum = jnp.zeros((wide, 128), F32)
            value_sum = jnp.zeros((wide, 128), F32)
            for head in range(2):
                logits = lax.dot_general(keys[head], query, NT, preferred_element_type=F32)
                probs = jnp.exp(logits - level[head : head + 1, spans])
                if masked:
                    key_pos = step * wide + lax.broadcasted_iota(jnp.int32, probs.shape, 0)
                    query_pos = block * tile + lax.broadcasted_iota(jnp.int32, probs.shape, 1)
                    probs = jnp.where(key_pos <= query_pos, probs, 0.0)
                grad_probs = lax.dot_general(
                    values[head], grad_out, NT, preferred_element_type=F32
                )
                grad_logits = (probs * (grad_probs - delta[head : head + 1, spans])).astype(BF)
                value_sum += jnp.dot(
                    probs.astype(BF), head_part(grad_out, head), preferred_element_type=F32
                )
                key_sum += jnp.dot(
                    grad_logits, head_part(query, head), preferred_element_type=F32
                )
                query_sum += lax.dot_general(
                    grad_logits, keys[head], TN, preferred_element_type=F32
                )
            query_acc[spans, :] += query_sum
            key_acc[...] += key_sum
            value_acc[...] += value_sum

        end = (used + tile - 1) // tile

        def body(block, carry, masked):
            visit(block, masked)
            return carry

        first = ratio * step
        lax.fori_loop(first, jnp.minimum(first + ratio, end), lambda b, s: body(b, s, True), 0)
        lax.fori_loop(first + ratio, end, lambda b, s: body(b, s, False), 0)

        def put(member, block, field):
            count = field.shape[0] // 128
            field = field.astype(BF).reshape(count, 8, 16, 128)
            for device in range(8):
                out_ref[device, member, pl.ds(count * block, count)] = field[:, device]

        start = pl.multiple_of(step * wide, wide)
        spans = pl.ds(start, wide)
        key_grad = key_acc[...] * 0.125
        put(1, step, turn(key_grad, cos_ref[spans, :], -sin_ref[spans, :]))
        if upper:
            half = 0.5 * value_acc[...]
            give_ref[spans, :] = half
            put(2, step, half)
        else:
            put(2, step, value_acc[...] + passed_ref[spans, :])

        @pl.when(step == slots // wide - 1)
        def _():
            for block in range(tiles):
                part = slice(tile * block, tile * block + tile)
                put(0, block, turn(query_acc[part, :], cos_ref[part, :], -sin_ref[part, :]))

    flat = lambda i: (0, 0)
    table = pl.BlockSpec((slots, 128), flat)
    in_specs = [SMEM, ANY, ANY, ANY, pl.BlockSpec((8, slots), flat), table, table]
    operands = [length, pieces, attended, grads, lse, cosine, signed_sine]
    out_specs = [pl.BlockSpec(pieces.shape, lambda i: (0, 0, 0, 0, 0))]
    out_shape = [jax.ShapeDtypeStruct(pieces.shape, BF)]
    if upper:
        out_specs.append(table)
        out_shape.append(jax.ShapeDtypeStruct((slots, 128), F32))
    else:
        in_specs.append(table)
        operands.append(passed)
    outs = pl.pallas_call(
        kernel,
        grid=(slots // wide,),
        in_specs=in_specs,
        out_specs=out_specs,
        out_shape=out_shape,
        scratch_shapes=[
            pltpu.VMEM((3, slots // 128, 8, 16, 128), BF),
            pltpu.VMEM((slots // 128, 8, 16, 128), BF),
            pltpu.VMEM((slots // 128, 8, 16, 128), BF),
            pltpu.VMEM((8, slots), F32),
            pltpu.VMEM((8, slots), F32),
            pltpu.VMEM((slots, 128), F32),
            pltpu.VMEM((wide, 128), F32),
            pltpu.VMEM((wide, 128), F32),
            pltpu.SemaphoreType.DMA((3, 8)),
        ],
        compiler_params=params(dimension_semantics=("arbitrary",)),
        name="attend_back",
    )(*operands)
    return outs if upper else (outs[0], None)


def block_spans(total_rows):
    return [(offset, min(512, total_rows - offset)) for offset in range(0, total_rows, 512)]


def rotate(field, cosine, sine_table):
    half_dim = field.shape[-1] // 2
    first_half = field[..., :half_dim]
    second_half = field[..., half_dim:]
    return jnp.concatenate(
        [
            first_half * cosine - second_half * sine_table,
            second_half * cosine + first_half * sine_table,
        ],
        axis=-1,
    )


def allowed(query_pos, key_pos, lengths):
    causal = key_pos[None, None, :] <= query_pos[None, :, None]
    inside = key_pos[None, None, :] < lengths[:, None, None]
    return (causal & inside)[:, None, :, :]


def attend_gathered(q_heads, k_flat, v_flat, lengths, positions, score_scale):
    seq_count, stretch_len, head_count, head_dim = q_heads.shape
    first_row = jnp.int32(0)
    k_piece = lax.all_gather(k_flat, "seq", axis=1, tiled=True)
    v_piece = lax.all_gather(v_flat, "seq", axis=1, tiled=True)
    running_max = jnp.full((seq_count, head_count, stretch_len), NEGATIVE, jnp.float32)
    row_total = jnp.zeros((seq_count, head_count, stretch_len), jnp.float32)
    weighted = jnp.zeros((seq_count, stretch_len, head_count, head_dim), jnp.float32)
    for offset, block_len in block_spans(k_piece.shape[1]):
        k_block = k_piece[:, offset : offset + block_len].reshape(
            seq_count, block_len, head_count, head_dim
        )
        v_block = (
            v_piece[:, offset : offset + block_len]
            .reshape(seq_count, block_len, head_count, head_dim)
            .astype(jnp.float32)
        )
        key_pos = first_row + offset + jnp.arange(block_len, dtype=jnp.int32)
        allowed_mask = allowed(positions, key_pos, lengths)
        logits = (
            jnp.einsum("sqhd,skhd->shqk", q_heads, k_block, preferred_element_type=jnp.float32)
            * score_scale
        )
        new_max = jnp.maximum(
            running_max, jnp.max(jnp.where(allowed_mask, logits, NEGATIVE), axis=-1)
        )
        probs = jnp.where(allowed_mask, jnp.exp(logits - new_max[..., None]), 0.0)
        rescale = jnp.exp(running_max - new_max)
        row_total = row_total * rescale + jnp.sum(probs, axis=-1)
        weighted = weighted * jnp.transpose(rescale, (0, 2, 1))[..., None] + jnp.einsum(
            "shqk,skhd->sqhd", probs, v_block, precision=PRECISE, preferred_element_type=jnp.float32
        )
        running_max = new_max
    running_max, row_total, weighted = (running_max, row_total, weighted)
    attended = weighted / jnp.transpose(row_total, (0, 2, 1))[..., None]
    return (attended, running_max + jnp.log(row_total))


def attend_back_gathered(
    q_heads,
    k_heads,
    v_heads,
    q_flat,
    k_flat,
    v_flat,
    grad_heads,
    grad_flat,
    log_total,
    delta_rows,
    lengths,
    positions,
    score_scale,
):
    seq_count, stretch_len, head_count, head_dim = q_heads.shape
    zeros_heads = jnp.zeros((seq_count, stretch_len, head_count, head_dim), jnp.float32)
    carry = zeros_heads
    first_row = jnp.int32(0)
    k_piece = lax.all_gather(k_flat, "seq", axis=1, tiled=True)
    v_piece = lax.all_gather(v_flat, "seq", axis=1, tiled=True)
    for offset, block_len in block_spans(k_piece.shape[1]):
        k_block = k_piece[:, offset : offset + block_len].reshape(
            seq_count, block_len, head_count, head_dim
        )
        v_block = v_piece[:, offset : offset + block_len].reshape(
            seq_count, block_len, head_count, head_dim
        )
        key_pos = first_row + offset + jnp.arange(block_len, dtype=jnp.int32)
        allowed_mask = allowed(positions, key_pos, lengths)
        logits = (
            jnp.einsum("sqhd,skhd->shqk", q_heads, k_block, preferred_element_type=jnp.float32)
            * score_scale
        )
        probs = jnp.where(allowed_mask, jnp.exp(logits - log_total[..., None]), 0.0)
        grad_probs = jnp.einsum(
            "sqhd,skhd->shqk", grad_heads, v_block, preferred_element_type=jnp.float32
        )
        grad_logits = (probs * (grad_probs - delta_rows[..., None])).astype(jnp.bfloat16)
        carry = (
            carry
            + jnp.einsum(
                "shqk,skhd->sqhd", grad_logits, k_block, preferred_element_type=jnp.float32
            )
            * score_scale
        )
    gathered_stats = (
        lax.all_gather(log_total, "seq", axis=2, tiled=True),
        lax.all_gather(delta_rows, "seq", axis=2, tiled=True),
    )
    first_row = jnp.int32(0)
    q_piece = lax.all_gather(q_flat, "seq", axis=1, tiled=True)
    g_piece = lax.all_gather(grad_flat, "seq", axis=1, tiled=True)
    grad_key = zeros_heads
    grad_value = zeros_heads
    for offset, block_len in block_spans(q_piece.shape[1]):
        q_block = q_piece[:, offset : offset + block_len].reshape(
            seq_count, block_len, head_count, head_dim
        )
        g_block = g_piece[:, offset : offset + block_len].reshape(
            seq_count, block_len, head_count, head_dim
        )
        query_pos = first_row + offset + jnp.arange(block_len, dtype=jnp.int32)
        allowed_mask = allowed(query_pos, positions, lengths)
        lse_block = lax.dynamic_slice_in_dim(gathered_stats[0], offset, block_len, 2)
        delta_block = lax.dynamic_slice_in_dim(gathered_stats[1], offset, block_len, 2)
        logits = (
            jnp.einsum("sqhd,skhd->shqk", q_block, k_heads, preferred_element_type=jnp.float32)
            * score_scale
        )
        probs = jnp.where(allowed_mask, jnp.exp(logits - lse_block[..., None]), 0.0)
        grad_value = grad_value + jnp.einsum(
            "shqk,sqhd->skhd",
            probs,
            g_block.astype(jnp.float32),
            precision=PRECISE,
            preferred_element_type=jnp.float32,
        )
        grad_probs = jnp.einsum(
            "sqhd,skhd->shqk", g_block, v_heads, preferred_element_type=jnp.float32
        )
        grad_logits = (probs * (grad_probs - delta_block[..., None])).astype(jnp.bfloat16)
        grad_key = (
            grad_key
            + jnp.einsum(
                "shqk,sqhd->skhd", grad_logits, q_block, preferred_element_type=jnp.float32
            )
            * score_scale
        )
    grad_key, grad_value = (grad_key, grad_value)
    return (carry, grad_key, grad_value)


def body(tokens, seq_lens, norm_attn, w_qkv, w_out, norm_ffn, w_gate, w_up, w_down, cotangent):
    seq_count, stretch_len, model_width = tokens.shape
    head_count = HEADS
    head_dim = model_width // head_count
    score_scale = head_dim ** (-0.5)
    lengths = seq_lens[0]
    positions = lax.axis_index("seq") * stretch_len + jnp.arange(stretch_len, dtype=jnp.int32)
    half_dim = head_dim // 2
    freqs = 10000.0 ** (-jnp.arange(half_dim, dtype=jnp.float32) / half_dim)
    angle = positions.astype(jnp.float32)[:, None] * freqs[None, :]
    cosine = jnp.cos(angle)[:, None, :]
    sine_table = jnp.sin(angle)[:, None, :]

    def heads_of(field):
        return field.reshape(seq_count, stretch_len, head_count, head_dim)

    def gather_layer(layer_index):
        return (
            lax.all_gather(norm_attn[layer_index], ("grp", "seq"), axis=0, tiled=True),
            lax.all_gather(w_qkv[layer_index], ("grp", "seq"), axis=0, tiled=True),
            lax.all_gather(w_out[layer_index], ("grp", "seq"), axis=0, tiled=True),
            lax.all_gather(norm_ffn[layer_index], ("grp", "seq"), axis=0, tiled=True),
            lax.all_gather(w_gate[layer_index], ("grp", "seq"), axis=0, tiled=True),
            lax.all_gather(w_up[layer_index], ("grp", "seq"), axis=0, tiled=True),
            lax.all_gather(w_down[layer_index], ("grp", "seq"), axis=0, tiled=True),
        )

    def gather_again(layer_index):
        return (
            lax.all_gather(norm_attn[layer_index], ("grp", "seq"), axis=0, tiled=True),
            lax.all_gather(w_qkv[layer_index], ("grp", "seq"), axis=0, tiled=True),
            lax.all_gather(w_out[layer_index], ("grp", "seq"), axis=0, tiled=True),
            lax.all_gather(norm_ffn[layer_index], ("grp", "seq"), axis=0, tiled=True),
            lax.all_gather(w_gate[layer_index], ("grp", "seq"), axis=0, tiled=True),
            lax.all_gather(w_up[layer_index], ("grp", "seq"), axis=0, tiled=True),
            lax.all_gather(w_down[layer_index], ("grp", "seq"), axis=0, tiled=True),
        )

    def forward_layer(inputs, params, first_value):
        gain_one, mat_qkv, mat_out, gain_two, mat_gate, mat_up, mat_down = params
        rms_one = lax.rsqrt(jnp.mean(inputs * inputs, axis=-1, keepdims=True) + EPSILON)
        normed = (inputs * rms_one * gain_one.astype(jnp.float32)).astype(jnp.bfloat16)
        projected = jnp.dot(normed, mat_qkv, preferred_element_type=jnp.float32)
        query_raw = projected[:, :model_width]
        key_raw = projected[:, model_width : 2 * model_width]
        value_raw = projected[:, 2 * model_width :]
        if first_value is None:
            values = value_raw.astype(jnp.bfloat16)
        else:
            values = (0.5 * value_raw + 0.5 * first_value.astype(jnp.float32)).astype(jnp.bfloat16)
        query_rot = rotate(heads_of(query_raw), cosine, sine_table).astype(jnp.bfloat16)
        key_rot = rotate(heads_of(key_raw), cosine, sine_table).astype(jnp.bfloat16)
        attended, log_total = attend_gathered(
            query_rot,
            key_rot.reshape(seq_count, stretch_len, model_width),
            values.reshape(seq_count, stretch_len, model_width),
            lengths,
            positions,
            score_scale,
        )
        attn_low = attended.reshape(-1, model_width).astype(jnp.bfloat16)
        middle = inputs + jnp.dot(attn_low, mat_out, preferred_element_type=jnp.float32)
        rms_two = lax.rsqrt(jnp.mean(middle * middle, axis=-1, keepdims=True) + EPSILON)
        normed_two = (middle * rms_two * gain_two.astype(jnp.float32)).astype(jnp.bfloat16)
        gate_pre = jnp.dot(normed_two, mat_gate, preferred_element_type=jnp.float32)
        up_pre = jnp.dot(normed_two, mat_up, preferred_element_type=jnp.float32)
        hidden = (jax.nn.silu(gate_pre) * up_pre).astype(jnp.bfloat16)
        result = middle + jnp.dot(hidden, mat_down, preferred_element_type=jnp.float32)
        kept = (
            inputs,
            rms_one,
            normed,
            query_rot,
            key_rot,
            values,
            attended,
            attn_low,
            log_total,
            middle,
            rms_two,
            normed_two,
            gate_pre,
            up_pre,
            hidden,
        )
        return (result, values, kept)

    def backward_layer(grad_in, params, kept, first_grad):
        gain_one, mat_qkv, mat_out, gain_two, mat_gate, mat_up, mat_down = params
        (
            inputs,
            rms_one,
            normed,
            query_rot,
            key_rot,
            values,
            attended,
            attn_low,
            log_total,
            middle,
            rms_two,
            normed_two,
            gate_pre,
            up_pre,
            hidden,
        ) = kept
        grad_low = grad_in.astype(jnp.bfloat16)
        grad_down = jnp.einsum("nf,nd->fd", hidden, grad_low, preferred_element_type=jnp.float32)
        grad_hidden = jnp.einsum(
            "nd,fd->nf", grad_low, mat_down, preferred_element_type=jnp.float32
        )
        sigma = jax.nn.sigmoid(gate_pre)
        grad_gate_pre = (grad_hidden * up_pre * sigma * (1.0 + gate_pre * (1.0 - sigma))).astype(
            jnp.bfloat16
        )
        grad_up_pre = (grad_hidden * gate_pre * sigma).astype(jnp.bfloat16)
        grad_gate = jnp.einsum(
            "nd,nf->df", normed_two, grad_gate_pre, preferred_element_type=jnp.float32
        )
        grad_up = jnp.einsum(
            "nd,nf->df", normed_two, grad_up_pre, preferred_element_type=jnp.float32
        )
        grad_normed_two = jnp.einsum(
            "nf,df->nd", grad_gate_pre, mat_gate, preferred_element_type=jnp.float32
        ) + jnp.einsum("nf,df->nd", grad_up_pre, mat_up, preferred_element_type=jnp.float32)
        scaled_two = middle * rms_two
        grad_gain_two = jnp.sum(grad_normed_two * scaled_two, axis=0)
        weighted_two = grad_normed_two * gain_two.astype(jnp.float32)
        grad_middle = grad_in + rms_two * (
            weighted_two - scaled_two * jnp.mean(weighted_two * scaled_two, axis=-1, keepdims=True)
        )
        grad_attn = grad_middle.astype(jnp.bfloat16)
        grad_out_mat = jnp.einsum(
            "nd,ne->de", attn_low, grad_attn, preferred_element_type=jnp.float32
        )
        grad_attended = jnp.einsum(
            "ne,de->nd", grad_attn, mat_out, preferred_element_type=jnp.float32
        ).astype(jnp.bfloat16)
        grad_heads = heads_of(grad_attended)
        delta_rows = jnp.transpose(
            jnp.sum(grad_heads.astype(jnp.float32) * attended, axis=-1), (0, 2, 1)
        )
        grad_query, grad_key, grad_value = attend_back_gathered(
            query_rot,
            key_rot,
            heads_of(values),
            query_rot.reshape(seq_count, stretch_len, model_width),
            key_rot.reshape(seq_count, stretch_len, model_width),
            values.reshape(seq_count, stretch_len, model_width),
            grad_heads,
            grad_attended.reshape(seq_count, stretch_len, model_width),
            log_total,
            delta_rows,
            lengths,
            positions,
            score_scale,
        )
        grad_query_raw = rotate(grad_query, cosine, -sine_table).reshape(-1, model_width)
        grad_key_raw = rotate(grad_key, cosine, -sine_table).reshape(-1, model_width)
        grad_value_flat = grad_value.reshape(-1, model_width)
        if first_grad is None:
            grad_value_raw = 0.5 * grad_value_flat
            passed = 0.5 * grad_value_flat
        else:
            grad_value_raw = grad_value_flat + first_grad
            passed = None
        grad_proj = jnp.concatenate([grad_query_raw, grad_key_raw, grad_value_raw], axis=-1).astype(
            jnp.bfloat16
        )
        grad_qkv = jnp.einsum("nd,ne->de", normed, grad_proj, preferred_element_type=jnp.float32)
        grad_normed = jnp.einsum(
            "ne,de->nd", grad_proj, mat_qkv, preferred_element_type=jnp.float32
        )
        scaled_one = inputs * rms_one
        grad_gain_one = jnp.sum(grad_normed * scaled_one, axis=0)
        weighted_one = grad_normed * gain_one.astype(jnp.float32)
        grad_inputs = grad_middle + rms_one * (
            weighted_one - scaled_one * jnp.mean(weighted_one * scaled_one, axis=-1, keepdims=True)
        )
        return (
            grad_inputs,
            (grad_gain_one, grad_qkv, grad_out_mat, grad_gain_two, grad_gate, grad_up, grad_down),
            passed,
        )

    def reduce_layer(grads):
        return (
            lax.psum_scatter(grads[0], ("grp", "seq"), scatter_dimension=0, tiled=True),
            lax.psum_scatter(grads[1], ("grp", "seq"), scatter_dimension=0, tiled=True),
            lax.psum_scatter(grads[2], ("grp", "seq"), scatter_dimension=0, tiled=True),
            lax.psum_scatter(grads[3], ("grp", "seq"), scatter_dimension=0, tiled=True),
            lax.psum_scatter(grads[4], ("grp", "seq"), scatter_dimension=0, tiled=True),
            lax.psum_scatter(grads[5], ("grp", "seq"), scatter_dimension=0, tiled=True),
            lax.psum_scatter(grads[6], ("grp", "seq"), scatter_dimension=0, tiled=True),
        )

    state_zero = tokens.astype(jnp.float32).reshape(-1, model_width)
    params_one = gather_layer(0)
    state_one, first_value, kept_one = forward_layer(state_zero, params_one, None)
    params_two = gather_layer(1)
    state_two, unused_value, kept_two = forward_layer(state_one, params_two, first_value)
    layer_out = state_two.astype(jnp.bfloat16).reshape(seq_count, stretch_len, model_width)
    valid_mask = (positions[None, :] < lengths[:, None]).astype(jnp.float32)
    grad_state = (cotangent.astype(jnp.float32) * valid_mask[:, :, None]).reshape(-1, model_width)
    params_two = gather_again(1)
    grad_mid, grads_two, passed = backward_layer(grad_state, params_two, kept_two, None)
    shards_two = reduce_layer(grads_two)
    params_one = gather_again(0)
    grad_inputs, grads_one, unused_grad = backward_layer(grad_mid, params_one, kept_one, passed)
    shards_one = reduce_layer(grads_one)
    stacked = tuple((jnp.stack([shards_one[member], shards_two[member]]) for member in range(7)))
    input_grad = grad_inputs.reshape(seq_count, stretch_len, model_width)
    return (
        layer_out,
        input_grad,
        stacked[0],
        stacked[1],
        stacked[2],
        stacked[3],
        stacked[4],
        stacked[5],
        stacked[6],
    )


def body_planes(
    tokens, seq_lens, norm_attn, w_qkv, w_out, norm_ffn, w_gate, w_up, w_down, cotangent
):
    seqs, stretch, width = tokens.shape
    y, c, z, x = (lax.axis_index(axis) for axis in ALL)
    lane = c * 4 + y * 2 + x
    where = jnp.stack([y, c, z, x]).astype(jnp.int32)
    rows = seqs * stretch
    ffn = w_gate.shape[2]

    def exchange(field):
        return lax.all_to_all(field, PLANE, 0, 0, tiled=True)

    def exchange_z(field):
        shape = field.shape
        moved = lax.all_to_all(field.reshape((4, 2) + shape[1:]), "z", 0, 0, tiled=True)
        return moved.reshape(shape)

    def cut_blocks(field):
        field = field.reshape(seqs, 2, 8, 16, width)
        return jnp.transpose(field, (2, 0, 1, 3, 4))

    def join_stripes(field):
        return jnp.transpose(field, (1, 0, 2, 3, 4)).reshape(rows, width)

    def cut_stripes(field):
        return jnp.transpose(field.reshape(seqs, 8, 2, 16, width), (1, 0, 2, 3, 4))

    def join_blocks(field):
        return jnp.transpose(field, (1, 2, 0, 3, 4)).reshape(seqs, stretch, width)

    def gather_all(shard):
        return lax.all_gather(shard, ALL, axis=0, tiled=True)

    def gain_shard(layer):
        gain = jnp.stack([norm_attn[layer], norm_ffn[layer]], axis=1)
        return jnp.pad(gain, ((0, 0), (0, 126)))

    def gains(columns):
        return jnp.transpose(columns)[:2].astype(F32)

    def gather_ffn(layer, *after):
        cuts = [w_gate[layer], w_up[layer], pack(w_down[layer])]
        if layer == 0:
            cuts.append(w_out[layer])
        shard = jnp.concatenate(cuts, axis=1)
        if after:
            shard, *_ = fence(shard, *after)
        gathered = gather_all(shard)
        packed = gathered[:, 2 * ffn : 2 * ffn + 3 * width]
        w_d = unpack(packed.reshape(32, -1, 3 * width)).reshape(-1, width)
        return gathered, w_d

    def pack(rows_of_down):
        tall = w_qkv.shape[1]
        spare = 3 * tall - rows_of_down.shape[-2]
        lead = [(0, 0)] * (rows_of_down.ndim - 2)
        padded = jnp.pad(rows_of_down, lead + [(0, spare), (0, 0)])
        cuts = [padded[..., n * tall : n * tall + tall, :] for n in range(3)]
        return jnp.concatenate(cuts, axis=-1)

    def unpack(packed):
        cols = packed.shape[-1] // 3
        cuts = [packed[..., n * cols : n * cols + cols] for n in range(3)]
        return jnp.concatenate(cuts, axis=-2)[..., : w_down.shape[1], :]

    def gather_first():
        shard = w_qkv[0]
        first = jnp.concatenate([shard[:, :width], gain_shard(0)], axis=1)
        w_q = gather_z_first(where, first, "x", "y")
        w_k = gather_z_first(where, shard[:, width : 2 * width], "y", "x")
        w_v = gather_z_first(where, shard[:, 2 * width :], "x", "y")
        weights = [(w_q, 0), (w_k, 0), (w_v, 0)]
        return weights, [w_q[:, :width], w_k, w_v], gains(w_q[:, width:])

    def second_weights(whole):
        weights = [(whole, 0), (whole, 1), (whole, 2)]
        turned = [whole[:, : 3 * width]]
        return weights, turned, (whole, 3 * width), gains(whole[:, 4 * width :])

    here = z * 2 + x
    routes = []
    for k in range(8):
        route = []
        for sy in range(2):
            for sc in range(2):
                for sb in range(8):
                    to = sb ^ k
                    target = (((to >> 1) & 1) * 2 + (to >> 2)) * 4 + 2 * sc + sy
                    route.append(((sy * 2 + sc) * 8 + sb, target * 2 + (to & 1)))
        routes.append(route)
    lengths = lax.ppermute(seq_lens, ALL, routes[0])[0]
    length = [lengths[n : n + 1] for n in range(2)]
    slots = stretch * 8
    half_dim = width // HEADS // 2
    freqs = 10000.0 ** (-jnp.arange(half_dim, dtype=F32) / half_dim)
    angle = jnp.arange(slots, dtype=F32)[:, None] * freqs[None, :]
    cosine, sine = jnp.cos(angle), jnp.sin(angle)
    cosine = jnp.concatenate([cosine] * 4, axis=1)
    sine = jnp.concatenate([-sine, sine] * 2, axis=1)

    def mine(table):
        own = lax.dynamic_index_in_dim(
            table.reshape(slots // 128, 8, 16, 128), lane, 1, keepdims=False
        )
        return own.reshape(stretch, 128)

    my_cos, my_sin = mine(cosine), mine(sine)
    step = jnp.arange(stretch, dtype=jnp.int32)
    places = (step // 16) * 128 + lane * 16 + step % 16
    valid = (places[None, :] < lengths[:, None]).astype(F32).reshape(rows, 1)

    shape = (8, 3, stretch // 16, 16, 128)

    def project(inputs, weights, gain, first_value):
        return project_qkv(inputs, gain, weights, my_cos, my_sin, first_value)

    def near(field):
        return swap(field, "c")

    def norm_back(grad_normed, source, gain):
        rms = lax.rsqrt(jnp.mean(source * source, axis=-1, keepdims=True) + EPSILON)
        scaled = source * rms
        weighted = grad_normed * gain
        return rms * (weighted - scaled * jnp.mean(weighted * scaled, axis=-1, keepdims=True))

    def blocks_of(grad):
        return grad.reshape(4, 2, 2, 32, grad.shape[-1])

    def dots(grads, weights):
        total = None
        for grad, weight in zip(grads, weights):
            part = lax.dot_general(grad, weight, NT, preferred_element_type=F32)
            total = part if total is None else total + part
        return total

    def attn_grads(one, att, proj, mid, places):
        return weight_grads(core, [(one, [proj]), (att, [mid])], places)

    def sum_z(grad):
        flat = grad.reshape(4, 128, grad.shape[-1])
        flat = lax.psum_scatter(flat, "z", scatter_dimension=0, tiled=True)
        return flat.reshape(2, 2, 32, grad.shape[-1])

    def pair_sums(summed):
        half = summed.shape[-1] // 2
        return [
            Reduction(summed[..., :half], "xy", "yx"),
            Reduction(summed[..., half:], "yx", "yx"),
        ]

    def ffn_grads(two, gates, ups, hid, low):
        half = ffn // 2
        parts = [[(0, half, 0, 0), (half, half, 0, half)]]
        parts.append([(0, half, 0, ffn), (half, half, 0, ffn + half)])
        (grad,) = weight_grads(
            core, [(two, [gates, ups]), (hid, [low])], [parts, [[(0, width, 0, 2 * ffn)]]]
        )
        return grad

    def backward_layer(grad_in, w_attn, w_ffn, kept, passed, upper, beside):
        w_turned, w_o, gain = w_attn
        w_o = w_o[0][:, w_o[1] : w_o[1] + width]
        w_gu, w_d = w_ffn
        inputs, normed, pieces, attended, lse, buffers = kept
        attn_low, middle, normed_two, gate, up, hidden = buffers
        inputs = jnp.concatenate(inputs).astype(F32)
        normed = jnp.concatenate(normed)
        gate, up = gate.astype(F32), up.astype(F32)
        grad_low = grad_in.astype(BF)
        low = (grad_low, near(grad_low))
        hid = (hidden, near(hidden))
        two = (normed_two, near(normed_two))
        att = (attn_low, near(attn_low))
        one = (normed, near(normed))
        grad_hidden = lax.dot_general(grad_low, w_d, NT, preferred_element_type=F32)
        sigma = jax.nn.sigmoid(gate)
        grad_gate = (grad_hidden * up * sigma * (1.0 + gate * (1.0 - sigma))).astype(BF)
        grad_up = (grad_hidden * gate * sigma).astype(BF)
        gates = (grad_gate, near(grad_gate))
        ups = (grad_up, near(grad_up))
        if upper is None:
            beside, grad_gate, grad_up, *gates = fence(beside, grad_gate, grad_up, *gates)
        summed = ffn_grads(two, gates, ups, hid, low)
        summed, grad_gate, grad_up = fence(summed, grad_gate, grad_up)
        summed = sum_z(summed)
        grad_normed = dots([grad_gate, grad_up], [w_gu[:, :ffn], w_gu[:, ffn : 2 * ffn]])
        grad_middle = grad_in + norm_back(grad_normed, middle, gain[1])
        grad_attn = grad_middle.astype(BF)
        mid = (grad_attn, near(grad_attn))
        grad_o = lax.dot_general(grad_attn, w_o, NT, preferred_element_type=F32).astype(BF)
        grad_o = jnp.transpose(grad_o.reshape(rows, 8, 128), (1, 0, 2))
        if upper is not None:
            grad_o, beside = fence(grad_o, beside)

        grad_o = exchange(grad_o)
        ffn_pair = []
        if upper is not None:
            upper_ffn, upper_attn = upper
            upper_ffn, grad_o = fence(upper_ffn, grad_o)
            ffn_pair = pair_sums(upper_ffn)
            (grad_o,) = send_all(ffn_pair, grad_o)
        grad_o = grad_o.reshape(8, 2, stretch // 16, 16, 128)
        cos_sin = (cosine, sine)
        parts_a, pass_a = attend_back(
            length[0], pieces[0], attended[0], grad_o[:, 0], lse[0], *cos_sin, passed and passed[0]
        )
        parts_a, grad_b = fence(parts_a, grad_o[:, 1])
        if ffn_pair:
            parts_a, grad_b = add_all(ffn_pair, parts_a, grad_b)
            parts_a, grad_b = send_all(ffn_pair, parts_a, grad_b)
        moved_a = exchange(parts_a.reshape(8, 3, stretch, 128))
        parts_b, pass_b = attend_back(
            length[1], pieces[1], attended[1], grad_b, lse[1], *cos_sin, passed and passed[1]
        )
        moved_a, parts_b = fence(moved_a, parts_b)
        moved_b = exchange(parts_b.reshape(8, 3, stretch, 128))
        attn_pair = []
        if ffn_pair:
            (moved_b,) = add_all(ffn_pair, moved_b)
            upper_attn, moved_b = fence(upper_attn, moved_b)
            attn_pair = pair_sums(upper_attn)
            (moved_b,) = send_all(attn_pair, moved_b)
        grad_proj = jnp.concatenate(
            [
                jnp.transpose(moved, (2, 1, 0, 3)).reshape(stretch, 3 * width)
                for moved in (moved_a, moved_b)
            ]
        )
        proj = (grad_proj, near(grad_proj))
        cuts, at = [], 0
        for weight in w_turned:
            cuts.append(grad_proj[:, at : at + weight.shape[1]])
            at += weight.shape[1]
        grad_normed = dots(cuts, w_turned)
        grad = grad_middle + norm_back(grad_normed, inputs, gain[0])
        todo = one + att + proj + mid
        return grad, summed, todo, (pass_a, pass_b), ffn_pair, attn_pair, beside

    core = c.astype(jnp.int32).reshape(1)
    ffn_one = gather_ffn(0)
    state = join_stripes(exchange_z(exchange(cut_blocks(tokens))))
    in_one = (state[:stretch], state[stretch:])
    qkv_one, turned_one, gain_one = gather_first()
    out_one = (ffn_one[0], 2 * ffn + 3 * width)

    shard = jnp.concatenate([w_qkv[1], w_out[1], gain_shard(1)], axis=1)
    parts_a, normed_a = project(in_one[0], qkv_one, gain_one, None)
    pieces_a = exchange(parts_a)
    parts_b, normed_b = project(in_one[1], qkv_one, gain_one, None)
    shard, pieces_a, sent_b = fence(shard, pieces_a, parts_b)
    hops = [hop(shard, k) for k in (1, 2, 3)]
    pieces_a = pieces_a.reshape(shape)
    pieces_b = exchange(sent_b)
    attended_a, lse_a = attend(length[0], pieces_a)
    attended_a, pieces_b, ffn_one, *hops = fence(attended_a, pieces_b, ffn_one, *hops)
    out_one = (ffn_one[0], out_one[1])
    stack = jnp.stack([shard] + hops)
    cut = stack.shape[2] // 256 * 128
    stacks = [stack[..., :cut], stack[..., cut:]]
    besides = [swap(stacks[0], "x"), swap(stacks[1], "y")]
    pieces_b = pieces_b.reshape(shape)
    low_a = exchange(attended_a.reshape(8, stretch, 128))
    attended_b, lse_b = attend(length[1], pieces_b)
    ffn_two = gather_ffn(1, attended_a)
    low_a, sent_b, besides = fence(low_a, attended_b, besides)
    rings = [
        [((0, 0), stacks[0]), ((0, 1), besides[0])],
        [((0, 0), stacks[1]), ((1, 0), besides[1])],
    ]
    for axis, ring in zip(("y", "x"), rings):
        for (dy, dx), piece in list(ring):
            place = (1, dx) if axis == "y" else (dy, 1)
            ring.append((place, swap(piece, axis)))
    low_b = exchange(sent_b.reshape(8, stretch, 128))
    rest = (ffn_one[0], ffn_one[1], gain_one, ffn)
    result_a, buffers = forward_ffn(
        low_a, in_one[0].astype(F32), out_one, *rest, None, 0, rows
    )
    held = fence(result_a, *[piece for ring in rings for _, piece in ring])
    result_a = held[0]
    rings = [
        [(place, piece) for (place, _), piece in zip(ring, held[1 + 4 * n : 5 + 4 * n])]
        for n, ring in enumerate(rings)
    ]
    rings = [
        [
            ((dy, dc, dx), swap(piece, "c") if dc else piece)
            for (dy, dx), piece in ring
            for dc in (0, 1)
        ]
        for ring in rings
    ]
    relative = [[place for place, _ in ring] for ring in rings]
    sides = [[piece for _, piece in ring] for ring in rings]
    whole = assemble(where, sides, relative)
    kept_one = (in_one, (normed_a, normed_b), (pieces_a, pieces_b), (attended_a, attended_b))
    kept_one += ((lse_a, lse_b),)
    qkv_two, turned_two, out_two, gain_two = second_weights(whole)

    next_a, normed_a = project(result_a, qkv_two, gain_two, parts_a)
    next_a, low_b = fence(next_a, low_b)
    pieces_a = exchange(next_a)
    result_b, buffers = forward_ffn(
        low_b, in_one[1].astype(F32), out_one, *rest, buffers, stretch, rows
    )
    kept_one += (buffers,)
    in_two = (result_a, result_b)
    next_b, normed_b = project(result_b, qkv_two, gain_two, parts_b)
    pieces_a, sent_b = fence(pieces_a, next_b)
    pieces_a = pieces_a.reshape(shape)
    pieces_b = exchange(sent_b)
    attended_a, lse_a = attend(length[0], pieces_a)
    attended_a, pieces_b, other = fence(attended_a, pieces_b, cut_blocks(cotangent))
    other = [
        lax.ppermute(lax.dynamic_index_in_dim(other, here ^ k, 0, keepdims=False), ALL, routes[k])
        for k in range(8)
    ]
    pieces_b = pieces_b.reshape(shape)
    low_a = exchange(attended_a.reshape(8, stretch, 128))
    attended_b, lse_b = attend(length[1], pieces_b)
    low_a, sent_b, *other = fence(low_a, attended_b, *other)
    low_b = exchange(sent_b.reshape(8, stretch, 128))
    rest = (ffn_two[0], ffn_two[1], gain_two, ffn)
    final_a, buffers = forward_ffn(low_a, result_a, out_two, *rest, None, 0, rows)
    final_a, low_b = fence(final_a, low_b)
    moved_a = exchange_z(final_a.astype(BF).reshape(8, 2, 16, width))
    final_b, buffers = forward_ffn(low_b, result_b, out_two, *rest, buffers, stretch, rows)
    kept_two = (in_two, (normed_a, normed_b), (pieces_a, pieces_b), (attended_a, attended_b))
    kept_two += ((lse_a, lse_b), buffers)
    moved_a, final_b, *other = fence(moved_a, final_b, *other)
    moved_b = exchange_z(final_b.astype(BF).reshape(8, 2, 16, width))
    grad = jnp.zeros((8, seqs, 2, 16, width), BF)
    for k in range(8):
        grad = lax.dynamic_update_index_in_dim(grad, other[k], lane ^ k, 0)
    grad = join_stripes(grad).astype(F32) * valid
    layer_out = jnp.stack([moved_a, moved_b], axis=1)
    grad, ffn_two_sum, todo, passed, _, _, layer_out = backward_layer(
        grad, (turned_two, out_two, gain_two), ffn_two, kept_two, None, None, layer_out
    )
    grad, *todo = fence(grad, *todo)
    todo = [tuple(todo[n : n + 2]) for n in (0, 2, 4, 6)]
    (attn_two,) = attn_grads(*todo, [[[(0, 3 * width, 0, 0)]], [[(0, width, 0, 3 * width)]]])
    attn_two, grad, layer_out = fence(attn_two, grad, layer_out)
    attn_two = sum_z(attn_two)
    layer_out = exchange(layer_out)
    grad, ffn_one_sum, todo, _, ffn_pair_two, attn_pair_two, layer_out = backward_layer(
        grad,
        (turned_one, out_one, gain_one),
        ffn_one,
        kept_one,
        passed,
        (ffn_two_sum, attn_two),
        layer_out,
    )
    layer_out = join_blocks(layer_out)
    grad, *todo = fence(grad, *todo)
    todo = [tuple(todo[n : n + 2]) for n in (0, 2, 4, 6)]
    places = [[[(0, 2 * width, 0, 0), (2 * width, width, 1, 0)]], [[(0, width, 1, width)]]]
    attn_pair_one = [
        Reduction(part.reshape(4, 2, 2, 32, -1), order)
        for part, order in zip(attn_grads(*todo, places), ("yxz", "xyz"))
    ]
    (grad,) = send_all(attn_pair_one, grad)
    input_grad = cut_stripes(grad.astype(BF))
    add_all(attn_pair_two, *[r.partial for r in attn_pair_one])
    send_all(attn_pair_two)
    add_all(attn_pair_one, *[r.partial for r in attn_pair_two])
    send_all(attn_pair_one)
    mark = [r.partial for r in attn_pair_one]
    ffn_one_sum, input_grad, *mark = fence(ffn_one_sum, input_grad, *mark)
    ffn_pair_one = pair_sums(ffn_one_sum)
    input_grad = exchange_z(input_grad)
    send_all(ffn_pair_one)
    add_all(attn_pair_one)
    send_all(attn_pair_one)
    input_grad = exchange(input_grad)
    add_all(ffn_pair_one)
    send_all(ffn_pair_one)
    add_all(attn_pair_two + ffn_pair_one)
    add_all(attn_pair_one)
    input_grad = join_blocks(input_grad).astype(F32)

    out_grad, qkv_grad, gate_grad, up_grad, down_grad = [], [], [], [], []
    for attn_pair, ffn_pair in ((attn_pair_one, ffn_pair_one), (attn_pair_two, ffn_pair_two)):
        field = jnp.concatenate([r.partial for r in attn_pair], axis=1)
        qkv_grad.append(field[:, : 3 * width])
        out_grad.append(field[:, 3 * width :])
        field = jnp.concatenate([r.partial for r in ffn_pair], axis=1)
        gate_grad.append(field[:, :ffn])
        up_grad.append(field[:, ffn : 2 * ffn])
        down_grad.append(unpack(field[:, 2 * ffn :]))

    def gain_grad(pairs, gain):
        total = sum(jnp.sum(w.astype(F32) * grad, axis=1) for w, grad in pairs)
        return total / gain.astype(F32)

    attn_gain = [gain_grad([(w_qkv[n], qkv_grad[n])], norm_attn[n]) for n in range(2)]
    ffn_gain = [
        gain_grad([(w_gate[n], gate_grad[n]), (w_up[n], up_grad[n])], norm_ffn[n])
        for n in range(2)
    ]
    return (
        layer_out,
        input_grad,
        jnp.stack(attn_gain),
        jnp.stack(qkv_grad),
        jnp.stack(out_grad),
        jnp.stack(ffn_gain),
        jnp.stack(gate_grad),
        jnp.stack(up_grad),
        jnp.stack(down_grad),
    )


IN_SPECS = (
    ("grp", "seq", None),
    ("grp", None),
    (None, ("grp", "seq")),
    (None, ("grp", "seq"), None),
    (None, ("grp", "seq"), None),
    (None, ("grp", "seq")),
    (None, ("grp", "seq"), None),
    (None, ("grp", "seq"), None),
    (None, ("grp", "seq"), None),
    ("grp", "seq", None),
)
OUT_SPECS = (
    ("grp", "seq", None),
    ("grp", "seq", None),
    (None, ("grp", "seq")),
    (None, ("grp", "seq"), None),
    (None, ("grp", "seq"), None),
    (None, ("grp", "seq")),
    (None, ("grp", "seq"), None),
    (None, ("grp", "seq"), None),
    (None, ("grp", "seq"), None),
)


def solution(mesh):
    if mesh.shape["grp"] == 4 and mesh.shape["seq"] == 8:
        split = Mesh(mesh.devices.reshape(2, 2, 4, 2), ALL)
        names = {"grp": ("y", "c"), "seq": ("z", "x"), ("grp", "seq"): ALL, None: None}
        program = body_planes
    else:
        split = mesh
        names = {"grp": "grp", "seq": "seq", ("grp", "seq"): ("grp", "seq"), None: None}
        program = body

    def specs(table):
        return tuple(P(*(names[name] for name in row)) for row in table)

    return jax.shard_map(
        program,
        mesh=split,
        in_specs=specs(IN_SPECS),
        out_specs=specs(OUT_SPECS),
        check_vma=False,
    )
```
